128 devices in a mesh: lon: 16 (over x, y), lat: 8 (over z, core).
Axes of the slice: x: 4, y: 4, z: 4, core: 2. Of those that a mesh axis runs over, the one named last changes fastest.
Arguments:
- lam_tracer: float32 [2, 50, 256, 2048], P(None, None, 'lat', 'lon'), may hold values from -6 to 6
- tracer: float32 [2, 50, 256, 2048], P(None, None, 'lat', 'lon'), may hold values from -6 to 6
- velocity: float32 [2, 50, 256, 2048], P(None, None, 'lat', 'lon'), may hold values from -4 to 4
- diffusivity: float32 [50, 256, 2048], P(None, 'lat', 'lon'), may hold values from 0.5 to 20
- lam_surface: float32 [256, 2048], P('lat', 'lon'), may hold values from -6 to 6
- sea_depth: float32 [256, 2048], P('lat', 'lon'), may hold values from 0.2 to 5
- levels: int32 [256, 2048], P('lat', 'lon'), may hold values from 0 to 50, as said below
Outputs:
- adjoint_tracer: float32 [2, 50, 256, 2048], P(None, None, 'lat', 'lon')
- adjoint_velocity: float32 [2, 50, 256, 2048], P(None, None, 'lat', 'lon')
- solution: float32 [256, 2048], P('lat', 'lon')
The draws below stay inside these ranges and needn't reach their ends.
Inputs may be any that keep to these rules, and one draw needn't show every extreme that they name: A sea column is wet in its top levels; land columns are 0. Land comes in whole rows of a tile of 128 columns, far more often in some longitude bands than in others.
All inputs are finite; a program needn't handle non-finite values.
Results may differ from the reference program's by a relative error of at most 0.0001.
Values sent between devices are 32-bit elements; how exact they have to be, the bound alone decides.
No kernel may reach another device: no remote copies, remote signals or barrier semaphores. Data moves between devices by JAX's collectives and lax.ppermute only.
A program may use at most 64 MiB of HBM per device.

```python
import math
import jax
import jax.numpy as jnp
from jax import lax

LEVELS = 50
CX = 128
ITERS = 4
NY = 256
NX = 2048


def draw_levels(key, part):
    key = jax.random.fold_in(key, 11)
    land_key, column_key = jax.random.split(key)
    tile_ids = jnp.arange(NX // CX, dtype=jnp.int32)[None, :]
    land_share = jnp.where(tile_ids * 4 // (NX // CX) % 2 == 0, 85, 10)
    land_roll = jax.random.randint(land_key, (NY, NX // CX), 0, 100)
    land_rows = jnp.repeat(land_roll < land_share, CX, axis=1)
    sea_levels = jax.random.randint(column_key, (NY, NX), 1, LEVELS + 1)
    result = jnp.where(land_rows, 0, sea_levels).astype(jnp.int32)
    return result.at[NY // 2, NX - 1].set(LEVELS)


def block_levels(stream_key, extent, cuts, low, high):
    gain, own = 1.0, jax.random.fold_in(stream_key, 6)
    for position, parts in cuts:
        steps = jnp.exp(jax.random.uniform(jax.random.fold_in(own, position), (parts,), jnp.float32, low / len(cuts), high / len(cuts)))
        gain = gain * jnp.repeat(steps, extent[position] // parts).reshape([-1 if axis == position else 1 for axis in range(len(extent))])
    return gain


def normal_values(stream_key, extent, spread, reach, pieces=(), held_as=jnp.bfloat16):
    drawn = spread * jax.random.normal(stream_key, extent, jnp.float32)
    if pieces:
        drawn = drawn * block_levels(stream_key, extent, pieces, -0.22, 0.18)
    return jnp.clip(drawn, -reach, reach).astype(held_as)


def setup_inputs(seed: int = 0) -> dict:
    streams_of = jax.random.split(jax.random.key(seed), 8)
    lam_tracer = normal_values(streams_of[0], (2, LEVELS, NY, NX), 1.0, 6.0, ((2, 8), (3, 16)), jnp.float32)
    tracer = normal_values(streams_of[1], (2, LEVELS, NY, NX), 1.0, 6.0, ((2, 8), (3, 16)), jnp.float32)
    velocity = normal_values(streams_of[2], (2, LEVELS, NY, NX), 1.0, 4.0, ((2, 8), (3, 16)), jnp.float32)
    diffusivity = jnp.clip(jnp.exp(math.log(20.0) - 3.6888795 * jax.random.uniform(streams_of[3], (LEVELS, NY, NX), jnp.float32) ** block_levels(streams_of[3], (LEVELS, NY, NX), ((1, 8), (2, 16)), -0.2, 0.2)), 0.5, 20.0)
    lam_surface = normal_values(streams_of[4], (NY, NX), 1.0, 6.0, ((0, 8), (1, 16)), jnp.float32)
    sea_depth = jnp.clip(jnp.exp(math.log(5.0) - 3.218876 * jax.random.uniform(streams_of[5], (NY, NX), jnp.float32) ** block_levels(streams_of[5], (NY, NX), ((0, 8), (1, 16)), -0.2, 0.2)), 0.2, 5.0)
    levels = draw_levels(jax.random.fold_in(streams_of[7], 71), 0)
    return {"lam_tracer": lam_tracer, "tracer": tracer, "velocity": velocity, "diffusivity": diffusivity, "lam_surface": lam_surface, "sea_depth": sea_depth, "levels": levels}


SURFACE_DAMPING = 0.05
COURANT = 0.25
GAIN_HEAT = 0.7
GAIN_SALT = -0.5

def to_east(field):
    return jnp.roll(field, -1, axis=-1)

def to_west(field):
    return jnp.roll(field, 1, axis=-1)

def to_north(field):
    zero_row = jnp.zeros_like(field[..., :1, :])
    return jnp.concatenate([field[..., 1:, :], zero_row], axis=-2)

def to_south(field):
    zero_row = jnp.zeros_like(field[..., :1, :])
    return jnp.concatenate([zero_row, field[..., :-1, :]], axis=-2)

def column_solve(right_side, coupling):
    level_count = coupling.shape[0]
    ratios = []
    values = []
    ratio_prev = jnp.zeros_like(coupling[0])
    value_prev = jnp.zeros_like(right_side[:, 0])
    for level_idx in range(level_count):
        above_coef = coupling[level_idx]
        if level_idx > 0:
            below_coef = coupling[level_idx - 1]
        else:
            below_coef = jnp.zeros_like(above_coef)
        denominator = 1.0 + below_coef + above_coef + below_coef * ratio_prev
        ratio_prev = -above_coef / denominator
        value_prev = (right_side[:, level_idx] + below_coef * value_prev) / denominator
        ratios.append(ratio_prev)
        values.append(value_prev)
    results = [None] * level_count
    following = jnp.zeros_like(value_prev)
    for level_idx in range(level_count - 1, -1, -1):
        following = values[level_idx] - ratios[level_idx] * following
        results[level_idx] = following
    return jnp.stack(results, axis=1)

def surface_operator(field, sea_surface, face_east, face_west, face_north, face_south, east_field, west_field, north_field, south_field):
    return field * (1.0 - sea_surface) + SURFACE_DAMPING * sea_surface * field + face_east * (field - east_field) + face_west * (field - west_field) + face_north * (field - north_field) + face_south * (field - south_field)

def reference(lam_tracer, tracer, velocity, diffusivity, lam_surface, sea_depth, levels):
    level_ids = jnp.arange(LEVELS, dtype=jnp.int32)[:, None, None]
    wet_cells = (level_ids < levels[None]).astype(jnp.float32)
    sea_surface = (levels > 0).astype(jnp.float32)
    wet_below = jnp.concatenate([wet_cells[1:], jnp.zeros_like(wet_cells[:1])], axis=0)
    mixed = column_solve(wet_cells[None] * lam_tracer, diffusivity * wet_below)
    forcing = sea_surface * (lam_surface + (GAIN_HEAT * lax.optimization_barrier(jnp.sum(mixed[0], axis=0)) + GAIN_SALT * lax.optimization_barrier(jnp.sum(mixed[1], axis=0))) / math.sqrt(LEVELS))
    face_east = 0.5 * (sea_depth + to_east(sea_depth)) * sea_surface * to_east(sea_surface)
    face_west = 0.5 * (sea_depth + to_west(sea_depth)) * sea_surface * to_west(sea_surface)
    face_north = 0.5 * (sea_depth + to_north(sea_depth)) * sea_surface * to_north(sea_surface)
    face_south = 0.5 * (sea_depth + to_south(sea_depth)) * sea_surface * to_south(sea_surface)

    def operate(field):
        return surface_operator(field, sea_surface, face_east, face_west, face_north, face_south, to_east(field), to_west(field), to_north(field), to_south(field))
    solution = jnp.zeros_like(forcing)
    residual = forcing
    direction = forcing
    norm_now = jnp.sum(residual * residual)
    for step_idx in range(ITERS):
        image_field = operate(direction)
        step_size = norm_now / jnp.sum(direction * image_field)
        solution = solution + step_size * direction
        residual = residual - step_size * image_field
        norm_next = jnp.sum(residual * residual)
        direction = residual + norm_next / norm_now * direction
        norm_now = norm_next
    tracer_gains = jnp.array([GAIN_HEAT, GAIN_SALT], dtype=jnp.float32)[:, None, None, None]
    adjoint = mixed + tracer_gains * wet_cells[None] * solution[None, None]
    zonal = velocity[0]
    meridional = velocity[1]

    def zonal_sweep(field):
        flux_field = zonal * field
        return field + COURANT * wet_cells * (to_east(flux_field) - to_west(flux_field))

    def meridional_sweep(field):
        flux_field = meridional * field
        return field + COURANT * wet_cells * (to_north(flux_field) - to_south(flux_field))
    adjoint = zonal_sweep(adjoint)
    adjoint = meridional_sweep(adjoint)
    adjoint = meridional_sweep(adjoint)
    adjoint = zonal_sweep(adjoint)
    lam_zonal = -COURANT * wet_cells * (adjoint[0] * (to_east(tracer[0]) - to_west(tracer[0])) + adjoint[1] * (to_east(tracer[1]) - to_west(tracer[1])))
    lam_meridional = -COURANT * wet_cells * (adjoint[0] * (to_north(tracer[0]) - to_south(tracer[0])) + adjoint[1] * (to_north(tracer[1]) - to_south(tracer[1])))
    return (adjoint, jnp.stack([lam_zonal, lam_meridional]), solution)
```

```python
import math

import jax
import jax.numpy as jnp
from jax import lax
from jax.experimental import pallas as pl
from jax.experimental.pallas import tpu as pltpu
from jax.sharding import PartitionSpec as P

LEVELS = 50
SURFACE_DAMPING = 0.05
COURANT = 0.25
GAINS = (0.7, -0.5)
ROWS = 32
COLS = 128
HALF = LEVELS // 2
SLOTS = 32
FIELDS = 6
GROUPS = -(-LEVELS // 4)
VMEM_LIMIT = 56 * 1024 * 1024
F32 = jnp.float32
VMEM = pltpu.VMEM

PAIRS = tuple((i, j) for i in range(4) for j in range(i, 5))


def iota(shape, dim):
    return lax.broadcasted_iota(jnp.int32, shape, dim)


def pick(parity, even, odd):
    return jnp.where(jnp.broadcast_to(parity, even.shape) == 0, even, odd)


def roll(x, shift, axis):
    return pltpu.roll(x, shift, axis)


def two_sum(a, b):
    s = a + b
    bb = s - a
    return s, (a - (s - bb)) + (b - bb)


def quick_sum(a, b):
    s = a + b
    return s, b - (s - a)


def split(a):
    t = 4097.0 * a
    hi = t - (t - a)
    return hi, a - hi


def two_prod(a, b, sa=None, sb=None):
    ah, al = sa or split(a)
    bh, bl = sb or split(b)
    p = a * b
    return p, ((ah * bh - p) + ah * bl + al * bh) + al * bl


def dd_add(a, b):
    s, e = two_sum(a[0], b[0])
    return quick_sum(s, e + (a[1] + b[1]))


def dd_mul(a, b):
    p, e = two_prod(a[0], b[0])
    return quick_sum(p, e + (a[0] * b[1] + a[1] * b[0]))


def dd_neg(a):
    return -a[0], -a[1]


def dd_inv(a):
    r = 1.0 / a[0]
    p, e = two_prod(a[0], r)
    rest = ((1.0 - p) - e) - a[1] * r
    return quick_sum(r, r * rest)


def solve_kernel(
    lam_h, vel_h, tr_h, dif_h, lams_ref, depth_ref, lev_ref,
    mixed_ref, f_ref, osm_ref, big1_ref, big2_ref, slots_ref, g1_ref, g2_ref,
    lam, vel, tr, dif, w_s, z_s, col_sem, rest_sem,
):
    lon_par = lax.rem(lax.axis_index("lon"), 2)
    lat_par = lax.rem(lax.axis_index("lat"), 2)
    step = 5
    copies = []
    for i in range(HALF // step):
        top, low = i * step, LEVELS - (i + 1) * step
        part = []
        for n, at in enumerate((top, low)):
            part.append(pltpu.make_async_copy(dif_h.at[pl.ds(at, step)], dif.at[pl.ds(at, step)], col_sem.at[i, 2 * n]))
            part.append(pltpu.make_async_copy(lam_h.at[:, pl.ds(at, step)], lam.at[:, pl.ds(at, step)], col_sem.at[i, 2 * n + 1]))
        copies.append(part)
    for part in copies:
        for c in part:
            c.start()
    rest = [
        pltpu.make_async_copy(vel_h, vel, rest_sem.at[0]),
        pltpu.make_async_copy(tr_h, tr, rest_sem.at[1]),
    ]
    for c in rest:
        c.start()

    lev = lev_ref[...]
    zero = jnp.zeros((ROWS, COLS), F32)

    def coef(k):
        return jnp.where(lev > k + 1, dif[k], 0.0)

    def right(n, k):
        return jnp.where(lev > k, lam[n, k], 0.0)

    e = jnp.ones((ROWS, COLS), F32)
    y = [zero, zero]
    w = zero
    eb = e
    yb = [zero, zero]
    wb = zero
    cb = zero
    waited = 0
    for k in range(HALF):
        need = min((k + 1) // step, HALF // step - 1)
        while waited <= need:
            for c in copies[waited]:
                c.wait()
            waited += 1
        c_k = coef(k)
        y = [right(n, k) + w * y[n] for n in range(2)]
        inv = 1.0 / (e + c_k)
        w = c_k * inv
        w_s[k] = w
        for n in range(2):
            z_s[n, k] = y[n] * inv
        e = 1.0 + e * w
        if k < HALF - 1:
            m = LEVELS - 1 - k
            c_m = coef(m - 1)
            yb = [right(n, m) + wb * yb[n] for n in range(2)]
            invb = 1.0 / (eb + c_m)
            wb = c_m * invb
            w_s[m] = wb
            for n in range(2):
                z_s[n, m] = yb[n] * invb
            eb = 1.0 + eb * wb
    inv = 1.0 / (e + eb - 1.0)
    below = [(right(n, HALF) + wb * yb[n] + w * y[n]) * inv for n in range(2)]
    total = list(below)
    for n in range(2):
        mixed_ref[n, HALF] = below[n]
    above = list(below)
    for i in range(1, HALF + 1):
        k = HALF - i
        for n in range(2):
            above[n] = z_s[n, k] + w_s[k] * above[n]
            mixed_ref[n, k] = above[n]
            total[n] = total[n] + above[n]
        m = HALF + i
        if m < LEVELS:
            for n in range(2):
                below[n] = z_s[n, m] + w_s[m] * below[n]
                mixed_ref[n, m] = below[n]
                total[n] = total[n] + below[n]
    f = jnp.where(lev > 0, lams_ref[...] + (GAINS[0] * total[0] + GAINS[1] * total[1]) / math.sqrt(LEVELS), 0.0)
    f_ref[...] = f
    lane = iota((ROWS, COLS), 1)
    osm = jnp.where(
        lane < 16, roll(f, 8, 1), jnp.where(lane < 32, roll(depth_ref[...], 24, 1), roll(lev.astype(F32), 40, 1))
    )
    osm_ref[...] = osm

    for c in rest:
        c.wait()

    sources = (
        lambda k: mixed_ref[0, k], lambda k: mixed_ref[1, k], lambda k: vel[0, k],
        lambda k: vel[1, k], lambda k: tr[0, k], lambda k: tr[1, k],
    )
    slot = lane // 4
    for tile in range(2):
        count = min(SLOTS, LEVELS - tile * SLOTS)

        def gather(s, acc, tile=tile):
            here = slot == s
            return tuple(jnp.where(here, roll(src(s + tile * SLOTS), 4 * s + 2, 1), a) for src, a in zip(sources, acc))

        got = lax.fori_loop(0, count, gather, (zero,) * FIELDS)
        for i in range(FIELDS):
            slots_ref[i, tile] = got[i]
    near = lane % 4 < 2
    for i in range(FIELDS):
        a, b = slots_ref[i, 0], slots_ref[i, 1]
        east_edge = jnp.where(near, a, roll(b, 2, 1))
        west_edge = jnp.where(near, roll(a, COLS - 2, 1), b)
        big1_ref[i] = pick(lon_par, east_edge, west_edge)
        big2_ref[i] = pick(lon_par, west_edge, east_edge)

    pair = iota((8, COLS), 0) // 2
    for i, src in enumerate(sources):
        for g in range(GROUPS):
            first = jnp.zeros((8, COLS), F32)
            last = first
            for q in range(min(4, LEVELS - 4 * g)):
                tile = src(4 * g + q)
                first = jnp.where(pair == q, roll(tile[:8], 2 * q, 0) if q else tile[:8], first)
                last = jnp.where(pair == (q + 3) % 4, roll(tile[ROWS - 8 :], 2 * q, 0) if q else tile[ROWS - 8 :], last)
            g1_ref[i * GROUPS + g] = pick(lat_par, last, first)
            g2_ref[i * GROUPS + g] = pick(lat_par, first, last)


CORNERS = 4


def lon_kernel(
    f_ref, depth_ref, lev_ref, o1_ref, o2_ref, slots_ref, b1_ref, b2_ref, g1_ref, g2_ref,
    ext_ref, s1_ref, s2_ref, side_ref, h1_ref, h2_ref,
):
    lon_par = lax.rem(lax.axis_index("lon"), 2)
    lat_par = lax.rem(lax.axis_index("lat"), 2)
    lane = iota((ROWS, COLS), 1)
    o1, o2 = o1_ref[...], o2_ref[...]
    from_east, from_west = pick(lon_par, o1, o2), pick(lon_par, o2, o1)
    for i, own in enumerate((f_ref[...], depth_ref[...], lev_ref[...].astype(F32))):
        edge = jnp.where(lane < 16 * i + 8, from_west, from_east)
        edge = roll(edge, COLS - 8 - 16 * i, 1)
        edge = jnp.where((lane < 8) | (lane >= COLS - 8), edge, 0.0)
        ext_ref[i, :, :COLS] = own
        ext_ref[i, :, COLS:] = edge
        for at, here in ((0, own), (COLS, edge)):
            first, last = here[:8], here[ROWS - 8 :]
            s1_ref[i, :, at : at + COLS] = pick(lat_par, last, first)
            s2_ref[i, :, at : at + COLS] = pick(lat_par, first, last)
    near = lane % 4 < 2
    for i in range(FIELDS):
        b1, b2 = b1_ref[i], b2_ref[i]
        east, west = pick(lon_par, b1, b2), pick(lon_par, b2, b1)
        own_a, own_b = slots_ref[i, 0], slots_ref[i, 1]
        side_ref[0, i, 0] = jnp.where(near, west, own_a)
        side_ref[0, i, 1] = jnp.where(near, roll(west, COLS - 2, 1), own_b)
        side_ref[1, i, 0] = jnp.where(near, own_a, roll(east, 2, 1))
        side_ref[1, i, 1] = jnp.where(near, own_b, east)
    h1_ref[: FIELDS * GROUPS] = g1_ref[...]
    h2_ref[: FIELDS * GROUPS] = g2_ref[...]
    pair = iota((8, COLS), 0) // 2
    for c in range(CORNERS):
        first = jnp.zeros((8, COLS), F32)
        last = first
        for q in range(4):
            side, field, tile = corner_of(4 * c + q)
            x = side_ref[side, field, tile]
            first = jnp.where(pair == q, roll(x[:8], 2 * q, 0) if q else x[:8], first)
            last = jnp.where(pair == (q + 3) % 4, roll(x[ROWS - 8 :], 2 * q, 0) if q else x[ROWS - 8 :], last)
        h1_ref[FIELDS * GROUPS + c] = pick(lat_par, last, first)
        h2_ref[FIELDS * GROUPS + c] = pick(lat_par, first, last)


def corner_of(index):
    return index // 8, index // 2 % 4, index % 2


def krylov_kernel(ext_ref, s1_ref, s2_ref, vec_ref, lev_ref, gram_ref):
    lat_par = lax.rem(lax.axis_index("lat"), 2)
    rows, cols = ROWS + 16, 2 * COLS
    whole = []
    for i in range(3):
        s1, s2 = s1_ref[i], s2_ref[i]
        whole.append(jnp.concatenate([ext_ref[i], pick(lat_par, s1, s2), pick(lat_par, s2, s1)], axis=0))
    f, depth, lev = whole

    def east(x):
        return roll(x, cols - 1, 1)

    def west(x):
        return roll(x, 1, 1)

    def north(x):
        return roll(x, rows - 1, 0)

    def south(x):
        return roll(x, 1, 0)

    sea = jnp.where(lev > 0.0, 1.0, 0.0)
    face_east = 0.5 * (depth + east(depth)) * sea * east(sea)
    face_north = 0.5 * (depth + north(depth)) * sea * north(sea)
    base = (1.0 - sea) + SURFACE_DAMPING * sea
    sub = iota((8, cols), 0)

    def trim(x):
        return jnp.concatenate([x[:ROWS], jnp.where(sub < 4, x[ROWS : ROWS + 8], x[ROWS + 8 :])], axis=0)

    lev_ref[...] = trim(lev)
    vectors = [f]
    vec_ref[0] = trim(f)
    for i in range(1, 5):
        p = vectors[-1]
        flow_east = face_east * (p - east(p))
        flow_north = face_north * (p - north(p))
        p = base * p + (flow_east - west(flow_east)) + (flow_north - south(flow_north))
        vectors.append(p)
        if i < 4:
            vec_ref[i] = trim(p)
    own = [v[:ROWS, :COLS] for v in vectors]
    parts = [split(v) for v in own]
    row = iota((16, COLS), 0)
    hi = jnp.zeros((16, COLS), F32)
    lo = hi
    for at, (i, j) in enumerate(PAIRS):
        p, e = two_prod(own[i], own[j], parts[i], parts[j])
        quarters = [(p[8 * r : 8 * r + 8], e[8 * r : 8 * r + 8]) for r in range(ROWS // 8)]
        total = dd_add(dd_add(quarters[0], quarters[1]), dd_add(quarters[2], quarters[3]))
        for s in (4, 2, 1):
            total = dd_add(total, (roll(total[0], s, 0), roll(total[1], s, 0)))
        hi = jnp.where(row == at, jnp.concatenate([total[0]] * 2, axis=0), hi)
        lo = jnp.where(row == at, jnp.concatenate([total[1]] * 2, axis=0), lo)
    total = (hi, lo)
    for s in (64, 32, 16, 8, 4, 2, 1):
        total = dd_add(total, (roll(total[0], s, 1), roll(total[1], s, 1)))
    lane = iota((16, COLS), 1)
    line = jnp.where(lane == row, total[0], jnp.where(lane == row + 16, total[1], 0.0))
    line = line[:8] + line[8:]
    for s in (4, 2, 1):
        line = line + roll(line, s, 0)
    gram_ref[...] = jnp.concatenate([line] * (gram_ref.shape[0] // 8), axis=0)


def galerkin(gram):
    rows = gram.shape[0]
    parts = [(gram[8 * r : 8 * r + 8], roll(gram[8 * r : 8 * r + 8], COLS - 16, 1)) for r in range(rows // 8)]
    while len(parts) > 1:
        parts = [dd_add(parts[i], parts[i + 1]) for i in range(0, len(parts) - 1, 2)] + parts[len(parts) // 2 * 2 :]
    total = parts[0]
    for s in (4, 2, 1):
        total = dd_add(total, (roll(total[0], s, 0), roll(total[1], s, 0)))
    entry = {}
    for at, (i, j) in enumerate(PAIRS):
        entry[i, j] = entry[j, i] = tuple(jnp.broadcast_to(t[:, at : at + 1], (8, COLS)) for t in total)
    mat = [[entry[i, j + 1] for j in range(4)] for i in range(4)]
    rhs = [entry[i, 0] for i in range(4)]
    size = [jnp.abs(mat[i][i][0]) for i in range(4)]
    for k in range(4):
        fine = mat[k][k][0] > 1e-12 * size[k]
        inv = dd_inv((jnp.where(fine, mat[k][k][0], 1.0), jnp.where(fine, mat[k][k][1], 0.0)))
        inv = tuple(jnp.where(fine, t, 0.0) for t in inv)
        for j in range(k + 1, 4):
            mat[k][j] = dd_mul(mat[k][j], inv)
        rhs[k] = dd_mul(rhs[k], inv)
        for i in range(k + 1, 4):
            less = dd_neg(mat[i][k])
            for j in range(k + 1, 4):
                mat[i][j] = dd_add(mat[i][j], dd_mul(less, mat[k][j]))
            rhs[i] = dd_add(rhs[i], dd_mul(less, rhs[k]))
    for k in range(2, -1, -1):
        for j in range(k + 1, 4):
            rhs[k] = dd_add(rhs[k], dd_neg(dd_mul(mat[k][j], rhs[j])))
    return [r[0] for r in rhs]


CHUNK = 12
CHUNKS = tuple((c * CHUNK, CHUNK if c < 3 else LEVELS - 3 * CHUNK) for c in range(4))


def final_kernel(
    gram_ref, vec_ref, lev_ref, side_ref, h1_ref, h2_ref, mixed_h, vel_h, tr_h,
    adj_h, avel_h, sol_ref,
    mixed, vel, tr, adj, avel, sol_s, edge1, edge2, edge3, in_sem, out_sem,
):
    lat_par = lax.rem(lax.axis_index("lat"), 2)
    reads = []
    for c, (at, count) in enumerate(CHUNKS):
        part = [
            pltpu.make_async_copy(src.at[:, pl.ds(at, count)], dst.at[:, pl.ds(at, count)], in_sem.at[c, i])
            for i, (src, dst) in enumerate(((mixed_h, mixed), (vel_h, vel), (tr_h, tr)))
        ]
        for r in part:
            r.start()
        reads.append(part)

    coefs = galerkin(gram_ref[...])
    tall = ROWS + 8
    for half in range(2):
        at = half * COLS
        total = 0.0
        for i in range(4):
            wide = jnp.concatenate([coefs[i]] * (tall // 8), axis=0)
            total = total + wide * vec_ref[i, :, at : at + COLS]
        sol_s[:, at : at + COLS] = total
    sol_ref[...] = sol_s[:ROWS, :COLS]

    lane = iota((tall, COLS), 1)
    pair = iota((8, COLS), 0) // 2
    even = jnp.broadcast_to(lat_par, (8, COLS)) == 0
    masks = [(pair == q) == even for q in range(4)]

    def edge_rows(index, q):
        x = jnp.where(masks[q], h1_ref[index], h2_ref[index])
        return roll(x, 8 - 2 * q, 0) if q else x

    flux1, flux2 = [], []
    for side in range(2):
        def around(ref):
            own, edge = roll(ref[:, :COLS], 2, 1), roll(ref[:, COLS:], 2, 1)
            x = jnp.where(lane < 2, own, edge) if side else jnp.where(lane < 2, edge, own)
            for s in (4, 8, 16, 32, 64):
                x = jnp.where(lane < s, x, roll(x, s, 1))
            return x

        levels, pressure = around(lev_ref), around(sol_s)
        for tile in range(2):
            def column(field):
                index = side * 8 + field * 2 + tile
                return jnp.concatenate(
                    [side_ref[side, field, tile], edge_rows(FIELDS * GROUPS + index // 4, index % 4)], axis=0
                )

            wet = jnp.where((lane // 4 + tile * SLOTS).astype(F32) < levels, 1.0, 0.0)
            move = COURANT * wet
            u, v = column(2), column(3)
            for n in range(2):
                x = column(n) + GAINS[n] * wet * pressure
                flux = u * x
                flux1.append(flux)
                x = x + move * (roll(flux, COLS - 1, 1) - roll(flux, 1, 1))
                for _ in range(2):
                    flux = v * x
                    x = x + move * (roll(flux, tall - 1, 0) - roll(flux, 1, 0))
                flux2.append(u * x)
    own_rows = iota((ROWS, COLS), 1) % 4 == 2
    for tile in range(2):
        for n in range(2):
            west, east = tile * 2 + n, 4 + tile * 2 + n
            edge1[n, tile] = jnp.where(lane % 4 == 2, flux1[east], roll(flux1[west], 2, 1))
            edge2[n, tile] = jnp.where(lane % 4 == 2, flux2[east], roll(flux2[west], 2, 1))[:ROWS]
            edge3[n, tile] = jnp.where(own_rows, side_ref[1, 4 + n, tile], roll(side_ref[0, 4 + n, tile], 2, 1))

    def zonal(x, edge, shift):
        width = x.shape[0]
        at = lane[:width]
        around = roll(edge, shift, 1)
        high = jnp.where(at == COLS - 1, around, roll(x, COLS - 1, 1))
        low = jnp.where(at == 0, around, roll(x, 1, 1))
        return high - low

    def meridional(x):
        return roll(x, tall - 1, 0) - roll(x, 1, 0)

    def one_level(g, q):
        k = 4 * g + q
        tile, slot = k // SLOTS, lax.rem(k, SLOTS)
        shift = COLS - 3 - 4 * slot
        wet = jnp.where(k.astype(F32) < lev_ref[:, :COLS], 1.0, 0.0)
        move = COURANT * wet
        wet_sol = wet * sol_s[:, :COLS]

        def tall_field(ref, n, field):
            return jnp.concatenate([ref[n, k], edge_rows(field * GROUPS + g, q)], axis=0)

        u, v = tall_field(vel, 0, 2), tall_field(vel, 1, 3)
        east_sum, north_sum = 0.0, 0.0
        for n in range(2):
            x = tall_field(mixed, n, n) + GAINS[n] * wet_sol
            x = x + move * zonal(u * x, edge1[n, tile], shift)
            x = x + move * meridional(v * x)
            x = (x + move * meridional(v * x))[:ROWS]
            x = x + move[:ROWS] * zonal(u[:ROWS] * x, edge2[n, tile], shift)
            adj[n, k] = x
            t = tall_field(tr, n, 4 + n)
            east_sum = east_sum + x * zonal(t[:ROWS], edge3[n, tile], shift)
            north_sum = north_sum + x * meridional(t)[:ROWS]
        avel[0, k] = -move[:ROWS] * east_sum
        avel[1, k] = -move[:ROWS] * north_sum

    writes = []
    for c, (at, count) in enumerate(CHUNKS):
        for r in reads[c]:
            r.wait()

        def group(g, carry):
            for q in range(4):
                one_level(g, q)
            return carry

        lax.fori_loop(at // 4, (at + count) // 4, group, 0)
        for q in range(count % 4):
            one_level(jnp.int32(GROUPS - 1), q)
        for i, (src, dst) in enumerate(((adj, adj_h), (avel, avel_h))):
            copy = pltpu.make_async_copy(src.at[:, pl.ds(at, count)], dst.at[:, pl.ds(at, count)], out_sem.at[c, i])
            copy.start()
            writes.append(copy)
    for copy in writes:
        copy.wait()


def swaps(size, first, periodic):
    out = []
    for i in range(first, size, 2):
        if i + 1 < size or periodic:
            out += [(i, (i + 1) % size), ((i + 1) % size, i)]
    return out


def shape(*dims):
    return jax.ShapeDtypeStruct(dims, F32)


def call(kernel, name, outs, in_any, out_any, scratch, args):
    here, there = pl.BlockSpec(memory_space=VMEM), pl.BlockSpec(memory_space=pl.ANY)
    return pl.pallas_call(
        kernel,
        name=name,
        out_shape=outs,
        in_specs=[there if i in in_any else here for i in range(len(args))],
        out_specs=tuple(there if i in out_any else here for i in range(len(outs))),
        scratch_shapes=scratch,
        compiler_params=pltpu.CompilerParams(vmem_limit_bytes=VMEM_LIMIT),
    )(*args)


def per_device(lam_tracer, tracer, velocity, diffusivity, lam_surface, sea_depth, levels):
    lon, lat = lax.axis_size("lon"), lax.axis_size("lat")
    tile = (ROWS, COLS)
    deep = (2, LEVELS) + tile
    mixed, f, osm, big1, big2, slots, g1, g2 = call(
        solve_kernel, "column_solve",
        (shape(*deep), shape(*tile), shape(*tile), shape(FIELDS, *tile), shape(FIELDS, *tile),
         shape(FIELDS, 2, *tile), shape(FIELDS * GROUPS, 8, COLS), shape(FIELDS * GROUPS, 8, COLS)),
        (0, 1, 2, 3), (),
        [VMEM(deep, F32), VMEM(deep, F32), VMEM(deep, F32), VMEM((LEVELS,) + tile, F32), VMEM((LEVELS,) + tile, F32),
         VMEM(deep, F32), pltpu.SemaphoreType.DMA((HALF // 5, 4)), pltpu.SemaphoreType.DMA((2,))],
        (lam_tracer, velocity, tracer, diffusivity, lam_surface, sea_depth, levels),
    )
    even_lon, odd_lon = swaps(lon, 0, True), swaps(lon, 1, True)
    even_lat, odd_lat = swaps(lat, 0, False), swaps(lat, 1, False)
    o1, b1 = lax.ppermute(osm, "lon", even_lon), lax.ppermute(big1, "lon", even_lon)
    o2, b2 = lax.ppermute(osm, "lon", odd_lon), lax.ppermute(big2, "lon", odd_lon)
    height = FIELDS * GROUPS + CORNERS
    ext, s1, s2, side, h1, h2 = call(
        lon_kernel, "after_lon",
        (shape(3, ROWS, 2 * COLS), shape(3, 8, 2 * COLS), shape(3, 8, 2 * COLS), shape(2, FIELDS, 2, *tile),
         shape(height, 8, COLS), shape(height, 8, COLS)),
        (), (), [],
        (f, sea_depth, levels, o1, o2, slots, b1, b2, g1, g2),
    )
    s1, h1 = lax.ppermute(s1, "lat", even_lat), lax.ppermute(h1, "lat", even_lat)
    s2, h2 = lax.ppermute(s2, "lat", odd_lat), lax.ppermute(h2, "lat", odd_lat)
    vec, lev, gram = call(
        krylov_kernel, "krylov",
        (shape(4, ROWS + 8, 2 * COLS), shape(ROWS + 8, 2 * COLS), shape(lon * lat, COLS)),
        (), (), [],
        (ext, s1, s2),
    )
    gram = lax.all_to_all(gram, ("lon", "lat"), 0, 0, tiled=True)
    adjoint, adjoint_velocity, pressure = call(
        final_kernel, "sweeps",
        (shape(*deep), shape(*deep), shape(*tile)),
        (6, 7, 8), (0, 1),
        [VMEM(deep, F32)] * 5
        + [VMEM((ROWS + 8, 2 * COLS), F32), VMEM((2, 2, ROWS + 8, COLS), F32), VMEM((2, 2) + tile, F32), VMEM((2, 2) + tile, F32),
           pltpu.SemaphoreType.DMA((4, 3)), pltpu.SemaphoreType.DMA((4, 2))],
        (gram, vec, lev, side, h1, h2, mixed, velocity, tracer),
    )
    return adjoint, adjoint_velocity, pressure


def solution(mesh):
    deep, flat = P(None, None, "lat", "lon"), P("lat", "lon")
    return jax.shard_map(
        per_device,
        mesh=mesh,
        in_specs=(deep, deep, deep, P(None, "lat", "lon"), flat, flat, flat),
        out_specs=(deep, deep, flat),
        check_vma=False,
    )
```

```python
import math

import jax
import jax.numpy as jnp
from jax import lax
from jax.experimental import pallas as pl
from jax.experimental.pallas import tpu as pltpu
from jax.sharding import PartitionSpec as P

LEVELS = 50
SURFACE_DAMPING = 0.05
COURANT = 0.25
GAINS = (0.7, -0.5)
ROWS = 32
COLS = 128
HALF = LEVELS // 2
SLOTS = 32
FIELDS = 6
GROUPS = -(-LEVELS // 4)
VMEM_LIMIT = 56 * 1024 * 1024
F32 = jnp.float32
VMEM = pltpu.VMEM

PAIRS = tuple((i, j) for i in range(4) for j in range(i, 5))


def iota(shape, dim):
    return lax.broadcasted_iota(jnp.int32, shape, dim)


def pick(parity, even, odd):
    return jnp.where(jnp.broadcast_to(parity, even.shape) == 0, even, odd)


def roll(x, shift, axis):
    return pltpu.roll(x, shift, axis)


def two_sum(a, b):
    s = a + b
    bb = s - a
    return s, (a - (s - bb)) + (b - bb)


def quick_sum(a, b):
    s = a + b
    return s, b - (s - a)


def split(a):
    t = 4097.0 * a
    hi = t - (t - a)
    return hi, a - hi


def two_prod(a, b, sa=None, sb=None):
    ah, al = sa or split(a)
    bh, bl = sb or split(b)
    p = a * b
    return p, ((ah * bh - p) + ah * bl + al * bh) + al * bl


def dd_add(a, b):
    s, e = two_sum(a[0], b[0])
    return quick_sum(s, e + (a[1] + b[1]))


def dd_mul(a, b):
    p, e = two_prod(a[0], b[0])
    return quick_sum(p, e + (a[0] * b[1] + a[1] * b[0]))


def dd_neg(a):
    return -a[0], -a[1]


def dd_inv(a):
    r = 1.0 / a[0]
    p, e = two_prod(a[0], r)
    rest = ((1.0 - p) - e) - a[1] * r
    return quick_sum(r, r * rest)


def solve_kernel(
    lam_h, vel_h, tr_h, dif_h, lams_h, depth_h, lev_h,
    mixed_ref, vel, tr, base_ref, lon1_ref, lon2_ref, slots_ref, g1_ref, g2_ref,
    lam, dif, lams_s, lev_s, w_s, z_s, col_sem, rest_sem,
):
    lon_par = lax.rem(lax.axis_index("lon"), 2)
    lat_par = lax.rem(lax.axis_index("lat"), 2)
    step = 5
    flat = [
        pltpu.make_async_copy(lev_h, lev_s, rest_sem.at[0]),
        pltpu.make_async_copy(lams_h, lams_s, rest_sem.at[1]),
        pltpu.make_async_copy(depth_h, base_ref.at[1], rest_sem.at[2]),
    ]
    copies = []
    for i in range(HALF // step):
        top, low = i * step, LEVELS - (i + 1) * step
        part = []
        for n, at in enumerate((top, low)):
            part.append(pltpu.make_async_copy(dif_h.at[pl.ds(at, step)], dif.at[pl.ds(at, step)], col_sem.at[i, 2 * n]))
            part.append(pltpu.make_async_copy(lam_h.at[:, pl.ds(at, step)], lam.at[:, pl.ds(at, step)], col_sem.at[i, 2 * n + 1]))
        copies.append(part)
    rest = [
        pltpu.make_async_copy(vel_h, vel.at[:, pl.ds(0, LEVELS)], rest_sem.at[3]),
        pltpu.make_async_copy(tr_h, tr.at[:, pl.ds(0, LEVELS)], rest_sem.at[4]),
    ]
    for c in flat + sum(copies, []) + rest:
        c.start()
    for c in flat:
        c.wait()

    lev = lev_s[...]
    zero = jnp.zeros((ROWS, COLS), F32)

    def coef(k):
        return jnp.where(lev > k + 1, dif[k], 0.0)

    def right(n, k):
        return jnp.where(lev > k, lam[n, k], 0.0)

    e = jnp.ones((ROWS, COLS), F32)
    y = [zero, zero]
    w = zero
    eb = e
    yb = [zero, zero]
    wb = zero
    waited = 0
    for k in range(HALF):
        need = min((k + 1) // step, HALF // step - 1)
        while waited <= need:
            for c in copies[waited]:
                c.wait()
            waited += 1
        c_k = coef(k)
        y = [right(n, k) + w * y[n] for n in range(2)]
        inv = 1.0 / (e + c_k)
        w = c_k * inv
        w_s[k] = w
        for n in range(2):
            z_s[n, k] = y[n] * inv
        e = 1.0 + e * w
        if k < HALF - 1:
            m = LEVELS - 1 - k
            c_m = coef(m - 1)
            yb = [right(n, m) + wb * yb[n] for n in range(2)]
            invb = 1.0 / (eb + c_m)
            wb = c_m * invb
            w_s[m] = wb
            for n in range(2):
                z_s[n, m] = yb[n] * invb
            eb = 1.0 + eb * wb
    for c in rest:
        c.wait()

    lane = iota((ROWS, COLS), 1)
    slot = lane // 4
    begun = set()

    def gather(k, fields):
        tile, s = divmod(k, SLOTS)
        here = slot == s
        for i, x in enumerate(fields):
            before = slots_ref[i, tile] if (i, tile) in begun else zero
            begun.add((i, tile))
            slots_ref[i, tile] = jnp.where(here, roll(x, 4 * s + 2, 1), before)

    def level_done(k, solved):
        for n in range(2):
            mixed_ref[n, k] = solved[n]
        gather(k, (solved[0], solved[1], vel[0, k], vel[1, k], tr[0, k], tr[1, k]))

    inv = 1.0 / (e + eb - 1.0)
    below = [(right(n, HALF) + wb * yb[n] + w * y[n]) * inv for n in range(2)]
    total = list(below)
    level_done(HALF, below)
    above = list(below)
    for i in range(1, HALF + 1):
        k = HALF - i
        for n in range(2):
            above[n] = z_s[n, k] + w_s[k] * above[n]
            total[n] = total[n] + above[n]
        level_done(k, above)
        m = HALF + i
        if m < LEVELS:
            for n in range(2):
                below[n] = z_s[n, m] + w_s[m] * below[n]
                total[n] = total[n] + below[n]
            level_done(m, below)
    f = jnp.where(lev > 0, lams_s[...] + (GAINS[0] * total[0] + GAINS[1] * total[1]) / math.sqrt(LEVELS), 0.0)
    levels = lev.astype(F32)
    base_ref[0] = f
    base_ref[2] = levels
    small = jnp.where(lane < 16, roll(f, 8, 1), jnp.where(lane < 32, roll(base_ref[1], 24, 1), roll(levels, 40, 1)))
    lon1_ref[FIELDS] = small
    lon2_ref[FIELDS] = small
    near = lane % 4 < 2
    for i in range(FIELDS):
        a, b = slots_ref[i, 0], slots_ref[i, 1]
        east_edge = jnp.where(near, a, roll(b, 2, 1))
        west_edge = jnp.where(near, roll(a, COLS - 2, 1), b)
        lon1_ref[i] = pick(lon_par, east_edge, west_edge)
        lon2_ref[i] = pick(lon_par, west_edge, east_edge)

    pair = iota((8, COLS), 0) // 2
    for i, src in enumerate((mixed_ref, mixed_ref, vel, vel, tr, tr)):
        for g in range(GROUPS):
            first = jnp.zeros((8, COLS), F32)
            last = first
            for q in range(min(4, LEVELS - 4 * g)):
                top, end = src[i % 2, 4 * g + q, :8], src[i % 2, 4 * g + q, ROWS - 8 :]
                first = jnp.where(pair == q, roll(top, 2 * q, 0) if q else top, first)
                last = jnp.where(pair == (q + 3) % 4, roll(end, 2 * q, 0) if q else end, last)
            g1_ref[i * GROUPS + g] = pick(lat_par, last, first)
            g2_ref[i * GROUPS + g] = pick(lat_par, first, last)


CORNERS = 4
EDGES = FIELDS * GROUPS + CORNERS


def corner_of(index):
    return index // 8, index // 2 % 4, index % 2


def lon_kernel(
    base_ref, o1_ref, o2_ref, slots_ref, g1_ref, g2_ref,
    ext_ref, lat1_ref, s2_ref, h2_ref, side_ref,
):
    lon_par = lax.rem(lax.axis_index("lon"), 2)
    lat_par = lax.rem(lax.axis_index("lat"), 2)
    lane = iota((ROWS, COLS), 1)
    o1, o2 = o1_ref[FIELDS], o2_ref[FIELDS]
    from_east, from_west = pick(lon_par, o1, o2), pick(lon_par, o2, o1)
    for i in range(3):
        own = base_ref[i]
        edge = jnp.where(lane < 16 * i + 8, from_west, from_east)
        edge = roll(edge, COLS - 8 - 16 * i, 1)
        edge = jnp.where((lane < 8) | (lane >= COLS - 8), edge, 0.0)
        ext_ref[i, :, :COLS] = own
        ext_ref[i, :, COLS:] = edge
        for half, here in enumerate((own, edge)):
            first, last = here[:8], here[ROWS - 8 :]
            lat1_ref[EDGES + 2 * i + half] = pick(lat_par, last, first)
            s2_ref[2 * i + half] = pick(lat_par, first, last)
    near = lane % 4 < 2
    for i in range(FIELDS):
        b1, b2 = o1_ref[i], o2_ref[i]
        east, west = pick(lon_par, b1, b2), pick(lon_par, b2, b1)
        own_a, own_b = slots_ref[i, 0], slots_ref[i, 1]
        side_ref[0, i, 0] = jnp.where(near, west, own_a)
        side_ref[0, i, 1] = jnp.where(near, roll(west, COLS - 2, 1), own_b)
        side_ref[1, i, 0] = jnp.where(near, own_a, roll(east, 2, 1))
        side_ref[1, i, 1] = jnp.where(near, own_b, east)
    lat1_ref[: FIELDS * GROUPS] = g1_ref[...]
    h2_ref[: FIELDS * GROUPS] = g2_ref[...]
    pair = iota((8, COLS), 0) // 2
    for c in range(CORNERS):
        first = jnp.zeros((8, COLS), F32)
        last = first
        for q in range(4):
            side, field, tile = corner_of(4 * c + q)
            x = side_ref[side, field, tile]
            first = jnp.where(pair == q, roll(x[:8], 2 * q, 0) if q else x[:8], first)
            last = jnp.where(pair == (q + 3) % 4, roll(x[ROWS - 8 :], 2 * q, 0) if q else x[ROWS - 8 :], last)
        lat1_ref[FIELDS * GROUPS + c] = pick(lat_par, last, first)
        h2_ref[FIELDS * GROUPS + c] = pick(lat_par, first, last)


def krylov_kernel(ext_ref, lat1_ref, s2_ref, vec_ref, lev_ref, gram_ref):
    lat_par = lax.rem(lax.axis_index("lat"), 2)
    rows, cols = ROWS + 16, 2 * COLS
    whole = []
    for i in range(3):
        s1 = jnp.concatenate([lat1_ref[EDGES + 2 * i], lat1_ref[EDGES + 2 * i + 1]], axis=1)
        s2 = jnp.concatenate([s2_ref[2 * i], s2_ref[2 * i + 1]], axis=1)
        whole.append(jnp.concatenate([ext_ref[i], pick(lat_par, s1, s2), pick(lat_par, s2, s1)], axis=0))
    f, depth, lev = whole

    def east(x):
        return roll(x, cols - 1, 1)

    def west(x):
        return roll(x, 1, 1)

    def north(x):
        return roll(x, rows - 1, 0)

    def south(x):
        return roll(x, 1, 0)

    sea = jnp.where(lev > 0.0, 1.0, 0.0)
    face_east = 0.5 * (depth + east(depth)) * sea * east(sea)
    face_north = 0.5 * (depth + north(depth)) * sea * north(sea)
    base = (1.0 - sea) + SURFACE_DAMPING * sea
    sub = iota((8, cols), 0)

    def trim(x):
        return jnp.concatenate([x[:ROWS], jnp.where(sub < 4, x[ROWS : ROWS + 8], x[ROWS + 8 :])], axis=0)

    lev_ref[...] = trim(lev)
    vectors = [f]
    vec_ref[0] = trim(f)
    for i in range(1, 5):
        p = vectors[-1]
        flow_east = face_east * (p - east(p))
        flow_north = face_north * (p - north(p))
        p = base * p + (flow_east - west(flow_east)) + (flow_north - south(flow_north))
        vectors.append(p)
        if i < 4:
            vec_ref[i] = trim(p)
    own = [v[:ROWS, :COLS] for v in vectors]
    parts = [split(v) for v in own]
    row = iota((16, COLS), 0)
    hi = jnp.zeros((16, COLS), F32)
    lo = hi
    for at, (i, j) in enumerate(PAIRS):
        p, e = two_prod(own[i], own[j], parts[i], parts[j])
        quarters = [(p[8 * r : 8 * r + 8], e[8 * r : 8 * r + 8]) for r in range(ROWS // 8)]
        total = dd_add(dd_add(quarters[0], quarters[1]), dd_add(quarters[2], quarters[3]))
        for s in (4, 2, 1):
            total = dd_add(total, (roll(total[0], s, 0), roll(total[1], s, 0)))
        hi = jnp.where(row == at, jnp.concatenate([total[0]] * 2, axis=0), hi)
        lo = jnp.where(row == at, jnp.concatenate([total[1]] * 2, axis=0), lo)
    total = (hi, lo)
    for s in (64, 32, 16, 8, 4, 2, 1):
        total = dd_add(total, (roll(total[0], s, 1), roll(total[1], s, 1)))
    lane = iota((16, COLS), 1)
    line = jnp.where(lane == row, total[0], jnp.where(lane == row + 16, total[1], 0.0))
    line = line[:8] + line[8:]
    for s in (4, 2, 1):
        line = line + roll(line, s, 0)
    gram_ref[...] = jnp.concatenate([line] * (gram_ref.shape[0] // 8), axis=0)


def galerkin(gram):
    rows = gram.shape[0]
    parts = [(gram[8 * r : 8 * r + 8], roll(gram[8 * r : 8 * r + 8], COLS - 16, 1)) for r in range(rows // 8)]
    while len(parts) > 1:
        parts = [dd_add(parts[i], parts[i + 1]) for i in range(0, len(parts) - 1, 2)] + parts[len(parts) // 2 * 2 :]
    total = parts[0]
    for s in (4, 2, 1):
        total = dd_add(total, (roll(total[0], s, 0), roll(total[1], s, 0)))
    entry = {}
    for at, (i, j) in enumerate(PAIRS):
        entry[i, j] = entry[j, i] = tuple(jnp.broadcast_to(t[:, at : at + 1], (8, COLS)) for t in total)
    mat = [[entry[i, j + 1] for j in range(4)] for i in range(4)]
    rhs = [entry[i, 0] for i in range(4)]
    size = [jnp.abs(mat[i][i][0]) for i in range(4)]
    for k in range(4):
        fine = mat[k][k][0] > 1e-12 * size[k]
        inv = dd_inv((jnp.where(fine, mat[k][k][0], 1.0), jnp.where(fine, mat[k][k][1], 0.0)))
        inv = tuple(jnp.where(fine, t, 0.0) for t in inv)
        for j in range(k + 1, 4):
            mat[k][j] = dd_mul(mat[k][j], inv)
        rhs[k] = dd_mul(rhs[k], inv)
        for i in range(k + 1, 4):
            less = dd_neg(mat[i][k])
            for j in range(k + 1, 4):
                mat[i][j] = dd_add(mat[i][j], dd_mul(less, mat[k][j]))
            rhs[i] = dd_add(rhs[i], dd_mul(less, rhs[k]))
    for k in range(2, -1, -1):
        for j in range(k + 1, 4):
            rhs[k] = dd_add(rhs[k], dd_neg(dd_mul(mat[k][j], rhs[j])))
    return [r[0] for r in rhs]


SPANS = ((0, 3), (3, 6), (6, 9), (9, GROUPS))
TALL = ROWS + 8
PADDED = 4 * GROUPS
SPAN_LEVELS = 16
BF16 = jnp.bfloat16


def final_kernel(
    gram_ref, vec_ref, lev_ref, side_ref, h1_ref, h2_ref, mixed, vel, tr,
    adj_h, avel_h, sol_ref,
    adj, avel, sol_s, edge1, edge2, edge3, start_s, lhs, diff, weights, out_sem,
):
    lat_par = lax.rem(lax.axis_index("lat"), 2)
    shape = (COLS, COLS)
    source, target = iota(shape, 0), iota(shape, 1)
    shift = jnp.where(source == target + 1, 1.0, jnp.where(source == target - 1, -1.0, 0.0)).astype(BF16)
    ends = jnp.where(
        (target == COLS - 1) & (source % 2 == 0), 1.0, jnp.where((target == 0) & (source % 2 == 1), -1.0, 0.0)
    ).astype(BF16)
    weights[:COLS] = shift
    weights[COLS : 2 * COLS] = shift
    weights[2 * COLS :] = ends

    coefs = galerkin(gram_ref[...])
    for half in range(2):
        at = half * COLS
        total = 0.0
        for i in range(4):
            wide = jnp.concatenate([coefs[i]] * (TALL // 8), axis=0)
            total = total + wide * vec_ref[i, :, at : at + COLS]
        sol_s[:, at : at + COLS] = total
    sol_ref[...] = sol_s[:ROWS, :COLS]

    lane = iota((TALL, COLS), 1)
    pair = iota((8, COLS), 0) // 2
    even = jnp.broadcast_to(lat_par, (8, COLS)) == 0
    masks = [(pair == q) == even for q in range(4)]

    def edge_rows(index, q):
        x = jnp.where(masks[q], h1_ref[index], h2_ref[index])
        return roll(x, 8 - 2 * q, 0) if q else x

    def parts(x):
        hi = x.astype(BF16)
        return hi, (x - hi.astype(F32)).astype(BF16)

    flux1, flux2 = [], []
    for side in range(2):
        def around(ref):
            own, edge = roll(ref[:, :COLS], 2, 1), roll(ref[:, COLS:], 2, 1)
            x = jnp.where(lane < 2, own, edge) if side else jnp.where(lane < 2, edge, own)
            for s in (4, 8, 16, 32, 64):
                x = jnp.where(lane < s, x, roll(x, s, 1))
            return x

        levels, pressure = around(lev_ref), around(sol_s)
        for tile in range(2):
            def column(field):
                index = side * 8 + field * 2 + tile
                return jnp.concatenate(
                    [side_ref[side, field, tile], edge_rows(FIELDS * GROUPS + index // 4, index % 4)], axis=0
                )

            wet = jnp.where((lane // 4 + tile * SLOTS).astype(F32) < levels, 1.0, 0.0)
            move = COURANT * wet
            u, v = column(2), column(3)
            for n in range(2):
                x = column(n) + GAINS[n] * wet * pressure
                flux = u * x
                flux1.append(flux)
                x = x + move * (roll(flux, COLS - 1, 1) - roll(flux, 1, 1))
                for _ in range(2):
                    flux = v * x
                    x = x + move * (roll(flux, TALL - 1, 0) - roll(flux, 1, 0))
                flux2.append((u * x)[:ROWS])

    def pack(west, east):
        at = iota(east.shape, 1) % 4
        both = jnp.where(at == 2, east, roll(west, 2, 1))
        hi, mid = (t.astype(F32) for t in parts(both))
        return jnp.where(at >= 2, hi, roll(mid, COLS - 2, 1))

    for tile in range(2):
        for n in range(2):
            west, east = tile * 2 + n, 4 + tile * 2 + n
            edge1[tile, n * TALL : (n + 1) * TALL] = pack(flux1[west], flux1[east])
            edge2[tile, n * ROWS : (n + 1) * ROWS] = pack(flux2[west], flux2[east])
            edge3[tile, n * ROWS : (n + 1) * ROWS] = pack(side_ref[0, 4 + n, tile], side_ref[1, 4 + n, tile])

    def meridional(x):
        return roll(x, TALL - 1, 0) - roll(x, 1, 0)

    def tall_field(ref, n, field, g, q):
        return jnp.concatenate([ref[n, 4 * g + q], edge_rows(field * GROUPS + g, q)], axis=0)

    def wet_of(k, rows):
        return jnp.where(k.astype(F32) < lev_ref[:rows, :COLS], 1.0, 0.0)

    def put(at, rows, x, edge, k):
        here = iota(x.shape, 1) // 4 == lax.rem(k, SLOTS)
        hi, mid = parts(x)
        lhs[pl.ds(at, rows), :COLS] = hi
        lhs[pl.ds(at, rows), COLS : 2 * COLS] = mid
        lhs[pl.ds(at, rows), 2 * COLS :] = jnp.where(here, edge[k // SLOTS], 0.0).astype(BF16)

    writes = []
    for lo, hi in SPANS:
        def zonal_first(g, carry, lo=lo):
            for q in range(4):
                k, j = 4 * g + q, 4 * (g - lo) + q
                wet_sol = wet_of(k, TALL) * sol_s[:, :COLS]
                u = tall_field(vel, 0, 2, g, q)
                xs = [tall_field(mixed, n, n, g, q) + GAINS[n] * wet_sol for n in range(2)]
                for n in range(2):
                    start_s[j, n] = xs[n]
                at = pl.multiple_of(j * 2 * TALL, 16)
                put(at, 2 * TALL, jnp.concatenate([u * x for x in xs], axis=0), edge1, k)
            return carry

        def middle(g, carry, lo=lo):
            for q in range(4):
                k, j = 4 * g + q, 4 * (g - lo) + q
                move = COURANT * wet_of(k, TALL)
                v = tall_field(vel, 1, 3, g, q)
                u = vel[0, k]
                fluxes = []
                for n in range(2):
                    x = start_s[j, n] + move * diff[pl.ds(pl.multiple_of(j * 2 * TALL + n * TALL, 8), TALL)]
                    x = x + move * meridional(v * x)
                    x = (x + move * meridional(v * x))[:ROWS]
                    adj[n, k] = x
                    fluxes.append(u * x)
                at = pl.multiple_of(j * 4 * ROWS, 16)
                put(at, 2 * ROWS, jnp.concatenate(fluxes, axis=0), edge2, k)
                put(at + 2 * ROWS, 2 * ROWS, jnp.concatenate([tr[0, k], tr[1, k]], axis=0), edge3, k)
            return carry

        def zonal_last(g, carry, lo=lo):
            for q in range(4):
                k, j = 4 * g + q, 4 * (g - lo) + q
                move = COURANT * wet_of(k, ROWS)
                east_sum, north_sum = 0.0, 0.0
                for n in range(2):
                    at = j * 4 * ROWS + n * ROWS
                    x = adj[n, k] + move * diff[pl.ds(pl.multiple_of(at, 8), ROWS)]
                    adj[n, k] = x
                    east_sum = east_sum + x * diff[pl.ds(pl.multiple_of(at + 2 * ROWS, 8), ROWS)]
                    north_sum = north_sum + x * meridional(tall_field(tr, n, 4 + n, g, q))[:ROWS]
                avel[0, k] = -move * east_sum
                avel[1, k] = -move * north_sum
            return carry

        levels = 4 * (hi - lo)
        lax.fori_loop(lo, hi, zonal_first, 0)
        rows = levels * 2 * TALL
        diff[:rows] = jnp.dot(lhs[:rows], weights[...], preferred_element_type=F32)
        lax.fori_loop(lo, hi, middle, 0)
        rows = levels * 4 * ROWS
        diff[:rows] = jnp.dot(lhs[:rows], weights[...], preferred_element_type=F32)
        lax.fori_loop(lo, hi, zonal_last, 0)
        at, count = 4 * lo, min(4 * hi, LEVELS) - 4 * lo
        for i, (src, dst) in enumerate(((adj, adj_h), (avel, avel_h))):
            copy = pltpu.make_async_copy(
                src.at[:, pl.ds(at, count)], dst.at[:, pl.ds(at, count)], out_sem.at[len(writes) // 2, i]
            )
            copy.start()
            writes.append(copy)
    for copy in writes:
        copy.wait()


def swaps(size, first, periodic):
    out = []
    for i in range(first, size, 2):
        if i + 1 < size or periodic:
            out += [(i, (i + 1) % size), ((i + 1) % size, i)]
    return out


def shape(*dims):
    return jax.ShapeDtypeStruct(dims, F32)


def call(kernel, name, ins, outs, scratch, args):
    here, there = pl.BlockSpec(memory_space=VMEM), pl.BlockSpec(memory_space=pl.ANY)
    args = [a if far else pltpu.with_memory_space_constraint(a, VMEM) for a, far in zip(args, ins)]
    return pl.pallas_call(
        kernel,
        name=name,
        out_shape=tuple(o for o, _ in outs),
        in_specs=[there if far else here for far in ins],
        out_specs=tuple(there if far else here for _, far in outs),
        scratch_shapes=scratch,
        compiler_params=pltpu.CompilerParams(vmem_limit_bytes=VMEM_LIMIT),
    )(*args)


def kept(*dims):
    return VMEM(dims, F32), False


def per_device(lam_tracer, tracer, velocity, diffusivity, lam_surface, sea_depth, levels):
    lon, lat = lax.axis_size("lon"), lax.axis_size("lat")
    tile = (ROWS, COLS)
    deep, padded = (2, LEVELS) + tile, (2, PADDED) + tile
    mixed, vel, tr, base, lon1, lon2, slots, g1, g2 = call(
        solve_kernel, "column_solve", (True,) * 7,
        (kept(*padded), kept(*padded), kept(*padded), kept(3, *tile), kept(FIELDS + 1, *tile), kept(FIELDS + 1, *tile),
         kept(FIELDS, 2, *tile), kept(FIELDS * GROUPS, 8, COLS), kept(FIELDS * GROUPS, 8, COLS)),
        [VMEM(deep, F32), VMEM((LEVELS,) + tile, F32), VMEM(tile, F32), VMEM(tile, jnp.int32),
         VMEM((LEVELS,) + tile, F32), VMEM(deep, F32),
         pltpu.SemaphoreType.DMA((HALF // 5, 4)), pltpu.SemaphoreType.DMA((5,))],
        (lam_tracer, velocity, tracer, diffusivity, lam_surface, sea_depth, levels),
    )
    o1 = lax.ppermute(lon1, "lon", swaps(lon, 0, True))
    o2 = lax.ppermute(lon2, "lon", swaps(lon, 1, True))
    ext, lat1, s2, h2, side = call(
        lon_kernel, "after_lon", (False,) * 6,
        (kept(3, ROWS, 2 * COLS), kept(EDGES + 6, 8, COLS), kept(6, 8, COLS), kept(EDGES, 8, COLS),
         kept(2, FIELDS, 2, *tile)),
        [],
        (base, o1, o2, slots, g1, g2),
    )
    odd_lat = swaps(lat, 1, False)
    lat1 = lax.ppermute(lat1, "lat", swaps(lat, 0, False))
    s2 = lax.ppermute(s2, "lat", odd_lat)
    s2, h2 = lax.optimization_barrier((s2, h2))
    h2 = lax.ppermute(h2, "lat", odd_lat)
    vec, lev, gram = call(
        krylov_kernel, "krylov", (False,) * 3,
        (kept(4, TALL, 2 * COLS), kept(TALL, 2 * COLS), kept(lon * lat, COLS)),
        [],
        (ext, lat1, s2),
    )
    gram = lax.all_to_all(gram, ("lon", "lat"), 0, 0, tiled=True)
    return call(
        final_kernel, "sweeps", (False,) * 9,
        ((shape(*deep), True), (shape(*deep), True), (shape(*tile), False)),
        [VMEM(padded, F32), VMEM(padded, F32), VMEM((TALL, 2 * COLS), F32), VMEM((2, 2 * TALL, COLS), F32),
         VMEM((2, 2 * ROWS, COLS), F32), VMEM((2, 2 * ROWS, COLS), F32), VMEM((SPAN_LEVELS, 2, TALL, COLS), F32),
         VMEM((SPAN_LEVELS * 4 * ROWS, 3 * COLS), BF16), VMEM((SPAN_LEVELS * 4 * ROWS, COLS), F32),
         VMEM((3 * COLS, COLS), BF16), pltpu.SemaphoreType.DMA((len(SPANS), 2))],
        (gram, vec, lev, side, lat1, h2, mixed, vel, tr),
    )


def solution(mesh):
    deep, flat = P(None, None, "lat", "lon"), P("lat", "lon")
    return jax.shard_map(
        per_device,
        mesh=mesh,
        in_specs=(deep, deep, deep, P(None, "lat", "lon"), flat, flat, flat),
        out_specs=(deep, deep, flat),
        check_vma=False,
    )
```

```python
import math

import jax
import jax.numpy as jnp
from jax import lax
from jax.experimental import pallas as pl
from jax.experimental.pallas import tpu as pltpu
from jax.sharding import PartitionSpec as P

LEVELS = 50
SURFACE_DAMPING = 0.05
COURANT = 0.25
GAINS = (0.7, -0.5)
ROWS = 32
COLS = 128
HALF = LEVELS // 2
SLOTS = 32
FIELDS = 6
GROUPS = -(-LEVELS // 4)
VMEM_LIMIT = 12 * 1024 * 1024
F32 = jnp.float32
VMEM = pltpu.VMEM

PAIRS = tuple((i, j) for i in range(4) for j in range(i, 5))


def iota(shape, dim):
    return lax.broadcasted_iota(jnp.int32, shape, dim)


def pick(parity, even, odd):
    return jnp.where(jnp.broadcast_to(parity, even.shape) == 0, even, odd)


def roll(x, shift, axis):
    return pltpu.roll(x, shift, axis)


def two_sum(a, b):
    s = a + b
    bb = s - a
    return s, (a - (s - bb)) + (b - bb)


def quick_sum(a, b):
    s = a + b
    return s, b - (s - a)


def split(a):
    t = 4097.0 * a
    hi = t - (t - a)
    return hi, a - hi


def two_prod(a, b, sa=None, sb=None):
    ah, al = sa or split(a)
    bh, bl = sb or split(b)
    p = a * b
    return p, ((ah * bh - p) + ah * bl + al * bh) + al * bl


def dd_add(a, b):
    s, e = two_sum(a[0], b[0])
    return quick_sum(s, e + (a[1] + b[1]))


def dd_mul(a, b):
    p, e = two_prod(a[0], b[0])
    return quick_sum(p, e + (a[0] * b[1] + a[1] * b[0]))


def dd_neg(a):
    return -a[0], -a[1]


def dd_inv(a):
    r = 1.0 / a[0]
    p, e = two_prod(a[0], r)
    rest = ((1.0 - p) - e) - a[1] * r
    return quick_sum(r, r * rest)


def solve_kernel(
    lam_h, vel_h, tr_h, dif_h, lams_h, depth_h, lev_h,
    mixed_ref, vel, tr, base_ref, lon1_ref, lon2_ref, slots_ref, g1_ref, g2_ref,
    lam, dif, lams_s, lev_s, w_s, z_s, col_sem, rest_sem,
):
    lon_par = lax.rem(lax.axis_index("lon"), 2)
    lat_par = lax.rem(lax.axis_index("lat"), 2)
    step = 5
    flat = [
        pltpu.make_async_copy(lev_h, lev_s, rest_sem.at[0]),
        pltpu.make_async_copy(lams_h, lams_s, rest_sem.at[1]),
        pltpu.make_async_copy(depth_h, base_ref.at[1], rest_sem.at[2]),
    ]
    copies = []
    for i in range(HALF // step):
        top, low = i * step, LEVELS - (i + 1) * step
        part = []
        for n, at in enumerate((top, low)):
            part.append(pltpu.make_async_copy(dif_h.at[pl.ds(at, step)], dif.at[pl.ds(at, step)], col_sem.at[i, 2 * n]))
            part.append(pltpu.make_async_copy(lam_h.at[:, pl.ds(at, step)], lam.at[:, pl.ds(at, step)], col_sem.at[i, 2 * n + 1]))
        copies.append(part)
    rest = [
        pltpu.make_async_copy(vel_h, vel, rest_sem.at[3]),
        pltpu.make_async_copy(tr_h, tr, rest_sem.at[4]),
    ]
    for c in flat + sum(copies, []) + rest:
        c.start()
    for c in flat:
        c.wait()

    lev = lev_s[...]
    zero = jnp.zeros((ROWS, COLS), F32)

    def coef(k):
        return jnp.where(lev > k + 1, dif[k], 0.0)

    def right(n, k):
        return jnp.where(lev > k, lam[n, k], 0.0)

    e = jnp.ones((ROWS, COLS), F32)
    y = [zero, zero]
    w = zero
    eb = e
    yb = [zero, zero]
    wb = zero
    waited = 0
    for k in range(HALF):
        need = min((k + 1) // step, HALF // step - 1)
        while waited <= need:
            for c in copies[waited]:
                c.wait()
            waited += 1
        c_k = coef(k)
        y = [right(n, k) + w * y[n] for n in range(2)]
        inv = 1.0 / (e + c_k)
        w = c_k * inv
        w_s[k] = w
        for n in range(2):
            z_s[n, k] = y[n] * inv
        e = 1.0 + e * w
        if k < HALF - 1:
            m = LEVELS - 1 - k
            c_m = coef(m - 1)
            yb = [right(n, m) + wb * yb[n] for n in range(2)]
            invb = 1.0 / (eb + c_m)
            wb = c_m * invb
            w_s[m] = wb
            for n in range(2):
                z_s[n, m] = yb[n] * invb
            eb = 1.0 + eb * wb
    for c in rest:
        c.wait()

    lane = iota((ROWS, COLS), 1)
    slot = lane // 4
    begun = set()

    def gather(k, fields):
        tile, s = divmod(k, SLOTS)
        here = slot == s
        for i, x in enumerate(fields):
            before = slots_ref[i, tile] if (i, tile) in begun else zero
            begun.add((i, tile))
            slots_ref[i, tile] = jnp.where(here, roll(x, 4 * s + 2, 1), before)

    def level_done(k, solved):
        for n in range(2):
            mixed_ref[n, k] = solved[n]
        gather(k, (solved[0], solved[1], vel[0, k], vel[1, k], tr[0, k], tr[1, k]))

    inv = 1.0 / (e + eb - 1.0)
    below = [(right(n, HALF) + wb * yb[n] + w * y[n]) * inv for n in range(2)]
    total = list(below)
    level_done(HALF, below)
    above = list(below)
    for i in range(1, HALF + 1):
        k = HALF - i
        for n in range(2):
            above[n] = z_s[n, k] + w_s[k] * above[n]
            total[n] = total[n] + above[n]
        level_done(k, above)
        m = HALF + i
        if m < LEVELS:
            for n in range(2):
                below[n] = z_s[n, m] + w_s[m] * below[n]
                total[n] = total[n] + below[n]
            level_done(m, below)
    f = jnp.where(lev > 0, lams_s[...] + (GAINS[0] * total[0] + GAINS[1] * total[1]) / math.sqrt(LEVELS), 0.0)
    levels = lev.astype(F32)
    base_ref[0] = f
    base_ref[2] = levels
    small = jnp.where(lane < 16, roll(f, 8, 1), jnp.where(lane < 32, roll(base_ref[1], 24, 1), roll(levels, 40, 1)))
    lon1_ref[FIELDS] = small
    lon2_ref[FIELDS] = small
    near = lane % 4 < 2
    for i in range(FIELDS):
        a, b = slots_ref[i, 0], slots_ref[i, 1]
        east_edge = jnp.where(near, a, roll(b, 2, 1))
        west_edge = jnp.where(near, roll(a, COLS - 2, 1), b)
        lon1_ref[i] = pick(lon_par, east_edge, west_edge)
        lon2_ref[i] = pick(lon_par, west_edge, east_edge)

    pair = iota((8, COLS), 0) // 2
    for i, src in enumerate((mixed_ref, mixed_ref, vel, vel, tr, tr)):
        for g in range(GROUPS):
            first = jnp.zeros((8, COLS), F32)
            last = first
            for q in range(min(4, LEVELS - 4 * g)):
                top, end = src[i % 2, 4 * g + q, :8], src[i % 2, 4 * g + q, ROWS - 8 :]
                first = jnp.where(pair == q, roll(top, 2 * q, 0) if q else top, first)
                last = jnp.where(pair == (q + 3) % 4, roll(end, 2 * q, 0) if q else end, last)
            g1_ref[i * GROUPS + g] = pick(lat_par, last, first)
            g2_ref[i * GROUPS + g] = pick(lat_par, first, last)


CORNERS = 4
EDGES = FIELDS * GROUPS + CORNERS


def corner_of(index):
    return index // 8, index // 2 % 4, index % 2


def flat_kernel(base_ref, o1_ref, o2_ref, ext_ref, s1_ref, s2_ref):
    lon_par = lax.rem(lax.axis_index("lon"), 2)
    lat_par = lax.rem(lax.axis_index("lat"), 2)
    lane = iota((ROWS, COLS), 1)
    o1, o2 = o1_ref[FIELDS], o2_ref[FIELDS]
    from_east, from_west = pick(lon_par, o1, o2), pick(lon_par, o2, o1)
    for i in range(3):
        own = base_ref[i]
        edge = jnp.where(lane < 16 * i + 8, from_west, from_east)
        edge = roll(edge, COLS - 8 - 16 * i, 1)
        edge = jnp.where((lane < 8) | (lane >= COLS - 8), edge, 0.0)
        ext_ref[i, :, :COLS] = own
        ext_ref[i, :, COLS:] = edge
        for half, here in enumerate((own, edge)):
            first, last = here[:8], here[ROWS - 8 :]
            s1_ref[2 * i + half] = pick(lat_par, last, first)
            s2_ref[2 * i + half] = pick(lat_par, first, last)


def deep_kernel(s1_ref, o1_ref, o2_ref, slots_ref, g1_ref, g2_ref, lat1_ref, h2_ref, side_ref):
    lon_par = lax.rem(lax.axis_index("lon"), 2)
    lat_par = lax.rem(lax.axis_index("lat"), 2)
    near = iota((ROWS, COLS), 1) % 4 < 2
    for i in range(FIELDS):
        b1, b2 = o1_ref[i], o2_ref[i]
        east, west = pick(lon_par, b1, b2), pick(lon_par, b2, b1)
        own_a, own_b = slots_ref[i, 0], slots_ref[i, 1]
        side_ref[0, i, 0] = jnp.where(near, west, own_a)
        side_ref[0, i, 1] = jnp.where(near, roll(west, COLS - 2, 1), own_b)
        side_ref[1, i, 0] = jnp.where(near, own_a, roll(east, 2, 1))
        side_ref[1, i, 1] = jnp.where(near, own_b, east)
    lat1_ref[: FIELDS * GROUPS] = g1_ref[...]
    lat1_ref[EDGES:] = s1_ref[...]
    h2_ref[: FIELDS * GROUPS] = g2_ref[...]
    pair = iota((8, COLS), 0) // 2
    for c in range(CORNERS):
        first = jnp.zeros((8, COLS), F32)
        last = first
        for q in range(4):
            side, field, tile = corner_of(4 * c + q)
            x = side_ref[side, field, tile]
            first = jnp.where(pair == q, roll(x[:8], 2 * q, 0) if q else x[:8], first)
            last = jnp.where(pair == (q + 3) % 4, roll(x[ROWS - 8 :], 2 * q, 0) if q else x[ROWS - 8 :], last)
        lat1_ref[FIELDS * GROUPS + c] = pick(lat_par, last, first)
        h2_ref[FIELDS * GROUPS + c] = pick(lat_par, first, last)


def krylov_kernel(ext_ref, lat1_ref, s2_ref, vec_ref, lev_ref, gram_ref):
    lat_par = lax.rem(lax.axis_index("lat"), 2)
    rows, cols = ROWS + 16, 2 * COLS
    whole = []
    for i in range(3):
        s1 = jnp.concatenate([lat1_ref[EDGES + 2 * i], lat1_ref[EDGES + 2 * i + 1]], axis=1)
        s2 = jnp.concatenate([s2_ref[2 * i], s2_ref[2 * i + 1]], axis=1)
        whole.append(jnp.concatenate([ext_ref[i], pick(lat_par, s1, s2), pick(lat_par, s2, s1)], axis=0))
    f, depth, lev = whole

    def east(x):
        return roll(x, cols - 1, 1)

    def west(x):
        return roll(x, 1, 1)

    def north(x):
        return roll(x, rows - 1, 0)

    def south(x):
        return roll(x, 1, 0)

    sea = jnp.where(lev > 0.0, 1.0, 0.0)
    face_east = 0.5 * (depth + east(depth)) * sea * east(sea)
    face_north = 0.5 * (depth + north(depth)) * sea * north(sea)
    base = (1.0 - sea) + SURFACE_DAMPING * sea
    sub = iota((8, cols), 0)

    def trim(x):
        return jnp.concatenate([x[:ROWS], jnp.where(sub < 4, x[ROWS : ROWS + 8], x[ROWS + 8 :])], axis=0)

    lev_ref[...] = trim(lev)
    vectors = [f]
    vec_ref[0] = trim(f)
    for i in range(1, 5):
        p = vectors[-1]
        flow_east = face_east * (p - east(p))
        flow_north = face_north * (p - north(p))
        p = base * p + (flow_east - west(flow_east)) + (flow_north - south(flow_north))
        vectors.append(p)
        if i < 4:
            vec_ref[i] = trim(p)
    own = [v[:ROWS, :COLS] for v in vectors]
    parts = [split(v) for v in own]
    row = iota((16, COLS), 0)
    hi = jnp.zeros((16, COLS), F32)
    lo = hi
    for at, (i, j) in enumerate(PAIRS):
        p, e = two_prod(own[i], own[j], parts[i], parts[j])
        quarters = [(p[8 * r : 8 * r + 8], e[8 * r : 8 * r + 8]) for r in range(ROWS // 8)]
        total = dd_add(dd_add(quarters[0], quarters[1]), dd_add(quarters[2], quarters[3]))
        for s in (4, 2, 1):
            total = dd_add(total, (roll(total[0], s, 0), roll(total[1], s, 0)))
        hi = jnp.where(row == at, jnp.concatenate([total[0]] * 2, axis=0), hi)
        lo = jnp.where(row == at, jnp.concatenate([total[1]] * 2, axis=0), lo)
    total = (hi, lo)
    for s in (64, 32, 16, 8, 4, 2, 1):
        total = dd_add(total, (roll(total[0], s, 1), roll(total[1], s, 1)))
    lane = iota((16, COLS), 1)
    line = jnp.where(lane == row, total[0], jnp.where(lane == row + 16, total[1], 0.0))
    line = line[:8] + line[8:]
    for s in (4, 2, 1):
        line = line + roll(line, s, 0)
    gram_ref[...] = jnp.concatenate([line] * (gram_ref.shape[0] // 8), axis=0)


def galerkin(gram):
    rows = gram.shape[0]
    parts = [(gram[8 * r : 8 * r + 8], roll(gram[8 * r : 8 * r + 8], COLS - 16, 1)) for r in range(rows // 8)]
    while len(parts) > 1:
        parts = [dd_add(parts[i], parts[i + 1]) for i in range(0, len(parts) - 1, 2)] + parts[len(parts) // 2 * 2 :]
    total = parts[0]
    for s in (4, 2, 1):
        total = dd_add(total, (roll(total[0], s, 0), roll(total[1], s, 0)))
    entry = {}
    for at, (i, j) in enumerate(PAIRS):
        entry[i, j] = entry[j, i] = tuple(jnp.broadcast_to(t[:, at : at + 1], (8, COLS)) for t in total)
    mat = [[entry[i, j + 1] for j in range(4)] for i in range(4)]
    rhs = [entry[i, 0] for i in range(4)]
    size = [jnp.abs(mat[i][i][0]) for i in range(4)]
    for k in range(4):
        fine = mat[k][k][0] > 1e-12 * size[k]
        inv = dd_inv((jnp.where(fine, mat[k][k][0], 1.0), jnp.where(fine, mat[k][k][1], 0.0)))
        inv = tuple(jnp.where(fine, t, 0.0) for t in inv)
        for j in range(k + 1, 4):
            mat[k][j] = dd_mul(mat[k][j], inv)
        rhs[k] = dd_mul(rhs[k], inv)
        for i in range(k + 1, 4):
            less = dd_neg(mat[i][k])
            for j in range(k + 1, 4):
                mat[i][j] = dd_add(mat[i][j], dd_mul(less, mat[k][j]))
            rhs[i] = dd_add(rhs[i], dd_mul(less, rhs[k]))
    for k in range(2, -1, -1):
        for j in range(k + 1, 4):
            rhs[k] = dd_add(rhs[k], dd_neg(dd_mul(mat[k][j], rhs[j])))
    return [r[0] for r in rhs]


SPANS = ((0, 12), (12, 25), (25, 38), (38, LEVELS))
TALL = ROWS + 8
SPAN_LEVELS = 13
BF16 = jnp.bfloat16


def final_kernel(
    gram_ref, vec_ref, lev_ref, side_ref, h1_ref, h2_ref, mixed, vel, tr,
    adj_h, avel_h, sol_ref,
    adj, avel, sol_s, edge1, edge2, edge3, start_s, lhs, diff, weights, out_sem,
):
    lat_par = lax.rem(lax.axis_index("lat"), 2)
    shape = (COLS, COLS)
    source, target = iota(shape, 0), iota(shape, 1)
    shift = jnp.where(source == target + 1, 1.0, jnp.where(source == target - 1, -1.0, 0.0)).astype(BF16)
    ends = jnp.where(
        (target == COLS - 1) & (source % 2 == 0), 1.0, jnp.where((target == 0) & (source % 2 == 1), -1.0, 0.0)
    ).astype(BF16)
    weights[:COLS] = shift
    weights[COLS : 2 * COLS] = shift
    weights[2 * COLS :] = ends

    coefs = galerkin(gram_ref[...])
    for half in range(2):
        at = half * COLS
        total = 0.0
        for i in range(4):
            wide = jnp.concatenate([coefs[i]] * (TALL // 8), axis=0)
            total = total + wide * vec_ref[i, :, at : at + COLS]
        sol_s[:, at : at + COLS] = total
    sol_ref[...] = sol_s[:ROWS, :COLS]

    lane = iota((TALL, COLS), 1)
    pair = iota((8, COLS), 0) // 2
    even = jnp.broadcast_to(lat_par, (8, COLS)) == 0
    masks = [(pair == q) == even for q in range(4)]

    def edge_rows(index, q):
        x = jnp.where(masks[q], h1_ref[index], h2_ref[index])
        return roll(x, 8 - 2 * q, 0) if q else x

    def parts(x):
        hi = x.astype(BF16)
        return hi, (x - hi.astype(F32)).astype(BF16)

    flux1, flux2 = [], []
    for side in range(2):
        def around(ref):
            own, edge = roll(ref[:, :COLS], 2, 1), roll(ref[:, COLS:], 2, 1)
            x = jnp.where(lane < 2, own, edge) if side else jnp.where(lane < 2, edge, own)
            for s in (4, 8, 16, 32, 64):
                x = jnp.where(lane < s, x, roll(x, s, 1))
            return x

        levels, pressure = around(lev_ref), around(sol_s)
        for tile in range(2):
            def column(field):
                index = side * 8 + field * 2 + tile
                return jnp.concatenate(
                    [side_ref[side, field, tile], edge_rows(FIELDS * GROUPS + index // 4, index % 4)], axis=0
                )

            wet = jnp.where((lane // 4 + tile * SLOTS).astype(F32) < levels, 1.0, 0.0)
            move = COURANT * wet
            u, v = column(2), column(3)
            for n in range(2):
                x = column(n) + GAINS[n] * wet * pressure
                flux = u * x
                flux1.append(flux)
                x = x + move * (roll(flux, COLS - 1, 1) - roll(flux, 1, 1))
                for _ in range(2):
                    flux = v * x
                    x = x + move * (roll(flux, TALL - 1, 0) - roll(flux, 1, 0))
                flux2.append((u * x)[:ROWS])

    def pack(west, east):
        at = iota(east.shape, 1) % 4
        both = jnp.where(at == 2, east, roll(west, 2, 1))
        hi, mid = (t.astype(F32) for t in parts(both))
        return jnp.where(at >= 2, hi, roll(mid, COLS - 2, 1))

    for tile in range(2):
        for n in range(2):
            west, east = tile * 2 + n, 4 + tile * 2 + n
            edge1[tile, n * TALL : (n + 1) * TALL] = pack(flux1[west], flux1[east])
            edge2[tile, n * ROWS : (n + 1) * ROWS] = pack(flux2[west], flux2[east])
            edge3[tile, n * ROWS : (n + 1) * ROWS] = pack(side_ref[0, 4 + n, tile], side_ref[1, 4 + n, tile])

    def meridional(x):
        return roll(x, TALL - 1, 0) - roll(x, 1, 0)

    def tall_field(ref, n, field, k):
        return jnp.concatenate([ref[n, k], edge_rows(field * GROUPS + k // 4, k % 4)], axis=0)

    def wet_of(k, rows):
        return jnp.where(float(k) < lev_ref[:rows, :COLS], 1.0, 0.0)

    def put(at, rows, x, edge, k):
        here = iota(x.shape, 1) // 4 == k % SLOTS
        hi, mid = parts(x)
        lhs[pl.ds(at, rows), :COLS] = hi
        lhs[pl.ds(at, rows), COLS : 2 * COLS] = mid
        lhs[pl.ds(at, rows), 2 * COLS :] = jnp.where(here, edge[k // SLOTS], 0.0).astype(BF16)

    writes = []
    for first, last in SPANS:
        def zonal_first(k, j):
            wet_sol = wet_of(k, TALL) * sol_s[:, :COLS]
            u = tall_field(vel, 0, 2, k)
            xs = [tall_field(mixed, n, n, k) + GAINS[n] * wet_sol for n in range(2)]
            for n in range(2):
                start_s[j, n] = xs[n]
            at = j * 2 * TALL
            put(at, 2 * TALL, jnp.concatenate([u * x for x in xs], axis=0), edge1, k)

        def middle(k, j):
            move = COURANT * wet_of(k, TALL)
            v = tall_field(vel, 1, 3, k)
            u = vel[0, k]
            fluxes = []
            for n in range(2):
                x = start_s[j, n] + move * diff[pl.ds((2 * j + n) * TALL, TALL)]
                x = x + move * meridional(v * x)
                x = (x + move * meridional(v * x))[:ROWS]
                adj[n, k] = x
                fluxes.append(u * x)
            at = j * 4 * ROWS
            put(at, 2 * ROWS, jnp.concatenate(fluxes, axis=0), edge2, k)
            put(at + 2 * ROWS, 2 * ROWS, jnp.concatenate([tr[0, k], tr[1, k]], axis=0), edge3, k)

        def zonal_last(k, j):
            move = COURANT * wet_of(k, ROWS)
            east_sum, north_sum = 0.0, 0.0
            for n in range(2):
                at = j * 4 * ROWS + n * ROWS
                x = adj[n, k] + move * diff[pl.ds(at, ROWS)]
                adj[n, k] = x
                east_sum = east_sum + x * diff[pl.ds(at + 2 * ROWS, ROWS)]
                north_sum = north_sum + x * meridional(tall_field(tr, n, 4 + n, k))[:ROWS]
            avel[0, k] = -move * east_sum
            avel[1, k] = -move * north_sum

        levels = last - first
        for k in range(first, last):
            zonal_first(k, k - first)
        rows = levels * 2 * TALL
        diff[:rows] = jnp.dot(lhs[:rows], weights[...], preferred_element_type=F32)
        for k in range(first, last):
            middle(k, k - first)
        rows = levels * 4 * ROWS
        diff[:rows] = jnp.dot(lhs[:rows], weights[...], preferred_element_type=F32)
        for k in range(first, last):
            zonal_last(k, k - first)
        for i, (src, dst) in enumerate(((adj, adj_h), (avel, avel_h))):
            copy = pltpu.make_async_copy(
                src.at[:, pl.ds(first, levels)], dst.at[:, pl.ds(first, levels)], out_sem.at[len(writes) // 2, i]
            )
            copy.start()
            writes.append(copy)
    for copy in writes:
        copy.wait()


def swaps(size, first, periodic):
    out = []
    for i in range(first, size, 2):
        if i + 1 < size or periodic:
            out += [(i, (i + 1) % size), ((i + 1) % size, i)]
    return out


def shape(*dims):
    return jax.ShapeDtypeStruct(dims, F32)


def call(kernel, name, ins, outs, scratch, args):
    here, there = pl.BlockSpec(memory_space=VMEM), pl.BlockSpec(memory_space=pltpu.HBM)
    args = [pltpu.with_memory_space_constraint(a, pltpu.HBM if far else VMEM) for a, far in zip(args, ins)]
    return pl.pallas_call(
        kernel,
        name=name,
        out_shape=tuple(o for o, _ in outs),
        in_specs=[there if far else here for far in ins],
        out_specs=tuple(there if far else here for _, far in outs),
        scratch_shapes=scratch,
        compiler_params=pltpu.CompilerParams(vmem_limit_bytes=VMEM_LIMIT),
    )(*args)


def kept(*dims):
    return VMEM(dims, F32), False


def per_device(lam_tracer, tracer, velocity, diffusivity, lam_surface, sea_depth, levels):
    lon, lat = lax.axis_size("lon"), lax.axis_size("lat")
    tile = (ROWS, COLS)
    deep = (2, LEVELS) + tile
    mixed, vel, tr, base, lon1, lon2, slots, g1, g2 = call(
        solve_kernel, "column_solve", (True,) * 7,
        (kept(*deep), kept(*deep), kept(*deep), kept(3, *tile), kept(FIELDS + 1, *tile), kept(FIELDS + 1, *tile),
         kept(FIELDS, 2, *tile), kept(FIELDS * GROUPS, 8, COLS), kept(FIELDS * GROUPS, 8, COLS)),
        [VMEM(deep, F32), VMEM((LEVELS,) + tile, F32), VMEM(tile, F32), VMEM(tile, jnp.int32),
         VMEM((LEVELS,) + tile, F32), VMEM(deep, F32),
         pltpu.SemaphoreType.DMA((HALF // 5, 4)), pltpu.SemaphoreType.DMA((5,))],
        (lam_tracer, velocity, tracer, diffusivity, lam_surface, sea_depth, levels),
    )
    o1 = lax.ppermute(lon1, "lon", swaps(lon, 0, True))
    o2 = lax.ppermute(lon2, "lon", swaps(lon, 1, True))
    ext, s1, s2 = call(
        flat_kernel, "flat_edges", (False,) * 3,
        (kept(3, ROWS, 2 * COLS), kept(6, 8, COLS), kept(6, 8, COLS)),
        [],
        (base, o1, o2),
    )
    lat1, h2, side = call(
        deep_kernel, "deep_edges", (False,) * 6,
        (kept(EDGES + 6, 8, COLS), kept(EDGES, 8, COLS), kept(2, FIELDS, 2, *tile)),
        [],
        (s1, o1, o2, slots, g1, g2),
    )
    odd_lat = swaps(lat, 1, False)
    s2 = lax.ppermute(s2, "lat", odd_lat)
    lat1 = lax.ppermute(lat1, "lat", swaps(lat, 0, False))
    h2 = lax.ppermute(h2, "lat", odd_lat)
    vec, lev, gram = call(
        krylov_kernel, "krylov", (False,) * 3,
        (kept(4, TALL, 2 * COLS), kept(TALL, 2 * COLS), kept(lon * lat, COLS)),
        [],
        (ext, lat1, s2),
    )
    gram = lax.all_to_all(gram, ("lon", "lat"), 0, 0, tiled=True)
    return call(
        final_kernel, "sweeps", (False,) * 9,
        ((shape(*deep), True), (shape(*deep), True), (shape(*tile), False)),
        [VMEM(deep, F32), VMEM(deep, F32), VMEM((TALL, 2 * COLS), F32), VMEM((2, 2 * TALL, COLS), F32),
         VMEM((2, 2 * ROWS, COLS), F32), VMEM((2, 2 * ROWS, COLS), F32), VMEM((SPAN_LEVELS, 2, TALL, COLS), F32),
         VMEM((SPAN_LEVELS * 4 * ROWS, 3 * COLS), BF16), VMEM((SPAN_LEVELS * 4 * ROWS, COLS), F32),
         VMEM((3 * COLS, COLS), BF16), pltpu.SemaphoreType.DMA((len(SPANS), 2))],
        (gram, vec, lev, side, lat1, h2, mixed, vel, tr),
    )


def solution(mesh):
    deep, flat = P(None, None, "lat", "lon"), P("lat", "lon")
    return jax.shard_map(
        per_device,
        mesh=mesh,
        in_specs=(deep, deep, deep, P(None, "lat", "lon"), flat, flat, flat),
        out_specs=(deep, deep, flat),
        check_vma=False,
    )
```

```python
import math

import jax
import jax.numpy as jnp
from jax import lax
from jax.experimental import pallas as pl
from jax.experimental.pallas import tpu as pltpu
from jax.sharding import PartitionSpec as P

LEVELS = 50
SURFACE_DAMPING = 0.05
COURANT = 0.25
GAINS = (0.7, -0.5)
ROWS = 32
COLS = 128
HALF = LEVELS // 2
SLOTS = 32
FIELDS = 6
GROUPS = -(-LEVELS // 4)
VMEM_LIMIT = 16 * 1024 * 1024
F32 = jnp.float32
VMEM = pltpu.VMEM

PAIRS = tuple((i, j) for i in range(4) for j in range(i, 5))


def iota(shape, dim):
    return lax.broadcasted_iota(jnp.int32, shape, dim)


def pick(parity, even, odd):
    return jnp.where(jnp.broadcast_to(parity, even.shape) == 0, even, odd)


def roll(x, shift, axis):
    return pltpu.roll(x, shift, axis)


def two_sum(a, b):
    s = a + b
    bb = s - a
    return s, (a - (s - bb)) + (b - bb)


def quick_sum(a, b):
    s = a + b
    return s, b - (s - a)


def split(a):
    t = 4097.0 * a
    hi = t - (t - a)
    return hi, a - hi


def two_prod(a, b, sa=None, sb=None):
    ah, al = sa or split(a)
    bh, bl = sb or split(b)
    p = a * b
    return p, ((ah * bh - p) + ah * bl + al * bh) + al * bl


def dd_add(a, b):
    s, e = two_sum(a[0], b[0])
    return quick_sum(s, e + (a[1] + b[1]))


def dd_mul(a, b):
    p, e = two_prod(a[0], b[0])
    return quick_sum(p, e + (a[0] * b[1] + a[1] * b[0]))


def dd_neg(a):
    return -a[0], -a[1]


def dd_inv(a):
    r = 1.0 / a[0]
    p, e = two_prod(a[0], r)
    rest = ((1.0 - p) - e) - a[1] * r
    return quick_sum(r, r * rest)


def solve_kernel(
    lam_h, vel_h, tr_h, dif_h, lams_h, depth_h, lev_h,
    mixed_ref, base_ref, lon1_ref, lon2_ref, slots_ref, g1_ref, g2_ref,
    lam, vel, tr, dif, lams_s, lev_s, w_s, z_s, col_sem, rest_sem,
):
    lon_par = lax.rem(lax.axis_index("lon"), 2)
    lat_par = lax.rem(lax.axis_index("lat"), 2)
    step = 5
    flat = [
        pltpu.make_async_copy(lev_h, lev_s, rest_sem.at[0]),
        pltpu.make_async_copy(lams_h, lams_s, rest_sem.at[1]),
        pltpu.make_async_copy(depth_h, base_ref.at[1], rest_sem.at[2]),
    ]
    copies = []
    for i in range(HALF // step):
        top, low = i * step, LEVELS - (i + 1) * step
        part = []
        for n, at in enumerate((top, low)):
            part.append(pltpu.make_async_copy(dif_h.at[pl.ds(at, step)], dif.at[pl.ds(at, step)], col_sem.at[i, 2 * n]))
            part.append(pltpu.make_async_copy(lam_h.at[:, pl.ds(at, step)], lam.at[:, pl.ds(at, step)], col_sem.at[i, 2 * n + 1]))
        copies.append(part)
    rest = [
        pltpu.make_async_copy(vel_h, vel, rest_sem.at[3]),
        pltpu.make_async_copy(tr_h, tr, rest_sem.at[4]),
    ]
    for c in flat + sum(copies, []) + rest:
        c.start()
    for c in flat:
        c.wait()

    lev = lev_s[...]
    zero = jnp.zeros((ROWS, COLS), F32)

    def coef(k):
        return jnp.where(lev > k + 1, dif[k], 0.0)

    def right(n, k):
        return jnp.where(lev > k, lam[n, k], 0.0)

    e = jnp.ones((ROWS, COLS), F32)
    y = [zero, zero]
    w = zero
    eb = e
    yb = [zero, zero]
    wb = zero
    waited = 0
    for k in range(HALF):
        need = min((k + 1) // step, HALF // step - 1)
        while waited <= need:
            for c in copies[waited]:
                c.wait()
            waited += 1
        c_k = coef(k)
        y = [right(n, k) + w * y[n] for n in range(2)]
        inv = 1.0 / (e + c_k)
        w = c_k * inv
        w_s[k] = w
        for n in range(2):
            z_s[n, k] = y[n] * inv
        e = 1.0 + e * w
        if k < HALF - 1:
            m = LEVELS - 1 - k
            c_m = coef(m - 1)
            yb = [right(n, m) + wb * yb[n] for n in range(2)]
            invb = 1.0 / (eb + c_m)
            wb = c_m * invb
            w_s[m] = wb
            for n in range(2):
                z_s[n, m] = yb[n] * invb
            eb = 1.0 + eb * wb
    for c in rest:
        c.wait()

    lane = iota((ROWS, COLS), 1)
    slot = lane // 4
    begun = set()

    def gather(k, fields):
        tile, s = divmod(k, SLOTS)
        here = slot == s
        for i, x in enumerate(fields):
            before = slots_ref[i, tile] if (i, tile) in begun else zero
            begun.add((i, tile))
            slots_ref[i, tile] = jnp.where(here, roll(x, 4 * s + 2, 1), before)

    def level_done(k, solved):
        for n in range(2):
            mixed_ref[n, k] = solved[n]
        gather(k, (solved[0], solved[1], vel[0, k], vel[1, k], tr[0, k], tr[1, k]))

    inv = 1.0 / (e + eb - 1.0)
    below = [(right(n, HALF) + wb * yb[n] + w * y[n]) * inv for n in range(2)]
    total = list(below)
    level_done(HALF, below)
    above = list(below)
    for i in range(1, HALF + 1):
        k = HALF - i
        for n in range(2):
            above[n] = z_s[n, k] + w_s[k] * above[n]
            total[n] = total[n] + above[n]
        level_done(k, above)
        m = HALF + i
        if m < LEVELS:
            for n in range(2):
                below[n] = z_s[n, m] + w_s[m] * below[n]
                total[n] = total[n] + below[n]
            level_done(m, below)
    f = jnp.where(lev > 0, lams_s[...] + (GAINS[0] * total[0] + GAINS[1] * total[1]) / math.sqrt(LEVELS), 0.0)
    levels = lev.astype(F32)
    base_ref[0] = f
    base_ref[2] = levels
    small = jnp.where(lane < 16, roll(f, 8, 1), jnp.where(lane < 32, roll(base_ref[1], 24, 1), roll(levels, 40, 1)))
    lon1_ref[FIELDS] = small
    lon2_ref[FIELDS] = small
    near = lane % 4 < 2
    for i in range(FIELDS):
        a, b = slots_ref[i, 0], slots_ref[i, 1]
        east_edge = jnp.where(near, a, roll(b, 2, 1))
        west_edge = jnp.where(near, roll(a, COLS - 2, 1), b)
        lon1_ref[i] = pick(lon_par, east_edge, west_edge)
        lon2_ref[i] = pick(lon_par, west_edge, east_edge)

    pair = iota((8, COLS), 0) // 2
    for i, src in enumerate((mixed_ref, mixed_ref, vel, vel, tr, tr)):
        for g in range(GROUPS):
            first = jnp.zeros((8, COLS), F32)
            last = first
            for q in range(min(4, LEVELS - 4 * g)):
                top, end = src[i % 2, 4 * g + q, :8], src[i % 2, 4 * g + q, ROWS - 8 :]
                first = jnp.where(pair == q, roll(top, 2 * q, 0) if q else top, first)
                last = jnp.where(pair == (q + 3) % 4, roll(end, 2 * q, 0) if q else end, last)
            g1_ref[i * GROUPS + g] = pick(lat_par, last, first)
            g2_ref[i * GROUPS + g] = pick(lat_par, first, last)


CORNERS = 4
EDGES = FIELDS * GROUPS


def corner_of(index):
    return index // 8, index // 2 % 4, index % 2


def lon_kernel(base_ref, o1_ref, o2_ref, slots_ref, g1_ref, ext_ref, lat1_ref, lat2_ref, side_ref):
    lon_par = lax.rem(lax.axis_index("lon"), 2)
    lat_par = lax.rem(lax.axis_index("lat"), 2)
    lane = iota((ROWS, COLS), 1)
    o1, o2 = o1_ref[FIELDS], o2_ref[FIELDS]
    from_east, from_west = pick(lon_par, o1, o2), pick(lon_par, o2, o1)
    for i in range(3):
        own = base_ref[i]
        edge = jnp.where(lane < 16 * i + 8, from_west, from_east)
        edge = roll(edge, COLS - 8 - 16 * i, 1)
        edge = jnp.where((lane < 8) | (lane >= COLS - 8), edge, 0.0)
        ext_ref[i, :, :COLS] = own
        ext_ref[i, :, COLS:] = edge
        for half, here in enumerate((own, edge)):
            first, last = here[:8], here[ROWS - 8 :]
            lat1_ref[EDGES + CORNERS + 2 * i + half] = pick(lat_par, last, first)
            lat2_ref[CORNERS + 2 * i + half] = pick(lat_par, first, last)
    near = lane % 4 < 2
    for i in range(FIELDS):
        b1, b2 = o1_ref[i], o2_ref[i]
        east, west = pick(lon_par, b1, b2), pick(lon_par, b2, b1)
        own_a, own_b = slots_ref[i, 0], slots_ref[i, 1]
        side_ref[0, i, 0] = jnp.where(near, west, own_a)
        side_ref[0, i, 1] = jnp.where(near, roll(west, COLS - 2, 1), own_b)
        side_ref[1, i, 0] = jnp.where(near, own_a, roll(east, 2, 1))
        side_ref[1, i, 1] = jnp.where(near, own_b, east)
    lat1_ref[:EDGES] = g1_ref[...]
    pair = iota((8, COLS), 0) // 2
    for c in range(CORNERS):
        first = jnp.zeros((8, COLS), F32)
        last = first
        for q in range(4):
            side, field, tile = corner_of(4 * c + q)
            x = side_ref[side, field, tile]
            first = jnp.where(pair == q, roll(x[:8], 2 * q, 0) if q else x[:8], first)
            last = jnp.where(pair == (q + 3) % 4, roll(x[ROWS - 8 :], 2 * q, 0) if q else x[ROWS - 8 :], last)
        lat1_ref[EDGES + c] = pick(lat_par, last, first)
        lat2_ref[c] = pick(lat_par, first, last)


def krylov_kernel(ext_ref, lat1_ref, lat2_ref, vec_ref, lev_ref, gram_ref):
    lat_par = lax.rem(lax.axis_index("lat"), 2)
    rows, cols = ROWS + 16, 2 * COLS
    whole = []
    for i in range(3):
        s1 = jnp.concatenate([lat1_ref[EDGES + CORNERS + 2 * i + half] for half in range(2)], axis=1)
        s2 = jnp.concatenate([lat2_ref[CORNERS + 2 * i + half] for half in range(2)], axis=1)
        whole.append(jnp.concatenate([ext_ref[i], pick(lat_par, s1, s2), pick(lat_par, s2, s1)], axis=0))
    f, depth, lev = whole

    def east(x):
        return roll(x, cols - 1, 1)

    def west(x):
        return roll(x, 1, 1)

    def north(x):
        return roll(x, rows - 1, 0)

    def south(x):
        return roll(x, 1, 0)

    sea = jnp.where(lev > 0.0, 1.0, 0.0)
    face_east = 0.5 * (depth + east(depth)) * sea * east(sea)
    face_north = 0.5 * (depth + north(depth)) * sea * north(sea)
    base = (1.0 - sea) + SURFACE_DAMPING * sea
    sub = iota((8, cols), 0)

    def trim(x):
        return jnp.concatenate([x[:ROWS], jnp.where(sub < 4, x[ROWS : ROWS + 8], x[ROWS + 8 :])], axis=0)

    lev_ref[...] = trim(lev)
    vectors = [f]
    vec_ref[0] = trim(f)
    for i in range(1, 5):
        p = vectors[-1]
        flow_east = face_east * (p - east(p))
        flow_north = face_north * (p - north(p))
        p = base * p + (flow_east - west(flow_east)) + (flow_north - south(flow_north))
        vectors.append(p)
        if i < 4:
            vec_ref[i] = trim(p)
    own = [v[:ROWS, :COLS] for v in vectors]
    parts = [split(v) for v in own]
    row = iota((16, COLS), 0)
    hi = jnp.zeros((16, COLS), F32)
    lo = hi
    for at, (i, j) in enumerate(PAIRS):
        p, e = two_prod(own[i], own[j], parts[i], parts[j])
        quarters = [(p[8 * r : 8 * r + 8], e[8 * r : 8 * r + 8]) for r in range(ROWS // 8)]
        total = dd_add(dd_add(quarters[0], quarters[1]), dd_add(quarters[2], quarters[3]))
        for s in (4, 2, 1):
            total = dd_add(total, (roll(total[0], s, 0), roll(total[1], s, 0)))
        hi = jnp.where(row == at, jnp.concatenate([total[0]] * 2, axis=0), hi)
        lo = jnp.where(row == at, jnp.concatenate([total[1]] * 2, axis=0), lo)
    total = (hi, lo)
    for s in (64, 32, 16, 8, 4, 2, 1):
        total = dd_add(total, (roll(total[0], s, 1), roll(total[1], s, 1)))
    lane = iota((16, COLS), 1)
    line = jnp.where(lane == row, total[0], jnp.where(lane == row + 16, total[1], 0.0))
    line = line[:8] + line[8:]
    for s in (4, 2, 1):
        line = line + roll(line, s, 0)
    gram_ref[...] = jnp.concatenate([line] * (gram_ref.shape[0] // 8), axis=0)


def galerkin(gram):
    rows = gram.shape[0]
    parts = [(gram[8 * r : 8 * r + 8], roll(gram[8 * r : 8 * r + 8], COLS - 16, 1)) for r in range(rows // 8)]
    while len(parts) > 1:
        parts = [dd_add(parts[i], parts[i + 1]) for i in range(0, len(parts) - 1, 2)] + parts[len(parts) // 2 * 2 :]
    total = parts[0]
    for s in (4, 2, 1):
        total = dd_add(total, (roll(total[0], s, 0), roll(total[1], s, 0)))
    entry = {}
    for at, (i, j) in enumerate(PAIRS):
        entry[i, j] = entry[j, i] = tuple(jnp.broadcast_to(t[:, at : at + 1], (8, COLS)) for t in total)
    mat = [[entry[i, j + 1] for j in range(4)] for i in range(4)]
    rhs = [entry[i, 0] for i in range(4)]
    size = [jnp.abs(mat[i][i][0]) for i in range(4)]
    for k in range(4):
        fine = mat[k][k][0] > 1e-12 * size[k]
        inv = dd_inv((jnp.where(fine, mat[k][k][0], 1.0), jnp.where(fine, mat[k][k][1], 0.0)))
        inv = tuple(jnp.where(fine, t, 0.0) for t in inv)
        for j in range(k + 1, 4):
            mat[k][j] = dd_mul(mat[k][j], inv)
        rhs[k] = dd_mul(rhs[k], inv)
        for i in range(k + 1, 4):
            less = dd_neg(mat[i][k])
            for j in range(k + 1, 4):
                mat[i][j] = dd_add(mat[i][j], dd_mul(less, mat[k][j]))
            rhs[i] = dd_add(rhs[i], dd_mul(less, rhs[k]))
    for k in range(2, -1, -1):
        for j in range(k + 1, 4):
            rhs[k] = dd_add(rhs[k], dd_neg(dd_mul(mat[k][j], rhs[j])))
    return [r[0] for r in rhs]


SPANS = ((0, 12), (12, 26), (26, 38), (38, LEVELS))
SPAN_LEVELS = 14
TALL = ROWS + 8
BF16 = jnp.bfloat16


class Sweeps:
    def __init__(self, lev_ref, side_ref, h1_ref, h2_ref, c2_ref, lhs, weights):
        self.lev_ref, self.side_ref, self.lhs = lev_ref, side_ref, lhs
        self.h1_ref, self.h2_ref, self.c2_ref = h1_ref, h2_ref, c2_ref
        shape = (COLS, COLS)
        source, target = iota(shape, 0), iota(shape, 1)
        shift = jnp.where(source == target + 1, 1.0, jnp.where(source == target - 1, -1.0, 0.0)).astype(BF16)
        ends = jnp.where(
            (target == COLS - 1) & (source % 2 == 0), 1.0, jnp.where((target == 0) & (source % 2 == 1), -1.0, 0.0)
        ).astype(BF16)
        weights[:COLS] = shift
        weights[COLS : 2 * COLS] = shift
        weights[2 * COLS :] = ends
        self.lane = iota((TALL, COLS), 1)
        pair = iota((8, COLS), 0) // 2
        even = jnp.broadcast_to(lax.rem(lax.axis_index("lat"), 2), (8, COLS)) == 0
        self.masks = [(pair == q) == even for q in range(4)]

    def edge_rows(self, index, q):
        other = self.h2_ref[index] if index < EDGES else self.c2_ref[index - EDGES]
        x = jnp.where(self.masks[q], self.h1_ref[index], other)
        return roll(x, 8 - 2 * q, 0) if q else x

    def tall(self, ref, n, field, k):
        return jnp.concatenate([ref[n, k], self.edge_rows(field * GROUPS + k // 4, k % 4)], axis=0)

    def wet(self, k, rows):
        return jnp.where(float(k) < self.lev_ref[:rows, :COLS], 1.0, 0.0)

    def around(self, ref, side):
        lane = self.lane
        own, edge = roll(ref[:, :COLS], 2, 1), roll(ref[:, COLS:], 2, 1)
        x = jnp.where(lane < 2, own, edge) if side else jnp.where(lane < 2, edge, own)
        for s in (4, 8, 16, 32, 64):
            x = jnp.where(lane < s, x, roll(x, s, 1))
        return x

    def columns(self, first_fields):
        flux1, flux2 = [], []
        for side in range(2):
            levels = self.around(self.lev_ref, side)
            flux1.append([])
            flux2.append([])
            for tile in range(2):
                def column(field, side=side, tile=tile):
                    index = side * 8 + field * 2 + tile
                    return jnp.concatenate(
                        [self.side_ref[side, field, tile], self.edge_rows(EDGES + index // 4, index % 4)], axis=0
                    )

                wet = jnp.where((self.lane // 4 + tile * SLOTS).astype(F32) < levels, 1.0, 0.0)
                move = COURANT * wet
                u, v = column(2), column(3)
                flux1[-1].append([])
                flux2[-1].append([])
                for x in first_fields(side, tile, column, wet):
                    flux = u * x
                    flux1[-1][-1].append(flux)
                    x = x + move * (roll(flux, COLS - 1, 1) - roll(flux, 1, 1))
                    for _ in range(2):
                        x = x + move * self.meridional(v * x)
                    flux2[-1][-1].append((u * x)[:ROWS])
        return flux1, flux2

    @staticmethod
    def meridional(x):
        return roll(x, TALL - 1, 0) - roll(x, 1, 0)

    @staticmethod
    def parts(x):
        hi = x.astype(BF16)
        return hi, (x - hi.astype(F32)).astype(BF16)

    def pack(self, west, east):
        at = iota(east.shape, 1) % 4
        both = jnp.where(at == 2, east, roll(west, 2, 1))
        hi, mid = (t.astype(F32) for t in self.parts(both))
        return jnp.where(at >= 2, hi, roll(mid, COLS - 2, 1))

    def put(self, at, fields):
        x = jnp.concatenate([f for f, _, _ in fields], axis=0)
        edge = [
            jnp.where(iota(e.shape, 1) // 4 == k % SLOTS, e, 0.0) for _, e, k in fields
        ]
        here = pl.ds(at, x.shape[0])
        hi, mid = self.parts(x)
        self.lhs[here, :COLS] = hi
        self.lhs[here, COLS : 2 * COLS] = mid
        self.lhs[here, 2 * COLS :] = jnp.concatenate(edge, axis=0).astype(BF16)


def fetch(pairs, sem):
    out = []
    for c, (first, last) in enumerate(SPANS):
        here = pl.ds(first, last - first)
        out.append([pltpu.make_async_copy(a.at[:, here], b.at[:, here], sem.at[c, i]) for i, (a, b) in enumerate(pairs)])
    return out


def mixed_kernel(
    lev_ref, side_ref, h1_ref, h2_ref, c2_ref, mixed, vel_h,
    swept,
    vel, edge1, edge2, lhs, diff, weights, in_sem,
):
    reads = fetch(((vel_h, vel),), in_sem)
    for r in sum(reads, []):
        r.start()
    sw = Sweeps(lev_ref, side_ref, h1_ref, h2_ref, c2_ref, lhs, weights)
    flux1, flux2 = sw.columns(lambda side, tile, column, wet: (column(0), column(1)))
    for tile in range(2):
        for n in range(2):
            edge1[n, tile] = sw.pack(flux1[0][tile][n], flux1[1][tile][n])
            edge2[n, tile] = sw.pack(flux2[0][tile][n], flux2[1][tile][n])
    for (first, last), part in zip(SPANS, reads):
        for r in part:
            r.wait()
        rows = 0
        for k in range(first, last):
            u, tile = sw.tall(vel, 0, 2, k), k // SLOTS
            sw.put(rows, [(u * sw.tall(mixed, n, n, k), edge1[n, tile], k) for n in range(2)])
            rows += 2 * TALL
        diff[:rows] = jnp.dot(lhs[:rows], weights[...], preferred_element_type=F32)
        rows = 0
        for k in range(first, last):
            move, tile = COURANT * sw.wet(k, TALL), k // SLOTS
            u, v = vel[0, k], sw.tall(vel, 1, 3, k)
            fields = []
            for n in range(2):
                at = (2 * (k - first) + n) * TALL
                x = sw.tall(mixed, n, n, k) + move * diff[at : at + TALL]
                x = x + move * sw.meridional(v * x)
                x = (x + move * sw.meridional(v * x))[:ROWS]
                swept[n, k] = x
                fields.append((u * x, edge2[n, tile], k))
            sw.put(rows, fields)
            rows += 2 * ROWS
        diff[:rows] = jnp.dot(lhs[:rows], weights[...], preferred_element_type=F32)
        for k in range(first, last):
            move = COURANT * sw.wet(k, ROWS)
            for n in range(2):
                at = (2 * (k - first) + n) * ROWS
                swept[n, k] = swept[n, k] + move * diff[at : at + ROWS]


def final_kernel(
    gram_ref, vec_ref, lev_ref, side_ref, h1_ref, h2_ref, c2_ref, swept, vel_h, tr_h,
    adj_h, avel_h, sol_ref,
    vel, tr, adj, avel, sol_s, edge1, edge2, edge3, late, lhs, diff, weights, in_sem, out_sem,
):
    reads = fetch(((vel_h, vel), (tr_h, tr)), in_sem)
    for r in sum(reads, []):
        r.start()
    sw = Sweeps(lev_ref, side_ref, h1_ref, h2_ref, c2_ref, lhs, weights)
    coefs = galerkin(gram_ref[...])
    for half in range(2):
        at = half * COLS
        total = 0.0
        for i in range(4):
            wide = jnp.concatenate([coefs[i]] * (TALL // 8), axis=0)
            total = total + wide * vec_ref[i, :, at : at + COLS]
        sol_s[:, at : at + COLS] = total
    sol_ref[...] = sol_s[:ROWS, :COLS]
    flux1, flux2 = sw.columns(lambda side, tile, column, wet: (wet * sw.around(sol_s, side),))
    for tile in range(2):
        edge1[tile] = sw.pack(flux1[0][tile][0], flux1[1][tile][0])
        edge2[tile] = sw.pack(flux2[0][tile][0], flux2[1][tile][0])
        for n in range(2):
            edge3[n, tile] = sw.pack(side_ref[0, 4 + n, tile], side_ref[1, 4 + n, tile])
    writes = []
    for (first, last), part in zip(SPANS, reads):
        for r in part:
            r.wait()
        rows = 0
        for k in range(first, last, 2):
            fields = []
            for m in (k, k + 1):
                x = sw.wet(m, TALL) * sol_s[:, :COLS]
                fields.append((sw.tall(vel, 0, 2, m) * x, edge1[m // SLOTS], m))
            sw.put(rows, fields)
            rows += 2 * TALL
        diff[:rows] = jnp.dot(lhs[:rows], weights[...], preferred_element_type=F32)
        rows = 0
        for k in range(first, last):
            wet = sw.wet(k, TALL)
            move, at = COURANT * wet, (k - first) * TALL
            v = sw.tall(vel, 1, 3, k)
            x = wet * sol_s[:, :COLS] + move * diff[at : at + TALL]
            x = x + move * sw.meridional(v * x)
            x = (x + move * sw.meridional(v * x))[:ROWS]
            late[k - first] = x
            tile = k // SLOTS
            sw.put(rows, [(vel[0, k] * x, edge2[tile], k)] + [(tr[n, k], edge3[n, tile], k) for n in range(2)])
            rows += 3 * ROWS
        diff[:rows] = jnp.dot(lhs[:rows], weights[...], preferred_element_type=F32)
        for k in range(first, last):
            at = 3 * (k - first) * ROWS
            move = COURANT * sw.wet(k, ROWS)
            x = late[k - first] + move * diff[at : at + ROWS]
            east_sum, north_sum = 0.0, 0.0
            for n in range(2):
                total = swept[n, k] + GAINS[n] * x
                adj[n, k] = total
                at += ROWS
                east_sum = east_sum + total * diff[at : at + ROWS]
                north_sum = north_sum + total * sw.meridional(sw.tall(tr, n, 4 + n, k))[:ROWS]
            avel[0, k] = -move * east_sum
            avel[1, k] = -move * north_sum
        here = pl.ds(first, last - first)
        for i, (src, dst) in enumerate(((adj, adj_h), (avel, avel_h))):
            copy = pltpu.make_async_copy(src.at[:, here], dst.at[:, here], out_sem.at[len(writes) // 2, i])
            copy.start()
            writes.append(copy)
    for copy in writes:
        copy.wait()


def swaps(size, first, periodic):
    out = []
    for i in range(first, size, 2):
        if i + 1 < size or periodic:
            out += [(i, (i + 1) % size), ((i + 1) % size, i)]
    return out


def shape(*dims):
    return jax.ShapeDtypeStruct(dims, F32)


def call(kernel, name, ins, outs, scratch, args, aliases=None):
    here, there = pl.BlockSpec(memory_space=VMEM), pl.BlockSpec(memory_space=pltpu.HBM)
    args = [pltpu.with_memory_space_constraint(a, pltpu.HBM if far else VMEM) for a, far in zip(args, ins)]
    return pl.pallas_call(
        kernel,
        name=name,
        out_shape=tuple(o for o, _ in outs),
        in_specs=[there if far else here for far in ins],
        out_specs=tuple(there if far else here for _, far in outs),
        scratch_shapes=scratch,
        input_output_aliases=aliases or {},
        compiler_params=pltpu.CompilerParams(vmem_limit_bytes=VMEM_LIMIT),
    )(*args)


def kept(*dims):
    return VMEM(dims, F32), False


def per_device(lam_tracer, tracer, velocity, diffusivity, lam_surface, sea_depth, levels):
    lon, lat = lax.axis_size("lon"), lax.axis_size("lat")
    tile = (ROWS, COLS)
    deep = (2, LEVELS) + tile
    mixed, base, lon1, lon2, slots, g1, g2 = call(
        solve_kernel, "column_solve", (True,) * 7,
        (kept(*deep), kept(3, *tile), kept(FIELDS + 1, *tile), kept(FIELDS + 1, *tile),
         kept(FIELDS, 2, *tile), kept(FIELDS * GROUPS, 8, COLS), kept(FIELDS * GROUPS, 8, COLS)),
        [VMEM(deep, F32), VMEM(deep, F32), VMEM(deep, F32), VMEM((LEVELS,) + tile, F32), VMEM(tile, F32), VMEM(tile, jnp.int32),
         VMEM((LEVELS,) + tile, F32), VMEM(deep, F32),
         pltpu.SemaphoreType.DMA((HALF // 5, 4)), pltpu.SemaphoreType.DMA((5,))],
        (lam_tracer, velocity, tracer, diffusivity, lam_surface, sea_depth, levels),
    )
    h2 = lax.ppermute(g2, "lat", swaps(lat, 1, False))
    o1 = lax.ppermute(lon1, "lon", swaps(lon, 0, True))
    o2 = lax.ppermute(lon2, "lon", swaps(lon, 1, True))
    o1, o2, h2 = lax.optimization_barrier((o1, o2, h2))
    ext, lat1, lat2, side = call(
        lon_kernel, "after_lon", (False,) * 5,
        (kept(3, ROWS, 2 * COLS), kept(EDGES + CORNERS + 6, 8, COLS), kept(CORNERS + 6, 8, COLS), kept(2, FIELDS, 2, *tile)),
        [],
        (base, o1, o2, slots, g1),
    )
    lat1 = lax.ppermute(lat1, "lat", swaps(lat, 0, False))
    lat2 = lax.ppermute(lat2, "lat", swaps(lat, 1, False))
    vec, lev, gram = call(
        krylov_kernel, "krylov", (False,) * 3,
        (kept(4, TALL, 2 * COLS), kept(TALL, 2 * COLS), kept(lon * lat, COLS)),
        [],
        (ext, lat1, lat2),
    )
    gram = lax.all_to_all(gram, ("lon", "lat"), 0, 0, tiled=True)
    rows = SPAN_LEVELS * 2 * TALL
    (swept,) = call(
        mixed_kernel, "mixed_sweeps", (False,) * 6 + (True,),
        (kept(*deep),),
        [VMEM(deep, F32), VMEM((2, 2, TALL, COLS), F32), VMEM((2, 2) + tile, F32),
         VMEM((rows, 3 * COLS), BF16), VMEM((rows, COLS), F32), VMEM((3 * COLS, COLS), BF16),
         pltpu.SemaphoreType.DMA((len(SPANS), 1))],
        (lev, side, lat1, h2, lat2, mixed, velocity), {5: 0},
    )
    rows = SPAN_LEVELS * 3 * ROWS
    return call(
        final_kernel, "sweeps", (False,) * 8 + (True,) * 2,
        ((shape(*deep), True), (shape(*deep), True), (shape(*tile), False)),
        [VMEM(deep, F32), VMEM(deep, F32), VMEM(deep, F32), VMEM(deep, F32), VMEM((TALL, 2 * COLS), F32),
         VMEM((2, TALL, COLS), F32), VMEM((2,) + tile, F32), VMEM((2, 2) + tile, F32), VMEM((SPAN_LEVELS,) + tile, F32),
         VMEM((rows, 3 * COLS), BF16), VMEM((rows, COLS), F32), VMEM((3 * COLS, COLS), BF16),
         pltpu.SemaphoreType.DMA((len(SPANS), 2)), pltpu.SemaphoreType.DMA((len(SPANS), 2))],
        (gram, vec, lev, side, lat1, h2, lat2, swept, velocity, tracer),
    )


def solution(mesh):
    deep, flat = P(None, None, "lat", "lon"), P("lat", "lon")
    return jax.shard_map(
        per_device,
        mesh=mesh,
        in_specs=(deep, deep, deep, P(None, "lat", "lon"), flat, flat, flat),
        out_specs=(deep, deep, flat),
        check_vma=False,
    )
```

```python
import math

import jax
import jax.numpy as jnp
from jax import lax
from jax.experimental import pallas as pl
from jax.experimental.pallas import tpu as pltpu
from jax.sharding import PartitionSpec as P

LEVELS = 50
SURFACE_DAMPING = 0.05
COURANT = 0.25
GAINS = (0.7, -0.5)
ROWS = 32
COLS = 128
HALF = LEVELS // 2
SLOTS = 32
FIELDS = 6
GROUPS = -(-LEVELS // 4)
VMEM_LIMIT = 16 * 1024 * 1024
F32 = jnp.float32
VMEM = pltpu.VMEM

PAIRS = tuple((i, j) for i in range(4) for j in range(i, 5))


def iota(shape, dim):
    return lax.broadcasted_iota(jnp.int32, shape, dim)


def pick(parity, even, odd):
    return jnp.where(jnp.broadcast_to(parity, even.shape) == 0, even, odd)


def roll(x, shift, axis):
    return pltpu.roll(x, shift, axis)


def two_sum(a, b):
    s = a + b
    bb = s - a
    return s, (a - (s - bb)) + (b - bb)


def quick_sum(a, b):
    s = a + b
    return s, b - (s - a)


def split(a):
    t = 4097.0 * a
    hi = t - (t - a)
    return hi, a - hi


def two_prod(a, b, sa=None, sb=None):
    ah, al = sa or split(a)
    bh, bl = sb or split(b)
    p = a * b
    return p, ((ah * bh - p) + ah * bl + al * bh) + al * bl


def dd_add(a, b):
    s, e = two_sum(a[0], b[0])
    return quick_sum(s, e + (a[1] + b[1]))


def dd_mul(a, b):
    p, e = two_prod(a[0], b[0])
    return quick_sum(p, e + (a[0] * b[1] + a[1] * b[0]))


def dd_neg(a):
    return -a[0], -a[1]


def dd_inv(a):
    r = 1.0 / a[0]
    p, e = two_prod(a[0], r)
    rest = ((1.0 - p) - e) - a[1] * r
    return quick_sum(r, r * rest)


PAIRED = (0, 1, 2, 5)
LON_TILES = 2 + len(PAIRED)


def put_tile(ref, i, x):
    ref[4 * i : 4 * i + 4] = x.reshape(4, 8, COLS)


def get_tile(ref, i):
    return ref[4 * i : 4 * i + 4].reshape(ROWS, COLS)


def quarter(at, *x):
    return jnp.where(at < 2, jnp.where(at == 0, x[0], x[1]), jnp.where(at == 2, x[2], x[3]))


def solve_kernel(
    lam_h, vel_h, tr_h, dif_h, lams_h, depth_h, lev_h,
    mixed_ref, base_ref, lon1_ref, lon2_ref, slots_ref, g1_ref, g2_ref,
    lam, vel, tr, dif, lams_s, lev_s, w_s, z_s, col_sem, rest_sem,
):
    lon_par = lax.rem(lax.axis_index("lon"), 2)
    lat_par = lax.rem(lax.axis_index("lat"), 2)
    step = 5
    flat = [
        pltpu.make_async_copy(lev_h, lev_s, rest_sem.at[0]),
        pltpu.make_async_copy(lams_h, lams_s, rest_sem.at[1]),
        pltpu.make_async_copy(depth_h, base_ref.at[1], rest_sem.at[2]),
    ]
    copies = []
    for i in range(HALF // step):
        top, low = i * step, LEVELS - (i + 1) * step
        part = []
        for n, at in enumerate((top, low)):
            part.append(pltpu.make_async_copy(dif_h.at[pl.ds(at, step)], dif.at[pl.ds(at, step)], col_sem.at[i, 2 * n]))
            part.append(pltpu.make_async_copy(lam_h.at[:, pl.ds(at, step)], lam.at[:, pl.ds(at, step)], col_sem.at[i, 2 * n + 1]))
        copies.append(part)
    rest = [
        pltpu.make_async_copy(vel_h, vel, rest_sem.at[3]),
        pltpu.make_async_copy(tr_h, tr, rest_sem.at[4]),
    ]
    for c in flat + sum(copies, []) + rest:
        c.start()
    for c in flat:
        c.wait()

    lev = lev_s[...]
    zero = jnp.zeros((ROWS, COLS), F32)

    def coef(k):
        return jnp.where(lev > k + 1, dif[k], 0.0)

    def right(n, k):
        return jnp.where(lev > k, lam[n, k], 0.0)

    e = jnp.ones((ROWS, COLS), F32)
    y = [zero, zero]
    w = zero
    eb = e
    yb = [zero, zero]
    wb = zero
    waited = 0
    for k in range(HALF):
        need = min((k + 1) // step, HALF // step - 1)
        while waited <= need:
            for c in copies[waited]:
                c.wait()
            waited += 1
        c_k = coef(k)
        y = [right(n, k) + w * y[n] for n in range(2)]
        inv = 1.0 / (e + c_k)
        w = c_k * inv
        w_s[k] = w
        for n in range(2):
            z_s[n, k] = y[n] * inv
        e = 1.0 + e * w
        if k < HALF - 1:
            m = LEVELS - 1 - k
            c_m = coef(m - 1)
            yb = [right(n, m) + wb * yb[n] for n in range(2)]
            invb = 1.0 / (eb + c_m)
            wb = c_m * invb
            w_s[m] = wb
            for n in range(2):
                z_s[n, m] = yb[n] * invb
            eb = 1.0 + eb * wb
    for c in rest:
        c.wait()

    lane = iota((ROWS, COLS), 1)
    slot = lane // 4
    begun = set()

    def gather(k, fields):
        tile, s = divmod(k, SLOTS)
        here = slot == s
        for i, x in enumerate(fields):
            before = slots_ref[i, tile] if (i, tile) in begun else zero
            begun.add((i, tile))
            slots_ref[i, tile] = jnp.where(here, roll(x, 4 * s + 2, 1), before)

    def level_done(k, solved):
        for n in range(2):
            mixed_ref[n, k] = solved[n]
        gather(k, (solved[0], solved[1], vel[0, k], vel[1, k], tr[0, k], tr[1, k]))

    inv = 1.0 / (e + eb - 1.0)
    below = [(right(n, HALF) + wb * yb[n] + w * y[n]) * inv for n in range(2)]
    total = list(below)
    level_done(HALF, below)
    above = list(below)
    for i in range(1, HALF + 1):
        k = HALF - i
        for n in range(2):
            above[n] = z_s[n, k] + w_s[k] * above[n]
            total[n] = total[n] + above[n]
        level_done(k, above)
        m = HALF + i
        if m < LEVELS:
            for n in range(2):
                below[n] = z_s[n, m] + w_s[m] * below[n]
                total[n] = total[n] + below[n]
            level_done(m, below)
    f = jnp.where(lev > 0, lams_s[...] + (GAINS[0] * total[0] + GAINS[1] * total[1]) / math.sqrt(LEVELS), 0.0)
    levels = lev.astype(F32)
    base_ref[0] = f
    base_ref[2] = levels
    small = jnp.where(lane < 16, roll(f, 8, 1), jnp.where(lane < 32, roll(base_ref[1], 24, 1), roll(levels, 40, 1)))
    put_tile(lon1_ref, 0, small)
    put_tile(lon2_ref, 0, small)
    at = lane % 4

    def send(place, east_edge, west_edge):
        put_tile(lon1_ref, place, pick(lon_par, east_edge, west_edge))
        put_tile(lon2_ref, place, pick(lon_par, west_edge, east_edge))

    for place, i in enumerate(PAIRED):
        a, b = slots_ref[i, 0], slots_ref[i, 1]
        send(1 + place, jnp.where(at < 2, a, roll(b, 2, 1)), jnp.where(at < 2, roll(a, COLS - 2, 1), b))
    va, vb, ta, tb = slots_ref[3, 0], slots_ref[3, 1], slots_ref[4, 0], slots_ref[4, 1]
    send(
        1 + len(PAIRED),
        quarter(at, roll(ta, COLS - 1, 1), va, roll(tb, 1, 1), roll(vb, 2, 1)),
        quarter(at, roll(vb, COLS - 2, 1), roll(tb, COLS - 1, 1), va, roll(ta, 1, 1)),
    )
    lon2_ref[4 * LON_TILES] = jnp.zeros((8, COLS), F32)

    pair = iota((8, COLS), 0) // 2
    for i, src in enumerate((mixed_ref, mixed_ref, vel, vel, tr, tr)):
        for g in range(GROUPS):
            first = jnp.zeros((8, COLS), F32)
            last = first
            for q in range(min(4, LEVELS - 4 * g)):
                top, end = src[i % 2, 4 * g + q, :8], src[i % 2, 4 * g + q, ROWS - 8 :]
                first = jnp.where(pair == q, roll(top, 2 * q, 0) if q else top, first)
                last = jnp.where(pair == (q + 3) % 4, roll(end, 2 * q, 0) if q else end, last)
            g1_ref[i * GROUPS + g] = pick(lat_par, last, first)
            g2_ref[i * GROUPS + g] = pick(lat_par, first, last)


CORNERS = 4
EDGES = FIELDS * GROUPS


def corner_of(index):
    return index // 8, index // 2 % 4, index % 2


def lon_kernel(base_ref, o1_ref, o2_ref, slots_ref, g1_ref, ext_ref, lat1_ref, lat2_ref, side_ref):
    lon_par = lax.rem(lax.axis_index("lon"), 2)
    lat_par = lax.rem(lax.axis_index("lat"), 2)
    lane = iota((ROWS, COLS), 1)
    o1, o2 = get_tile(o1_ref, 0), get_tile(o2_ref, 0)
    from_east, from_west = pick(lon_par, o1, o2), pick(lon_par, o2, o1)
    for i in range(3):
        own = base_ref[i]
        edge = jnp.where(lane < 16 * i + 8, from_west, from_east)
        edge = roll(edge, COLS - 8 - 16 * i, 1)
        edge = jnp.where((lane < 8) | (lane >= COLS - 8), edge, 0.0)
        ext_ref[i, :, :COLS] = own
        ext_ref[i, :, COLS:] = edge
        for half, here in enumerate((own, edge)):
            first, last = here[:8], here[ROWS - 8 :]
            lat1_ref[EDGES + CORNERS + 2 * i + half] = pick(lat_par, last, first)
            lat2_ref[CORNERS + 2 * i + half] = pick(lat_par, first, last)
    near = lane % 4 < 2

    def receive(place):
        b1, b2 = get_tile(o1_ref, place), get_tile(o2_ref, place)
        return pick(lon_par, b1, b2), pick(lon_par, b2, b1)

    def side_of(i, west_a, west_b, east_a, east_b):
        own_a, own_b = slots_ref[i, 0], slots_ref[i, 1]
        side_ref[0, i, 0] = jnp.where(near, west_a, own_a)
        side_ref[0, i, 1] = jnp.where(near, west_b, own_b)
        side_ref[1, i, 0] = jnp.where(near, own_a, east_a)
        side_ref[1, i, 1] = jnp.where(near, own_b, east_b)

    for place, i in enumerate(PAIRED):
        east, west = receive(1 + place)
        side_of(i, west, roll(west, COLS - 2, 1), roll(east, 2, 1), east)
    east, west = receive(1 + len(PAIRED))
    side_of(3, west, roll(west, COLS - 2, 1), east, roll(east, 2, 1))
    side_of(4, roll(west, 1, 1), roll(west, COLS - 1, 1), roll(east, COLS - 1, 1), roll(east, 1, 1))
    lat1_ref[:EDGES] = g1_ref[...]
    pair = iota((8, COLS), 0) // 2
    for c in range(CORNERS):
        first = jnp.zeros((8, COLS), F32)
        last = first
        for q in range(4):
            side, field, tile = corner_of(4 * c + q)
            x = side_ref[side, field, tile]
            first = jnp.where(pair == q, roll(x[:8], 2 * q, 0) if q else x[:8], first)
            last = jnp.where(pair == (q + 3) % 4, roll(x[ROWS - 8 :], 2 * q, 0) if q else x[ROWS - 8 :], last)
        lat1_ref[EDGES + c] = pick(lat_par, last, first)
        lat2_ref[c] = pick(lat_par, first, last)


def krylov_kernel(ext_ref, lat1_ref, lat2_ref, vec_ref, lev_ref, gram_ref):
    lat_par = lax.rem(lax.axis_index("lat"), 2)
    rows, cols = ROWS + 16, 2 * COLS
    whole = []
    for i in range(3):
        s1 = jnp.concatenate([lat1_ref[EDGES + CORNERS + 2 * i + half] for half in range(2)], axis=1)
        s2 = jnp.concatenate([lat2_ref[CORNERS + 2 * i + half] for half in range(2)], axis=1)
        whole.append(jnp.concatenate([ext_ref[i], pick(lat_par, s1, s2), pick(lat_par, s2, s1)], axis=0))
    f, depth, lev = whole

    def east(x):
        return roll(x, cols - 1, 1)

    def west(x):
        return roll(x, 1, 1)

    def north(x):
        return roll(x, rows - 1, 0)

    def south(x):
        return roll(x, 1, 0)

    sea = jnp.where(lev > 0.0, 1.0, 0.0)
    face_east = 0.5 * (depth + east(depth)) * sea * east(sea)
    face_north = 0.5 * (depth + north(depth)) * sea * north(sea)
    base = (1.0 - sea) + SURFACE_DAMPING * sea
    sub = iota((8, cols), 0)

    def trim(x):
        return jnp.concatenate([x[:ROWS], jnp.where(sub < 4, x[ROWS : ROWS + 8], x[ROWS + 8 :])], axis=0)

    lev_ref[...] = trim(lev)
    vectors = [f]
    vec_ref[0] = trim(f)
    for i in range(1, 5):
        p = vectors[-1]
        flow_east = face_east * (p - east(p))
        flow_north = face_north * (p - north(p))
        p = base * p + (flow_east - west(flow_east)) + (flow_north - south(flow_north))
        vectors.append(p)
        if i < 4:
            vec_ref[i] = trim(p)
    own = [v[:ROWS, :COLS] for v in vectors]
    parts = [split(v) for v in own]
    row = iota((16, COLS), 0)
    hi = jnp.zeros((16, COLS), F32)
    lo = hi
    for at, (i, j) in enumerate(PAIRS):
        p, e = two_prod(own[i], own[j], parts[i], parts[j])
        quarters = [(p[8 * r : 8 * r + 8], e[8 * r : 8 * r + 8]) for r in range(ROWS // 8)]
        total = dd_add(dd_add(quarters[0], quarters[1]), dd_add(quarters[2], quarters[3]))
        for s in (4, 2, 1):
            total = dd_add(total, (roll(total[0], s, 0), roll(total[1], s, 0)))
        hi = jnp.where(row == at, jnp.concatenate([total[0]] * 2, axis=0), hi)
        lo = jnp.where(row == at, jnp.concatenate([total[1]] * 2, axis=0), lo)
    total = (hi, lo)
    for s in (64, 32, 16, 8, 4, 2, 1):
        total = dd_add(total, (roll(total[0], s, 1), roll(total[1], s, 1)))
    lane = iota((16, COLS), 1)
    line = jnp.where(lane == row, total[0], jnp.where(lane == row + 16, total[1], 0.0))
    line = line[:8] + line[8:]
    for s in (4, 2, 1):
        line = line + roll(line, s, 0)
    gram_ref[...] = jnp.concatenate([line] * (gram_ref.shape[0] // 8), axis=0)


def galerkin(gram):
    rows = gram.shape[0]
    parts = [(gram[8 * r : 8 * r + 8], roll(gram[8 * r : 8 * r + 8], COLS - 16, 1)) for r in range(rows // 8)]
    while len(parts) > 1:
        parts = [dd_add(parts[i], parts[i + 1]) for i in range(0, len(parts) - 1, 2)] + parts[len(parts) // 2 * 2 :]
    total = parts[0]
    for s in (4, 2, 1):
        total = dd_add(total, (roll(total[0], s, 0), roll(total[1], s, 0)))
    entry = {}
    for at, (i, j) in enumerate(PAIRS):
        entry[i, j] = entry[j, i] = tuple(jnp.broadcast_to(t[:, at : at + 1], (8, COLS)) for t in total)
    mat = [[entry[i, j + 1] for j in range(4)] for i in range(4)]
    rhs = [entry[i, 0] for i in range(4)]
    size = [jnp.abs(mat[i][i][0]) for i in range(4)]
    for k in range(4):
        fine = mat[k][k][0] > 1e-12 * size[k]
        inv = dd_inv((jnp.where(fine, mat[k][k][0], 1.0), jnp.where(fine, mat[k][k][1], 0.0)))
        inv = tuple(jnp.where(fine, t, 0.0) for t in inv)
        for j in range(k + 1, 4):
            mat[k][j] = dd_mul(mat[k][j], inv)
        rhs[k] = dd_mul(rhs[k], inv)
        for i in range(k + 1, 4):
            less = dd_neg(mat[i][k])
            for j in range(k + 1, 4):
                mat[i][j] = dd_add(mat[i][j], dd_mul(less, mat[k][j]))
            rhs[i] = dd_add(rhs[i], dd_mul(less, rhs[k]))
    for k in range(2, -1, -1):
        for j in range(k + 1, 4):
            rhs[k] = dd_add(rhs[k], dd_neg(dd_mul(mat[k][j], rhs[j])))
    return [r[0] for r in rhs]


SPANS = ((0, 12), (12, 26), (26, 38), (38, LEVELS))
SPAN_LEVELS = 14
PART_LEVELS = 8
TALL = ROWS + 8
BF16 = jnp.bfloat16


class Sweeps:
    def __init__(self, lev_ref, side_ref, h1_ref, h2_ref, c2_ref, weights):
        self.lev_ref, self.side_ref = lev_ref, side_ref
        self.h1_ref, self.h2_ref, self.c2_ref = h1_ref, h2_ref, c2_ref
        shape = (COLS, COLS)
        source, target = iota(shape, 0), iota(shape, 1)
        shift = jnp.where(source == target + 1, 1.0, jnp.where(source == target - 1, -1.0, 0.0)).astype(BF16)
        ends = jnp.where(
            (target == COLS - 1) & (source % 2 == 0), 1.0, jnp.where((target == 0) & (source % 2 == 1), -1.0, 0.0)
        ).astype(BF16)
        weights[:COLS] = shift
        weights[COLS : 2 * COLS] = shift
        weights[2 * COLS :] = ends
        self.lane = iota((TALL, COLS), 1)
        pair = iota((8, COLS), 0) // 2
        even = jnp.broadcast_to(lax.rem(lax.axis_index("lat"), 2), (8, COLS)) == 0
        self.masks = [(pair == q) == even for q in range(4)]

    def edge_rows(self, index, q):
        other = self.h2_ref[index] if index < EDGES else self.c2_ref[index - EDGES]
        x = jnp.where(self.masks[q], self.h1_ref[index], other)
        return roll(x, 8 - 2 * q, 0) if q else x

    def tall(self, ref, n, field, k):
        return jnp.concatenate([ref[n, k], self.edge_rows(field * GROUPS + k // 4, k % 4)], axis=0)

    def wet(self, k, rows):
        return jnp.where(float(k) < self.lev_ref[:rows, :COLS], 1.0, 0.0)

    def around(self, ref, side):
        lane = self.lane
        own, edge = roll(ref[:, :COLS], 2, 1), roll(ref[:, COLS:], 2, 1)
        x = jnp.where(lane < 2, own, edge) if side else jnp.where(lane < 2, edge, own)
        for s in (4, 8, 16, 32, 64):
            x = jnp.where(lane < s, x, roll(x, s, 1))
        return x

    def columns(self, first_fields):
        flux1, flux2 = [], []
        for side in range(2):
            levels = self.around(self.lev_ref, side)
            flux1.append([])
            flux2.append([])
            for tile in range(2):
                def column(field, side=side, tile=tile):
                    index = side * 8 + field * 2 + tile
                    return jnp.concatenate(
                        [self.side_ref[side, field, tile], self.edge_rows(EDGES + index // 4, index % 4)], axis=0
                    )

                wet = jnp.where((self.lane // 4 + tile * SLOTS).astype(F32) < levels, 1.0, 0.0)
                move = COURANT * wet
                u, v = column(2), column(3)
                flux1[-1].append([])
                flux2[-1].append([])
                for x in first_fields(side, tile, column, wet):
                    flux = u * x
                    flux1[-1][-1].append(flux)
                    x = x + move * (roll(flux, COLS - 1, 1) - roll(flux, 1, 1))
                    for _ in range(2):
                        x = x + move * self.meridional(v * x)
                    flux2[-1][-1].append((u * x)[:ROWS])
        return flux1, flux2

    @staticmethod
    def meridional(x):
        return roll(x, TALL - 1, 0) - roll(x, 1, 0)

    @staticmethod
    def parts(x):
        hi = x.astype(BF16)
        return hi, (x - hi.astype(F32)).astype(BF16)

    def pack(self, west, east):
        at = iota(east.shape, 1) % 4
        both = jnp.where(at == 2, east, roll(west, 2, 1))
        hi, mid = (t.astype(F32) for t in self.parts(both))
        return jnp.where(at >= 2, hi, roll(mid, COLS - 2, 1))

    def put(self, lhs, at, fields):
        x = jnp.concatenate([f for f, _, _ in fields], axis=0)
        edge = [
            jnp.where(iota(e.shape, 1) // 4 == k % SLOTS, e, 0.0) for _, e, k in fields
        ]
        here = pl.ds(at, x.shape[0])
        hi, mid = self.parts(x)
        lhs[here, :COLS] = hi
        lhs[here, COLS : 2 * COLS] = mid
        lhs[here, 2 * COLS :] = jnp.concatenate(edge, axis=0).astype(BF16)


def halves(span, lhs, diff):
    first, last = span
    middle = first + (last - first) // 4 * 2
    return [(a, b, l, d) for (a, b), l, d in zip(((first, middle), (middle, last)), lhs, diff)]


def fetch(pairs, sem):
    out = []
    for c, (first, last) in enumerate(SPANS):
        here = pl.ds(first, last - first)
        out.append([pltpu.make_async_copy(a.at[:, here], b.at[:, here], sem.at[c, i]) for i, (a, b) in enumerate(pairs)])
    return out


def mixed_kernel(
    lev_ref, side_ref, h1_ref, h2_ref, c2_ref, mixed, vel_h, tr_h,
    swept, ties_h,
    vel, tr, ties, edge1, edge2, edge3, lhs0, lhs1, diff0, diff1, weights, in_sem, out_sem,
):
    reads = fetch(((vel_h, vel), (tr_h, tr)), in_sem)
    for r in sum(reads, []):
        r.start()
    sw = Sweeps(lev_ref, side_ref, h1_ref, h2_ref, c2_ref, weights)
    flux1, flux2 = sw.columns(lambda side, tile, column, wet: (column(0), column(1)))
    for tile in range(2):
        for n in range(2):
            edge1[n, tile] = sw.pack(flux1[0][tile][n], flux1[1][tile][n])
            edge2[n, tile] = sw.pack(flux2[0][tile][n], flux2[1][tile][n])
            edge3[n, tile] = sw.pack(side_ref[0, 4 + n, tile], side_ref[1, 4 + n, tile])
    writes = []
    for span, part in zip(SPANS, reads):
        for r in part:
            r.wait()
        parts = halves(span, (lhs0, lhs1), (diff0, diff1))
        for first, last, lhs, diff in parts:
            rows = 0
            for k in range(first, last):
                u, tile = sw.tall(vel, 0, 2, k), k // SLOTS
                sw.put(lhs, rows, [(u * sw.tall(mixed, n, n, k), edge1[n, tile], k) for n in range(2)])
                rows += 2 * TALL
            diff[:rows] = jnp.dot(lhs[:rows], weights[...], preferred_element_type=F32)
        for first, last, lhs, diff in parts:
            rows = 0
            for k in range(first, last):
                move, tile = COURANT * sw.wet(k, TALL), k // SLOTS
                u, v = vel[0, k], sw.tall(vel, 1, 3, k)
                fields = []
                for n in range(2):
                    at = (2 * (k - first) + n) * TALL
                    x = sw.tall(mixed, n, n, k) + move * diff[at : at + TALL]
                    x = x + move * sw.meridional(v * x)
                    x = (x + move * sw.meridional(v * x))[:ROWS]
                    swept[n, k] = x
                    fields.append((u * x, edge2[n, tile], k))
                sw.put(lhs, rows, fields + [(tr[n, k], edge3[n, tile], k) for n in range(2)])
                rows += 4 * ROWS
            diff[:rows] = jnp.dot(lhs[:rows], weights[...], preferred_element_type=F32)
        for first, last, lhs, diff in parts:
            for k in range(first, last):
                move, at = COURANT * sw.wet(k, ROWS), 4 * (k - first) * ROWS
                x, east, north = [], [], []
                for n in range(2):
                    x.append(swept[n, k] + move * diff[at + n * ROWS : at + (n + 1) * ROWS])
                    swept[n, k] = x[n]
                    east.append(diff[at + (2 + n) * ROWS : at + (3 + n) * ROWS])
                    north.append(sw.meridional(sw.tall(tr, n, 4 + n, k))[:ROWS])
                for i, d in enumerate((east, north)):
                    ties[2 * i, k] = -move * (x[0] * d[0] + x[1] * d[1])
                    ties[2 * i + 1, k] = -move * (GAINS[0] * d[0] + GAINS[1] * d[1])
        here = pl.ds(span[0], span[1] - span[0])
        copy = pltpu.make_async_copy(ties.at[:, here], ties_h.at[:, here], out_sem.at[len(writes)])
        copy.start()
        writes.append(copy)
    for copy in writes:
        copy.wait()


def final_kernel(
    gram_ref, vec_ref, lev_ref, side_ref, h1_ref, h2_ref, c2_ref, swept, vel_h, ties_h,
    adj_h, avel_h, sol_ref,
    vel, ties, adj, avel, sol_s, edge1, edge2, late, lhs0, lhs1, diff0, diff1, weights, in_sem, out_sem,
):
    reads = fetch(((vel_h, vel), (ties_h, ties)), in_sem)
    for r in sum(reads, []):
        r.start()
    sw = Sweeps(lev_ref, side_ref, h1_ref, h2_ref, c2_ref, weights)
    coefs = galerkin(gram_ref[...])
    for half in range(2):
        at = half * COLS
        total = 0.0
        for i in range(4):
            wide = jnp.concatenate([coefs[i]] * (TALL // 8), axis=0)
            total = total + wide * vec_ref[i, :, at : at + COLS]
        sol_s[:, at : at + COLS] = total
    sol_ref[...] = sol_s[:ROWS, :COLS]
    flux1, flux2 = sw.columns(lambda side, tile, column, wet: (wet * sw.around(sol_s, side),))
    for tile in range(2):
        edge1[tile] = sw.pack(flux1[0][tile][0], flux1[1][tile][0])
        edge2[tile] = sw.pack(flux2[0][tile][0], flux2[1][tile][0])
    writes = []
    for span, part in zip(SPANS, reads):
        for r in part:
            r.wait()
        parts = halves(span, (lhs0, lhs1), (diff0, diff1))
        for first, last, lhs, diff in parts:
            rows = 0
            for k in range(first, last, 2):
                fields = []
                for m in (k, k + 1):
                    x = sw.wet(m, TALL) * sol_s[:, :COLS]
                    fields.append((sw.tall(vel, 0, 2, m) * x, edge1[m // SLOTS], m))
                sw.put(lhs, rows, fields)
                rows += 2 * TALL
            diff[:rows] = jnp.dot(lhs[:rows], weights[...], preferred_element_type=F32)
        for first, last, lhs, diff in parts:
            rows = 0
            for k in range(first, last):
                wet = sw.wet(k, TALL)
                move, at = COURANT * wet, (k - first) * TALL
                v = sw.tall(vel, 1, 3, k)
                x = wet * sol_s[:, :COLS] + move * diff[at : at + TALL]
                x = x + move * sw.meridional(v * x)
                x = (x + move * sw.meridional(v * x))[:ROWS]
                late[k - span[0]] = x
                sw.put(lhs, rows, [(vel[0, k] * x, edge2[k // SLOTS], k)])
                rows += ROWS
            diff[:rows] = jnp.dot(lhs[:rows], weights[...], preferred_element_type=F32)
        for first, last, lhs, diff in parts:
            for k in range(first, last):
                at = (k - first) * ROWS
                x = late[k - span[0]] + COURANT * sw.wet(k, ROWS) * diff[at : at + ROWS]
                for n in range(2):
                    adj[n, k] = swept[n, k] + GAINS[n] * x
                    avel[n, k] = ties[2 * n, k] + ties[2 * n + 1, k] * x
        first, last = span
        here = pl.ds(first, last - first)
        for i, (src, dst) in enumerate(((adj, adj_h), (avel, avel_h))):
            copy = pltpu.make_async_copy(src.at[:, here], dst.at[:, here], out_sem.at[len(writes) // 2, i])
            copy.start()
            writes.append(copy)
    for copy in writes:
        copy.wait()


def swaps(size, first, periodic):
    out = []
    for i in range(first, size, 2):
        if i + 1 < size or periodic:
            out += [(i, (i + 1) % size), ((i + 1) % size, i)]
    return out


def shape(*dims):
    return jax.ShapeDtypeStruct(dims, F32)


def call(kernel, name, ins, outs, scratch, args, aliases=None):
    here, there = pl.BlockSpec(memory_space=VMEM), pl.BlockSpec(memory_space=pltpu.HBM)
    args = [pltpu.with_memory_space_constraint(a, pltpu.HBM if far else VMEM) for a, far in zip(args, ins)]
    return pl.pallas_call(
        kernel,
        name=name,
        out_shape=tuple(o for o, _ in outs),
        in_specs=[there if far else here for far in ins],
        out_specs=tuple(there if far else here for _, far in outs),
        scratch_shapes=scratch,
        input_output_aliases=aliases or {},
        compiler_params=pltpu.CompilerParams(vmem_limit_bytes=VMEM_LIMIT),
    )(*args)


def kept(*dims):
    return VMEM(dims, F32), False


def per_device(lam_tracer, tracer, velocity, diffusivity, lam_surface, sea_depth, levels):
    lon, lat = lax.axis_size("lon"), lax.axis_size("lat")
    tile = (ROWS, COLS)
    deep = (2, LEVELS) + tile
    mixed, base, lon1, lon2, slots, g1, g2 = call(
        solve_kernel, "column_solve", (True,) * 7,
        (kept(*deep), kept(3, *tile), kept(4 * LON_TILES, 8, COLS), kept(4 * LON_TILES + 1, 8, COLS),
         kept(FIELDS, 2, *tile), kept(FIELDS * GROUPS, 8, COLS), kept(FIELDS * GROUPS, 8, COLS)),
        [VMEM(deep, F32), VMEM(deep, F32), VMEM(deep, F32), VMEM((LEVELS,) + tile, F32), VMEM(tile, F32), VMEM(tile, jnp.int32),
         VMEM((LEVELS,) + tile, F32), VMEM(deep, F32),
         pltpu.SemaphoreType.DMA((HALF // 5, 4)), pltpu.SemaphoreType.DMA((5,))],
        (lam_tracer, velocity, tracer, diffusivity, lam_surface, sea_depth, levels),
    )
    h2 = lax.ppermute(g2, "lat", swaps(lat, 1, False))
    o1 = lax.ppermute(lon1, "lon", swaps(lon, 0, True))
    o2 = lax.ppermute(lon2, "lon", swaps(lon, 1, True))
    o1, o2, h2 = lax.optimization_barrier((o1, o2, h2))
    ext, lat1, lat2, side = call(
        lon_kernel, "after_lon", (False,) * 5,
        (kept(3, ROWS, 2 * COLS), kept(EDGES + CORNERS + 6, 8, COLS), kept(CORNERS + 6, 8, COLS), kept(2, FIELDS, 2, *tile)),
        [],
        (base, o1, o2, slots, g1),
    )
    lat1 = lax.ppermute(lat1, "lat", swaps(lat, 0, False))
    lat2 = lax.ppermute(lat2, "lat", swaps(lat, 1, False))
    vec, lev, gram = call(
        krylov_kernel, "krylov", (False,) * 3,
        (kept(4, TALL, 2 * COLS), kept(TALL, 2 * COLS), kept(lon * lat, COLS)),
        [],
        (ext, lat1, lat2),
    )
    gram = lax.all_to_all(gram, ("lon", "lat"), 0, 0, tiled=True)
    rows, many = PART_LEVELS * 4 * ROWS, (4, LEVELS) + tile
    swept, ties = call(
        mixed_kernel, "mixed_sweeps", (False,) * 6 + (True,) * 2,
        (kept(*deep), (pltpu.HBM(many, F32), True)),
        [VMEM(deep, F32), VMEM(deep, F32), VMEM(many, F32), VMEM((2, 2, TALL, COLS), F32), VMEM((2, 2) + tile, F32), VMEM((2, 2) + tile, F32),
         VMEM((rows, 3 * COLS), BF16), VMEM((rows, 3 * COLS), BF16), VMEM((rows, COLS), F32), VMEM((rows, COLS), F32), VMEM((3 * COLS, COLS), BF16),
         pltpu.SemaphoreType.DMA((len(SPANS), 2)), pltpu.SemaphoreType.DMA((len(SPANS),))],
        (lev, side, lat1, h2, lat2, mixed, velocity, tracer), {5: 0},
    )
    rows = PART_LEVELS * TALL
    return call(
        final_kernel, "sweeps", (False,) * 8 + (True,) * 2,
        ((shape(*deep), True), (shape(*deep), True), (shape(*tile), False)),
        [VMEM(deep, F32), VMEM(many, F32), VMEM(deep, F32), VMEM(deep, F32), VMEM((TALL, 2 * COLS), F32),
         VMEM((2, TALL, COLS), F32), VMEM((2,) + tile, F32), VMEM((SPAN_LEVELS,) + tile, F32),
         VMEM((rows, 3 * COLS), BF16), VMEM((rows, 3 * COLS), BF16), VMEM((rows, COLS), F32), VMEM((rows, COLS), F32), VMEM((3 * COLS, COLS), BF16),
         pltpu.SemaphoreType.DMA((len(SPANS), 2)), pltpu.SemaphoreType.DMA((len(SPANS), 2))],
        (gram, vec, lev, side, lat1, h2, lat2, swept, velocity, ties),
    )


def solution(mesh):
    deep, flat = P(None, None, "lat", "lon"), P("lat", "lon")
    return jax.shard_map(
        per_device,
        mesh=mesh,
        in_specs=(deep, deep, deep, P(None, "lat", "lon"), flat, flat, flat),
        out_specs=(deep, deep, flat),
        check_vma=False,
    )
```

```python
import math

import jax
import jax.numpy as jnp
from jax import lax
from jax.experimental import pallas as pl
from jax.experimental.pallas import tpu as pltpu
from jax.sharding import PartitionSpec as P

LEVELS = 50
SURFACE_DAMPING = 0.05
COURANT = 0.25
GAINS = (0.7, -0.5)
ROWS = 32
COLS = 128
HALF = LEVELS // 2
SLOTS = 32
FIELDS = 6
GROUPS = -(-LEVELS // 4)
VMEM_LIMIT = 16 * 1024 * 1024
F32 = jnp.float32
VMEM = pltpu.VMEM

PAIRS = tuple((i, j) for i in range(4) for j in range(i, 5))


def iota(shape, dim):
    return lax.broadcasted_iota(jnp.int32, shape, dim)


def pick(parity, even, odd):
    return jnp.where(jnp.broadcast_to(parity, even.shape) == 0, even, odd)


def roll(x, shift, axis):
    return pltpu.roll(x, shift, axis)


def two_sum(a, b):
    s = a + b
    bb = s - a
    return s, (a - (s - bb)) + (b - bb)


def quick_sum(a, b):
    s = a + b
    return s, b - (s - a)


def split(a):
    t = 4097.0 * a
    hi = t - (t - a)
    return hi, a - hi


def two_prod(a, b, sa=None, sb=None):
    ah, al = sa or split(a)
    bh, bl = sb or split(b)
    p = a * b
    return p, ((ah * bh - p) + ah * bl + al * bh) + al * bl


def dd_add(a, b):
    s, e = two_sum(a[0], b[0])
    return quick_sum(s, e + (a[1] + b[1]))


def dd_mul(a, b):
    p, e = two_prod(a[0], b[0])
    return quick_sum(p, e + (a[0] * b[1] + a[1] * b[0]))


def dd_neg(a):
    return -a[0], -a[1]


def dd_inv(a):
    r = 1.0 / a[0]
    p, e = two_prod(a[0], r)
    rest = ((1.0 - p) - e) - a[1] * r
    return quick_sum(r, r * rest)


PAIRED = (0, 1, 2, 5)
LON_TILES = 2 + len(PAIRED)


def put_tile(ref, i, x):
    ref[4 * i : 4 * i + 4] = x.reshape(4, 8, COLS)


def get_tile(ref, i):
    return ref[4 * i : 4 * i + 4].reshape(ROWS, COLS)


def quarter(at, *x):
    return jnp.where(at < 2, jnp.where(at == 0, x[0], x[1]), jnp.where(at == 2, x[2], x[3]))


def solve_kernel(
    lam_h, vel_h, tr_h, dif_h, lams_h, depth_h, lev_h,
    mixed_ref, base_ref, lon1_ref, lon2_ref, slots_ref, g1_ref, g2_ref,
    lam, vel, tr, dif, lams_s, lev_s, w_s, z_s, col_sem, rest_sem,
):
    lon_par = lax.rem(lax.axis_index("lon"), 2)
    lat_par = lax.rem(lax.axis_index("lat"), 2)
    step = 5
    flat = [
        pltpu.make_async_copy(lev_h, lev_s, rest_sem.at[0]),
        pltpu.make_async_copy(lams_h, lams_s, rest_sem.at[1]),
        pltpu.make_async_copy(depth_h, base_ref.at[1], rest_sem.at[2]),
    ]
    copies = []
    for i in range(HALF // step):
        top, low = i * step, LEVELS - (i + 1) * step
        part = []
        for n, at in enumerate((top, low)):
            part.append(pltpu.make_async_copy(dif_h.at[pl.ds(at, step)], dif.at[pl.ds(at, step)], col_sem.at[i, 2 * n]))
            part.append(pltpu.make_async_copy(lam_h.at[:, pl.ds(at, step)], lam.at[:, pl.ds(at, step)], col_sem.at[i, 2 * n + 1]))
        copies.append(part)
    rest = [
        pltpu.make_async_copy(vel_h, vel, rest_sem.at[3]),
        pltpu.make_async_copy(tr_h, tr, rest_sem.at[4]),
    ]
    for c in flat + sum(copies, []) + rest:
        c.start()
    for c in flat:
        c.wait()

    lev = lev_s[...]
    zero = jnp.zeros((ROWS, COLS), F32)

    def coef(k):
        return jnp.where(lev > k + 1, dif[k], 0.0)

    def right(n, k):
        return jnp.where(lev > k, lam[n, k], 0.0)

    e = jnp.ones((ROWS, COLS), F32)
    y = [zero, zero]
    w = zero
    eb = e
    yb = [zero, zero]
    wb = zero
    waited = 0
    for k in range(HALF):
        need = min((k + 1) // step, HALF // step - 1)
        while waited <= need:
            for c in copies[waited]:
                c.wait()
            waited += 1
        c_k = coef(k)
        y = [right(n, k) + w * y[n] for n in range(2)]
        inv = 1.0 / (e + c_k)
        w = c_k * inv
        w_s[k] = w
        for n in range(2):
            z_s[n, k] = y[n] * inv
        e = 1.0 + e * w
        if k < HALF - 1:
            m = LEVELS - 1 - k
            c_m = coef(m - 1)
            yb = [right(n, m) + wb * yb[n] for n in range(2)]
            invb = 1.0 / (eb + c_m)
            wb = c_m * invb
            w_s[m] = wb
            for n in range(2):
                z_s[n, m] = yb[n] * invb
            eb = 1.0 + eb * wb
    for c in rest:
        c.wait()

    lane = iota((ROWS, COLS), 1)
    slot = lane // 4
    begun = set()

    def gather(k, fields):
        tile, s = divmod(k, SLOTS)
        here = slot == s
        for i, x in enumerate(fields):
            before = slots_ref[i, tile] if (i, tile) in begun else zero
            begun.add((i, tile))
            slots_ref[i, tile] = jnp.where(here, roll(x, 4 * s + 2, 1), before)

    def level_done(k, solved):
        for n in range(2):
            mixed_ref[n, k] = solved[n]
        gather(k, (solved[0], solved[1], vel[0, k], vel[1, k], tr[0, k], tr[1, k]))

    inv = 1.0 / (e + eb - 1.0)
    below = [(right(n, HALF) + wb * yb[n] + w * y[n]) * inv for n in range(2)]
    total = list(below)
    level_done(HALF, below)
    above = list(below)
    for i in range(1, HALF + 1):
        k = HALF - i
        for n in range(2):
            above[n] = z_s[n, k] + w_s[k] * above[n]
            total[n] = total[n] + above[n]
        level_done(k, above)
        m = HALF + i
        if m < LEVELS:
            for n in range(2):
                below[n] = z_s[n, m] + w_s[m] * below[n]
                total[n] = total[n] + below[n]
            level_done(m, below)
    f = jnp.where(lev > 0, lams_s[...] + (GAINS[0] * total[0] + GAINS[1] * total[1]) / math.sqrt(LEVELS), 0.0)
    levels = lev.astype(F32)
    base_ref[0] = f
    base_ref[2] = levels
    small = jnp.where(lane < 16, roll(f, 8, 1), jnp.where(lane < 32, roll(base_ref[1], 24, 1), roll(levels, 40, 1)))
    put_tile(lon1_ref, 0, small)
    put_tile(lon2_ref, 0, small)
    at = lane % 4

    def send(place, east_edge, west_edge):
        put_tile(lon1_ref, place, pick(lon_par, east_edge, west_edge))
        put_tile(lon2_ref, place, pick(lon_par, west_edge, east_edge))

    for place, i in enumerate(PAIRED):
        a, b = slots_ref[i, 0], slots_ref[i, 1]
        send(1 + place, jnp.where(at < 2, a, roll(b, 2, 1)), jnp.where(at < 2, roll(a, COLS - 2, 1), b))
    va, vb, ta, tb = slots_ref[3, 0], slots_ref[3, 1], slots_ref[4, 0], slots_ref[4, 1]
    send(
        1 + len(PAIRED),
        quarter(at, roll(ta, COLS - 1, 1), va, roll(tb, 1, 1), roll(vb, 2, 1)),
        quarter(at, roll(vb, COLS - 2, 1), roll(tb, COLS - 1, 1), va, roll(ta, 1, 1)),
    )
    lon2_ref[4 * LON_TILES] = jnp.zeros((8, COLS), F32)

    pair = iota((8, COLS), 0) // 2
    for i, src in enumerate((mixed_ref, mixed_ref, vel, vel, tr, tr)):
        for g in range(GROUPS):
            first = jnp.zeros((8, COLS), F32)
            last = first
            for q in range(min(4, LEVELS - 4 * g)):
                top, end = src[i % 2, 4 * g + q, :8], src[i % 2, 4 * g + q, ROWS - 8 :]
                first = jnp.where(pair == q, roll(top, 2 * q, 0) if q else top, first)
                last = jnp.where(pair == (q + 3) % 4, roll(end, 2 * q, 0) if q else end, last)
            g1_ref[i * GROUPS + g] = pick(lat_par, last, first)
            g2_ref[i * GROUPS + g] = pick(lat_par, first, last)


CORNERS = 4
EDGES = FIELDS * GROUPS


def corner_of(index):
    return index // 8, index // 2 % 4, index % 2


def lon_kernel(base_ref, o1_ref, o2_ref, slots_ref, ext_ref, lat1_ref, lat2_ref, side_ref):
    lon_par = lax.rem(lax.axis_index("lon"), 2)
    lat_par = lax.rem(lax.axis_index("lat"), 2)
    lane = iota((ROWS, COLS), 1)
    o1, o2 = get_tile(o1_ref, 0), get_tile(o2_ref, 0)
    from_east, from_west = pick(lon_par, o1, o2), pick(lon_par, o2, o1)
    for i in range(3):
        own = base_ref[i]
        edge = jnp.where(lane < 16 * i + 8, from_west, from_east)
        edge = roll(edge, COLS - 8 - 16 * i, 1)
        edge = jnp.where((lane < 8) | (lane >= COLS - 8), edge, 0.0)
        ext_ref[i, :, :COLS] = own
        ext_ref[i, :, COLS:] = edge
        for half, here in enumerate((own, edge)):
            first, last = here[:8], here[ROWS - 8 :]
            lat1_ref[CORNERS + 2 * i + half] = pick(lat_par, last, first)
            lat2_ref[CORNERS + 2 * i + half] = pick(lat_par, first, last)
    lat2_ref[CORNERS + 6] = jnp.zeros((8, COLS), F32)
    near = lane % 4 < 2

    def receive(place):
        b1, b2 = get_tile(o1_ref, place), get_tile(o2_ref, place)
        return pick(lon_par, b1, b2), pick(lon_par, b2, b1)

    def side_of(i, west_a, west_b, east_a, east_b):
        own_a, own_b = slots_ref[i, 0], slots_ref[i, 1]
        side_ref[0, i, 0] = jnp.where(near, west_a, own_a)
        side_ref[0, i, 1] = jnp.where(near, west_b, own_b)
        side_ref[1, i, 0] = jnp.where(near, own_a, east_a)
        side_ref[1, i, 1] = jnp.where(near, own_b, east_b)

    for place, i in enumerate(PAIRED):
        east, west = receive(1 + place)
        side_of(i, west, roll(west, COLS - 2, 1), roll(east, 2, 1), east)
    east, west = receive(1 + len(PAIRED))
    side_of(3, west, roll(west, COLS - 2, 1), east, roll(east, 2, 1))
    side_of(4, roll(west, 1, 1), roll(west, COLS - 1, 1), roll(east, COLS - 1, 1), roll(east, 1, 1))
    pair = iota((8, COLS), 0) // 2
    for c in range(CORNERS):
        first = jnp.zeros((8, COLS), F32)
        last = first
        for q in range(4):
            side, field, tile = corner_of(4 * c + q)
            x = side_ref[side, field, tile]
            first = jnp.where(pair == q, roll(x[:8], 2 * q, 0) if q else x[:8], first)
            last = jnp.where(pair == (q + 3) % 4, roll(x[ROWS - 8 :], 2 * q, 0) if q else x[ROWS - 8 :], last)
        lat1_ref[c] = pick(lat_par, last, first)
        lat2_ref[c] = pick(lat_par, first, last)


def krylov_kernel(ext_ref, lat1_ref, lat2_ref, vec_ref, lev_ref, gram_ref):
    lat_par = lax.rem(lax.axis_index("lat"), 2)
    rows, cols = ROWS + 16, 2 * COLS
    whole = []
    for i in range(3):
        s1 = jnp.concatenate([lat1_ref[CORNERS + 2 * i + half] for half in range(2)], axis=1)
        s2 = jnp.concatenate([lat2_ref[CORNERS + 2 * i + half] for half in range(2)], axis=1)
        whole.append(jnp.concatenate([ext_ref[i], pick(lat_par, s1, s2), pick(lat_par, s2, s1)], axis=0))
    f, depth, lev = whole

    def east(x):
        return roll(x, cols - 1, 1)

    def west(x):
        return roll(x, 1, 1)

    def north(x):
        return roll(x, rows - 1, 0)

    def south(x):
        return roll(x, 1, 0)

    sea = jnp.where(lev > 0.0, 1.0, 0.0)
    face_east = 0.5 * (depth + east(depth)) * sea * east(sea)
    face_north = 0.5 * (depth + north(depth)) * sea * north(sea)
    base = (1.0 - sea) + SURFACE_DAMPING * sea
    sub = iota((8, cols), 0)

    def trim(x):
        return jnp.concatenate([x[:ROWS], jnp.where(sub < 4, x[ROWS : ROWS + 8], x[ROWS + 8 :])], axis=0)

    lev_ref[...] = trim(lev)
    vectors = [f]
    vec_ref[0] = trim(f)
    for i in range(1, 5):
        p = vectors[-1]
        flow_east = face_east * (p - east(p))
        flow_north = face_north * (p - north(p))
        p = base * p + (flow_east - west(flow_east)) + (flow_north - south(flow_north))
        vectors.append(p)
        if i < 4:
            vec_ref[i] = trim(p)
    own = [v[:ROWS, :COLS] for v in vectors]
    parts = [split(v) for v in own]
    row = iota((16, COLS), 0)
    hi = jnp.zeros((16, COLS), F32)
    lo = hi
    for at, (i, j) in enumerate(PAIRS):
        p, e = two_prod(own[i], own[j], parts[i], parts[j])
        quarters = [(p[8 * r : 8 * r + 8], e[8 * r : 8 * r + 8]) for r in range(ROWS // 8)]
        total = dd_add(dd_add(quarters[0], quarters[1]), dd_add(quarters[2], quarters[3]))
        for s in (4, 2, 1):
            total = dd_add(total, (roll(total[0], s, 0), roll(total[1], s, 0)))
        hi = jnp.where(row == at, jnp.concatenate([total[0]] * 2, axis=0), hi)
        lo = jnp.where(row == at, jnp.concatenate([total[1]] * 2, axis=0), lo)
    total = (hi, lo)
    for s in (64, 32, 16, 8, 4, 2, 1):
        total = dd_add(total, (roll(total[0], s, 1), roll(total[1], s, 1)))
    lane = iota((16, COLS), 1)
    line = jnp.where(lane == row, total[0], jnp.where(lane == row + 16, total[1], 0.0))
    line = line[:8] + line[8:]
    for s in (4, 2, 1):
        line = line + roll(line, s, 0)
    gram_ref[...] = jnp.concatenate([line] * (gram_ref.shape[0] // 8), axis=0)


def galerkin(gram):
    rows = gram.shape[0]
    parts = [(gram[8 * r : 8 * r + 8], roll(gram[8 * r : 8 * r + 8], COLS - 16, 1)) for r in range(rows // 8)]
    while len(parts) > 1:
        parts = [dd_add(parts[i], parts[i + 1]) for i in range(0, len(parts) - 1, 2)] + parts[len(parts) // 2 * 2 :]
    total = parts[0]
    for s in (4, 2, 1):
        total = dd_add(total, (roll(total[0], s, 0), roll(total[1], s, 0)))
    entry = {}
    for at, (i, j) in enumerate(PAIRS):
        entry[i, j] = entry[j, i] = tuple(jnp.broadcast_to(t[:, at : at + 1], (8, COLS)) for t in total)
    mat = [[entry[i, j + 1] for j in range(4)] for i in range(4)]
    rhs = [entry[i, 0] for i in range(4)]
    size = [jnp.abs(mat[i][i][0]) for i in range(4)]
    for k in range(4):
        fine = mat[k][k][0] > 1e-12 * size[k]
        inv = dd_inv((jnp.where(fine, mat[k][k][0], 1.0), jnp.where(fine, mat[k][k][1], 0.0)))
        inv = tuple(jnp.where(fine, t, 0.0) for t in inv)
        for j in range(k + 1, 4):
            mat[k][j] = dd_mul(mat[k][j], inv)
        rhs[k] = dd_mul(rhs[k], inv)
        for i in range(k + 1, 4):
            less = dd_neg(mat[i][k])
            for j in range(k + 1, 4):
                mat[i][j] = dd_add(mat[i][j], dd_mul(less, mat[k][j]))
            rhs[i] = dd_add(rhs[i], dd_mul(less, rhs[k]))
    for k in range(2, -1, -1):
        for j in range(k + 1, 4):
            rhs[k] = dd_add(rhs[k], dd_neg(dd_mul(mat[k][j], rhs[j])))
    return [r[0] for r in rhs]


SPANS = ((0, 8), (8, 20), (20, 32), (32, 44), (44, LEVELS))
SPAN_LEVELS = 14
PART_LEVELS = 8
TALL = ROWS + 8
BF16 = jnp.bfloat16


class Sweeps:
    def __init__(self, lev_ref, side_ref, h1_ref, h2_ref, c1_ref, c2_ref, weights):
        self.lev_ref, self.side_ref = lev_ref, side_ref
        self.deep, self.corners = (h1_ref, h2_ref), (c1_ref, c2_ref)
        shape = (COLS, COLS)
        source, target = iota(shape, 0), iota(shape, 1)
        shift = jnp.where(source == target + 1, 1.0, jnp.where(source == target - 1, -1.0, 0.0)).astype(BF16)
        ends = jnp.where(
            (target == COLS - 1) & (source % 2 == 0), 1.0, jnp.where((target == 0) & (source % 2 == 1), -1.0, 0.0)
        ).astype(BF16)
        weights[:COLS] = shift
        weights[COLS : 2 * COLS] = shift
        weights[2 * COLS :] = ends
        self.lane = iota((TALL, COLS), 1)
        pair = iota((8, COLS), 0) // 2
        even = jnp.broadcast_to(lax.rem(lax.axis_index("lat"), 2), (8, COLS)) == 0
        self.masks = [(pair == q) == even for q in range(4)]

    def edge_rows(self, index, q):
        one, two = (r[index] for r in self.deep) if index < EDGES else (r[index - EDGES] for r in self.corners)
        x = jnp.where(self.masks[q], one, two)
        return roll(x, 8 - 2 * q, 0) if q else x

    def tall(self, ref, n, field, k):
        return jnp.concatenate([ref[n, k], self.edge_rows(field * GROUPS + k // 4, k % 4)], axis=0)

    def wet(self, k, rows):
        return jnp.where(float(k) < self.lev_ref[:rows, :COLS], 1.0, 0.0)

    def around(self, ref, side):
        lane = self.lane
        own, edge = roll(ref[:, :COLS], 2, 1), roll(ref[:, COLS:], 2, 1)
        x = jnp.where(lane < 2, own, edge) if side else jnp.where(lane < 2, edge, own)
        for s in (4, 8, 16, 32, 64):
            x = jnp.where(lane < s, x, roll(x, s, 1))
        return x

    def columns(self, first_fields):
        flux1, flux2 = [], []
        for side in range(2):
            levels = self.around(self.lev_ref, side)
            flux1.append([])
            flux2.append([])
            for tile in range(2):
                def column(field, side=side, tile=tile):
                    index = side * 8 + field * 2 + tile
                    return jnp.concatenate(
                        [self.side_ref[side, field, tile], self.edge_rows(EDGES + index // 4, index % 4)], axis=0
                    )

                wet = jnp.where((self.lane // 4 + tile * SLOTS).astype(F32) < levels, 1.0, 0.0)
                move = COURANT * wet
                u, v = column(2), column(3)
                flux1[-1].append([])
                flux2[-1].append([])
                for x in first_fields(side, tile, column, wet):
                    flux = u * x
                    flux1[-1][-1].append(flux)
                    x = x + move * (roll(flux, COLS - 1, 1) - roll(flux, 1, 1))
                    for _ in range(2):
                        x = x + move * self.meridional(v * x)
                    flux2[-1][-1].append((u * x)[:ROWS])
        return flux1, flux2

    @staticmethod
    def meridional(x):
        return roll(x, TALL - 1, 0) - roll(x, 1, 0)

    @staticmethod
    def parts(x):
        hi = x.astype(BF16)
        return hi, (x - hi.astype(F32)).astype(BF16)

    def pack(self, west, east):
        at = iota(east.shape, 1) % 4
        both = jnp.where(at == 2, east, roll(west, 2, 1))
        hi, mid = (t.astype(F32) for t in self.parts(both))
        return jnp.where(at >= 2, hi, roll(mid, COLS - 2, 1))

    def put(self, lhs, at, fields):
        x = jnp.concatenate([f for f, _, _ in fields], axis=0)
        edge = [
            jnp.where(iota(e.shape, 1) // 4 == k % SLOTS, e, 0.0) for _, e, k in fields
        ]
        here = pl.ds(at, x.shape[0])
        hi, mid = self.parts(x)
        lhs[here, :COLS] = hi
        lhs[here, COLS : 2 * COLS] = mid
        lhs[here, 2 * COLS :] = jnp.concatenate(edge, axis=0).astype(BF16)


def halves(span, lhs, diff):
    first, last = span
    middle = first + (last - first) // 4 * 2
    return [(a, b, l, d) for (a, b), l, d in zip(((first, middle), (middle, last)), lhs, diff)]


def fetch(pairs, sem):
    out = []
    for c, (first, last) in enumerate(SPANS):
        here = pl.ds(first, last - first)
        out.append([pltpu.make_async_copy(a.at[:, here], b.at[:, here], sem.at[c, i]) for i, (a, b) in enumerate(pairs)])
    return out


def mixed_kernel(
    lev_ref, side_ref, h1_ref, h2_ref, c1_ref, c2_ref, mixed, vel_h, tr_h,
    swept, ties_h,
    vel, tr, ties, edge1, edge2, edge3, lhs0, lhs1, diff0, diff1, weights, in_sem, out_sem,
):
    reads = fetch(((vel_h, vel), (tr_h, tr)), in_sem)
    for r in sum(reads, []):
        r.start()
    sw = Sweeps(lev_ref, side_ref, h1_ref, h2_ref, c1_ref, c2_ref, weights)
    flux1, flux2 = sw.columns(lambda side, tile, column, wet: (column(0), column(1)))
    for tile in range(2):
        for n in range(2):
            edge1[n, tile] = sw.pack(flux1[0][tile][n], flux1[1][tile][n])
            edge2[n, tile] = sw.pack(flux2[0][tile][n], flux2[1][tile][n])
            edge3[n, tile] = sw.pack(side_ref[0, 4 + n, tile], side_ref[1, 4 + n, tile])
    writes = []
    for span, part in zip(SPANS, reads):
        for r in part:
            r.wait()
        parts = halves(span, (lhs0, lhs1), (diff0, diff1))
        for first, last, lhs, diff in parts:
            rows = 0
            for k in range(first, last):
                u, tile = sw.tall(vel, 0, 2, k), k // SLOTS
                sw.put(lhs, rows, [(u * sw.tall(mixed, n, n, k), edge1[n, tile], k) for n in range(2)])
                rows += 2 * TALL
            diff[:rows] = jnp.dot(lhs[:rows], weights[...], preferred_element_type=F32)
        for first, last, lhs, diff in parts:
            rows = 0
            for k in range(first, last):
                move, tile = COURANT * sw.wet(k, TALL), k // SLOTS
                u, v = vel[0, k], sw.tall(vel, 1, 3, k)
                fields = []
                for n in range(2):
                    at = (2 * (k - first) + n) * TALL
                    x = sw.tall(mixed, n, n, k) + move * diff[at : at + TALL]
                    x = x + move * sw.meridional(v * x)
                    x = (x + move * sw.meridional(v * x))[:ROWS]
                    swept[n, k] = x
                    fields.append((u * x, edge2[n, tile], k))
                sw.put(lhs, rows, fields + [(tr[n, k], edge3[n, tile], k) for n in range(2)])
                rows += 4 * ROWS
            diff[:rows] = jnp.dot(lhs[:rows], weights[...], preferred_element_type=F32)
        for first, last, lhs, diff in parts:
            for k in range(first, last):
                move, at = COURANT * sw.wet(k, ROWS), 4 * (k - first) * ROWS
                x, east, north = [], [], []
                for n in range(2):
                    x.append(swept[n, k] + move * diff[at + n * ROWS : at + (n + 1) * ROWS])
                    swept[n, k] = x[n]
                    east.append(diff[at + (2 + n) * ROWS : at + (3 + n) * ROWS])
                    north.append(sw.meridional(sw.tall(tr, n, 4 + n, k))[:ROWS])
                for i, d in enumerate((east, north)):
                    ties[2 * i, k] = -move * (x[0] * d[0] + x[1] * d[1])
                    ties[2 * i + 1, k] = -move * (GAINS[0] * d[0] + GAINS[1] * d[1])
        here = pl.ds(span[0], span[1] - span[0])
        copy = pltpu.make_async_copy(ties.at[:, here], ties_h.at[:, here], out_sem.at[len(writes)])
        copy.start()
        writes.append(copy)
    for copy in writes:
        copy.wait()


def final_kernel(
    gram_ref, vec_ref, lev_ref, side_ref, h1_ref, h2_ref, c1_ref, c2_ref, swept, vel_h, ties_h,
    adj_h, avel_h, sol_ref,
    vel, ties, adj, avel, sol_s, edge1, edge2, late, lhs0, lhs1, diff0, diff1, weights, in_sem, out_sem,
):
    reads = fetch(((vel_h, vel), (ties_h, ties)), in_sem)
    for r in sum(reads, []):
        r.start()
    sw = Sweeps(lev_ref, side_ref, h1_ref, h2_ref, c1_ref, c2_ref, weights)
    coefs = galerkin(gram_ref[...])
    for half in range(2):
        at = half * COLS
        total = 0.0
        for i in range(4):
            wide = jnp.concatenate([coefs[i]] * (TALL // 8), axis=0)
            total = total + wide * vec_ref[i, :, at : at + COLS]
        sol_s[:, at : at + COLS] = total
    sol_ref[...] = sol_s[:ROWS, :COLS]
    flux1, flux2 = sw.columns(lambda side, tile, column, wet: (wet * sw.around(sol_s, side),))
    for tile in range(2):
        edge1[tile] = sw.pack(flux1[0][tile][0], flux1[1][tile][0])
        edge2[tile] = sw.pack(flux2[0][tile][0], flux2[1][tile][0])
    writes = []
    for span, part in zip(SPANS, reads):
        for r in part:
            r.wait()
        parts = halves(span, (lhs0, lhs1), (diff0, diff1))
        for first, last, lhs, diff in parts:
            rows = 0
            for k in range(first, last, 2):
                fields = []
                for m in (k, k + 1):
                    x = sw.wet(m, TALL) * sol_s[:, :COLS]
                    fields.append((sw.tall(vel, 0, 2, m) * x, edge1[m // SLOTS], m))
                sw.put(lhs, rows, fields)
                rows += 2 * TALL
            diff[:rows] = jnp.dot(lhs[:rows], weights[...], preferred_element_type=F32)
        for first, last, lhs, diff in parts:
            rows = 0
            for k in range(first, last):
                wet = sw.wet(k, TALL)
                move, at = COURANT * wet, (k - first) * TALL
                v = sw.tall(vel, 1, 3, k)
                x = wet * sol_s[:, :COLS] + move * diff[at : at + TALL]
                x = x + move * sw.meridional(v * x)
                x = (x + move * sw.meridional(v * x))[:ROWS]
                late[k - span[0]] = x
                sw.put(lhs, rows, [(vel[0, k] * x, edge2[k // SLOTS], k)])
                rows += ROWS
            diff[:rows] = jnp.dot(lhs[:rows], weights[...], preferred_element_type=F32)
        for first, last, lhs, diff in parts:
            for k in range(first, last):
                at = (k - first) * ROWS
                x = late[k - span[0]] + COURANT * sw.wet(k, ROWS) * diff[at : at + ROWS]
                for n in range(2):
                    adj[n, k] = swept[n, k] + GAINS[n] * x
                    avel[n, k] = ties[2 * n, k] + ties[2 * n + 1, k] * x
        first, last = span
        here = pl.ds(first, last - first)
        for i, (src, dst) in enumerate(((adj, adj_h), (avel, avel_h))):
            copy = pltpu.make_async_copy(src.at[:, here], dst.at[:, here], out_sem.at[len(writes) // 2, i])
            copy.start()
            writes.append(copy)
    for copy in writes:
        copy.wait()


def swaps(size, first, periodic):
    out = []
    for i in range(first, size, 2):
        if i + 1 < size or periodic:
            out += [(i, (i + 1) % size), ((i + 1) % size, i)]
    return out


def shape(*dims):
    return jax.ShapeDtypeStruct(dims, F32)


def call(kernel, name, ins, outs, scratch, args, aliases=None):
    here, there = pl.BlockSpec(memory_space=VMEM), pl.BlockSpec(memory_space=pltpu.HBM)
    args = [pltpu.with_memory_space_constraint(a, pltpu.HBM if far else VMEM) for a, far in zip(args, ins)]
    return pl.pallas_call(
        kernel,
        name=name,
        out_shape=tuple(o for o, _ in outs),
        in_specs=[there if far else here for far in ins],
        out_specs=tuple(there if far else here for _, far in outs),
        scratch_shapes=scratch,
        input_output_aliases=aliases or {},
        compiler_params=pltpu.CompilerParams(vmem_limit_bytes=VMEM_LIMIT),
    )(*args)


def kept(*dims):
    return VMEM(dims, F32), False


def per_device(lam_tracer, tracer, velocity, diffusivity, lam_surface, sea_depth, levels):
    lon, lat = lax.axis_size("lon"), lax.axis_size("lat")
    tile = (ROWS, COLS)
    deep = (2, LEVELS) + tile
    mixed, base, lon1, lon2, slots, g1, g2 = call(
        solve_kernel, "column_solve", (True,) * 7,
        (kept(*deep), kept(3, *tile), kept(4 * LON_TILES, 8, COLS), kept(4 * LON_TILES + 1, 8, COLS),
         kept(FIELDS, 2, *tile), kept(FIELDS * GROUPS, 8, COLS), kept(FIELDS * GROUPS, 8, COLS)),
        [VMEM(deep, F32), VMEM(deep, F32), VMEM(deep, F32), VMEM((LEVELS,) + tile, F32), VMEM(tile, F32), VMEM(tile, jnp.int32),
         VMEM((LEVELS,) + tile, F32), VMEM(deep, F32),
         pltpu.SemaphoreType.DMA((HALF // 5, 4)), pltpu.SemaphoreType.DMA((5,))],
        (lam_tracer, velocity, tracer, diffusivity, lam_surface, sea_depth, levels),
    )
    h1 = lax.ppermute(g1, "lat", swaps(lat, 0, False))
    h2 = lax.ppermute(g2, "lat", swaps(lat, 1, False))
    o1 = lax.ppermute(lon1, "lon", swaps(lon, 0, True))
    o2 = lax.ppermute(lon2, "lon", swaps(lon, 1, True))
    o1, o2, h1, h2 = lax.optimization_barrier((o1, o2, h1, h2))
    ext, lat1, lat2, side = call(
        lon_kernel, "after_lon", (False,) * 4,
        (kept(3, ROWS, 2 * COLS), kept(CORNERS + 6, 8, COLS), kept(CORNERS + 7, 8, COLS), kept(2, FIELDS, 2, *tile)),
        [],
        (base, o1, o2, slots),
    )
    lat1 = lax.ppermute(lat1, "lat", swaps(lat, 0, False))
    lat2 = lax.ppermute(lat2, "lat", swaps(lat, 1, False))
    vec, lev, gram = call(
        krylov_kernel, "krylov", (False,) * 3,
        (kept(4, TALL, 2 * COLS), kept(TALL, 2 * COLS), kept(lon * lat, COLS)),
        [],
        (ext, lat1, lat2),
    )
    gram = lax.all_to_all(gram, ("lon", "lat"), 0, 0, tiled=True)
    rows, many = PART_LEVELS * 4 * ROWS, (4, LEVELS) + tile
    swept, ties = call(
        mixed_kernel, "mixed_sweeps", (False,) * 7 + (True,) * 2,
        (kept(*deep), (pltpu.HBM(many, F32), True)),
        [VMEM(deep, F32), VMEM(deep, F32), VMEM(many, F32), VMEM((2, 2, TALL, COLS), F32), VMEM((2, 2) + tile, F32), VMEM((2, 2) + tile, F32),
         VMEM((rows, 3 * COLS), BF16), VMEM((rows, 3 * COLS), BF16), VMEM((rows, COLS), F32), VMEM((rows, COLS), F32), VMEM((3 * COLS, COLS), BF16),
         pltpu.SemaphoreType.DMA((len(SPANS), 2)), pltpu.SemaphoreType.DMA((len(SPANS),))],
        (lev, side, h1, h2, lat1, lat2, mixed, velocity, tracer), {6: 0},
    )
    rows = PART_LEVELS * TALL
    return call(
        final_kernel, "sweeps", (False,) * 9 + (True,) * 2,
        ((shape(*deep), True), (shape(*deep), True), (shape(*tile), False)),
        [VMEM(deep, F32), VMEM(many, F32), VMEM(deep, F32), VMEM(deep, F32), VMEM((TALL, 2 * COLS), F32),
         VMEM((2, TALL, COLS), F32), VMEM((2,) + tile, F32), VMEM((SPAN_LEVELS,) + tile, F32),
         VMEM((rows, 3 * COLS), BF16), VMEM((rows, 3 * COLS), BF16), VMEM((rows, COLS), F32), VMEM((rows, COLS), F32), VMEM((3 * COLS, COLS), BF16),
         pltpu.SemaphoreType.DMA((len(SPANS), 2)), pltpu.SemaphoreType.DMA((len(SPANS), 2))],
        (gram, vec, lev, side, h1, h2, lat1, lat2, swept, velocity, ties),
    )


def solution(mesh):
    deep, flat = P(None, None, "lat", "lon"), P("lat", "lon")
    return jax.shard_map(
        per_device,
        mesh=mesh,
        in_specs=(deep, deep, deep, P(None, "lat", "lon"), flat, flat, flat),
        out_specs=(deep, deep, flat),
        check_vma=False,
    )
```

```python
import math

import jax
import jax.numpy as jnp
from jax import lax
from jax.experimental import pallas as pl
from jax.experimental.pallas import tpu as pltpu
from jax.sharding import PartitionSpec as P

LEVELS = 50
SURFACE_DAMPING = 0.05
COURANT = 0.25
GAINS = (0.7, -0.5)
ROWS = 32
COLS = 128
HALF = LEVELS // 2
SLOTS = 32
FIELDS = 6
GROUPS = -(-LEVELS // 4)
VMEM_LIMIT = 16 * 1024 * 1024
F32 = jnp.float32
VMEM = pltpu.VMEM

PAIRS = tuple((i, j) for i in range(4) for j in range(i, 5))


def iota(shape, dim):
    return lax.broadcasted_iota(jnp.int32, shape, dim)


def pick(parity, even, odd):
    return jnp.where(jnp.broadcast_to(parity, even.shape) == 0, even, odd)


def roll(x, shift, axis):
    return pltpu.roll(x, shift, axis)


def two_sum(a, b):
    s = a + b
    bb = s - a
    return s, (a - (s - bb)) + (b - bb)


def quick_sum(a, b):
    s = a + b
    return s, b - (s - a)


def split(a):
    t = 4097.0 * a
    hi = t - (t - a)
    return hi, a - hi


def two_prod(a, b, sa=None, sb=None):
    ah, al = sa or split(a)
    bh, bl = sb or split(b)
    p = a * b
    return p, ((ah * bh - p) + ah * bl + al * bh) + al * bl


def dd_add(a, b):
    s, e = two_sum(a[0], b[0])
    return quick_sum(s, e + (a[1] + b[1]))


def dd_mul(a, b):
    p, e = two_prod(a[0], b[0])
    return quick_sum(p, e + (a[0] * b[1] + a[1] * b[0]))


def dd_neg(a):
    return -a[0], -a[1]


def dd_inv(a):
    r = 1.0 / a[0]
    p, e = two_prod(a[0], r)
    rest = ((1.0 - p) - e) - a[1] * r
    return quick_sum(r, r * rest)


PAIRED = (0, 1, 2, 5)
LON_TILES = 2 + len(PAIRED)


def put_tile(ref, i, x):
    ref[4 * i : 4 * i + 4] = x.reshape(4, 8, COLS)


def get_tile(ref, i):
    return ref[4 * i : 4 * i + 4].reshape(ROWS, COLS)


def quarter(at, *x):
    return jnp.where(at < 2, jnp.where(at == 0, x[0], x[1]), jnp.where(at == 2, x[2], x[3]))


def solve_kernel(
    lam_h, vel_h, tr_h, dif_h, lams_h, depth_h, lev_h,
    mixed_ref, base_ref, lon1_ref, lon2_ref, slots_ref, g1_ref, g2_ref,
    lam, vel, tr, dif, lams_s, lev_s, w_s, z_s, col_sem, rest_sem,
):
    lon_par = lax.rem(lax.axis_index("lon"), 2)
    lat_par = lax.rem(lax.axis_index("lat"), 2)
    step = 5
    flat = [
        pltpu.make_async_copy(lev_h, lev_s, rest_sem.at[0]),
        pltpu.make_async_copy(lams_h, lams_s, rest_sem.at[1]),
        pltpu.make_async_copy(depth_h, base_ref.at[1], rest_sem.at[2]),
    ]
    copies = []
    for i in range(HALF // step):
        top, low = i * step, LEVELS - (i + 1) * step
        part = []
        for n, at in enumerate((top, low)):
            part.append(pltpu.make_async_copy(dif_h.at[pl.ds(at, step)], dif.at[pl.ds(at, step)], col_sem.at[i, 2 * n]))
            part.append(pltpu.make_async_copy(lam_h.at[:, pl.ds(at, step)], lam.at[:, pl.ds(at, step)], col_sem.at[i, 2 * n + 1]))
        copies.append(part)
    rest = [
        pltpu.make_async_copy(vel_h, vel, rest_sem.at[3]),
        pltpu.make_async_copy(tr_h, tr, rest_sem.at[4]),
    ]
    for c in flat + sum(copies, []) + rest:
        c.start()
    for c in flat:
        c.wait()

    lev = lev_s[...]
    zero = jnp.zeros((ROWS, COLS), F32)

    def coef(k):
        return jnp.where(lev > k + 1, dif[k], 0.0)

    def right(n, k):
        return jnp.where(lev > k, lam[n, k], 0.0)

    e = jnp.ones((ROWS, COLS), F32)
    y = [zero, zero]
    w = zero
    eb = e
    yb = [zero, zero]
    wb = zero
    waited = 0
    for k in range(HALF):
        need = min((k + 1) // step, HALF // step - 1)
        while waited <= need:
            for c in copies[waited]:
                c.wait()
            waited += 1
        c_k = coef(k)
        y = [right(n, k) + w * y[n] for n in range(2)]
        inv = 1.0 / (e + c_k)
        w = c_k * inv
        w_s[k] = w
        for n in range(2):
            z_s[n, k] = y[n] * inv
        e = 1.0 + e * w
        if k < HALF - 1:
            m = LEVELS - 1 - k
            c_m = coef(m - 1)
            yb = [right(n, m) + wb * yb[n] for n in range(2)]
            invb = 1.0 / (eb + c_m)
            wb = c_m * invb
            w_s[m] = wb
            for n in range(2):
                z_s[n, m] = yb[n] * invb
            eb = 1.0 + eb * wb
    for c in rest:
        c.wait()

    pair = iota((8, COLS), 0) // 2
    sources = (mixed_ref, mixed_ref, vel, vel, tr, tr)

    def edge_rows(i):
        src = sources[i]
        for g in range(GROUPS):
            first = jnp.zeros((8, COLS), F32)
            last = first
            for q in range(min(4, LEVELS - 4 * g)):
                top, end = src[i % 2, 4 * g + q, :8], src[i % 2, 4 * g + q, ROWS - 8 :]
                first = jnp.where(pair == q, roll(top, 2 * q, 0) if q else top, first)
                last = jnp.where(pair == (q + 3) % 4, roll(end, 2 * q, 0) if q else end, last)
            g1_ref[i * GROUPS + g] = pick(lat_par, last, first)
            g2_ref[i * GROUPS + g] = pick(lat_par, first, last)

    for i in range(2, FIELDS):
        edge_rows(i)

    lane = iota((ROWS, COLS), 1)
    slot = lane // 4
    begun = set()

    def gather(k, fields):
        tile, s = divmod(k, SLOTS)
        here = slot == s
        for i, x in enumerate(fields):
            before = slots_ref[i, tile] if (i, tile) in begun else zero
            begun.add((i, tile))
            slots_ref[i, tile] = jnp.where(here, roll(x, 4 * s + 2, 1), before)

    def level_done(k, solved):
        for n in range(2):
            mixed_ref[n, k] = solved[n]
        gather(k, (solved[0], solved[1], vel[0, k], vel[1, k], tr[0, k], tr[1, k]))

    inv = 1.0 / (e + eb - 1.0)
    below = [(right(n, HALF) + wb * yb[n] + w * y[n]) * inv for n in range(2)]
    total = list(below)
    level_done(HALF, below)
    above = list(below)
    for i in range(1, HALF + 1):
        k = HALF - i
        for n in range(2):
            above[n] = z_s[n, k] + w_s[k] * above[n]
            total[n] = total[n] + above[n]
        level_done(k, above)
        m = HALF + i
        if m < LEVELS:
            for n in range(2):
                below[n] = z_s[n, m] + w_s[m] * below[n]
                total[n] = total[n] + below[n]
            level_done(m, below)
    f = jnp.where(lev > 0, lams_s[...] + (GAINS[0] * total[0] + GAINS[1] * total[1]) / math.sqrt(LEVELS), 0.0)
    levels = lev.astype(F32)
    base_ref[0] = f
    base_ref[2] = levels
    small = jnp.where(lane < 16, roll(f, 8, 1), jnp.where(lane < 32, roll(base_ref[1], 24, 1), roll(levels, 40, 1)))
    put_tile(lon1_ref, 0, small)
    put_tile(lon2_ref, 0, small)
    at = lane % 4

    def send(place, east_edge, west_edge):
        put_tile(lon1_ref, place, pick(lon_par, east_edge, west_edge))
        put_tile(lon2_ref, place, pick(lon_par, west_edge, east_edge))

    for place, i in enumerate(PAIRED):
        a, b = slots_ref[i, 0], slots_ref[i, 1]
        send(1 + place, jnp.where(at < 2, a, roll(b, 2, 1)), jnp.where(at < 2, roll(a, COLS - 2, 1), b))
    va, vb, ta, tb = slots_ref[3, 0], slots_ref[3, 1], slots_ref[4, 0], slots_ref[4, 1]
    send(
        1 + len(PAIRED),
        quarter(at, roll(ta, COLS - 1, 1), va, roll(tb, 1, 1), roll(vb, 2, 1)),
        quarter(at, roll(vb, COLS - 2, 1), roll(tb, COLS - 1, 1), va, roll(ta, 1, 1)),
    )
    lon2_ref[4 * LON_TILES] = jnp.zeros((8, COLS), F32)

    for i in range(2):
        edge_rows(i)


CORNERS = 4
EDGES = FIELDS * GROUPS


def corner_of(index):
    return index // 8, index // 2 % 4, index % 2


def lon_kernel(base_ref, o1_ref, o2_ref, slots_ref, ext_ref, lat1_ref, lat2_ref, side_ref):
    lon_par = lax.rem(lax.axis_index("lon"), 2)
    lat_par = lax.rem(lax.axis_index("lat"), 2)
    lane = iota((ROWS, COLS), 1)
    o1, o2 = get_tile(o1_ref, 0), get_tile(o2_ref, 0)
    from_east, from_west = pick(lon_par, o1, o2), pick(lon_par, o2, o1)
    for i in range(3):
        own = base_ref[i]
        edge = jnp.where(lane < 16 * i + 8, from_west, from_east)
        edge = roll(edge, COLS - 8 - 16 * i, 1)
        edge = jnp.where((lane < 8) | (lane >= COLS - 8), edge, 0.0)
        ext_ref[i, :, :COLS] = own
        ext_ref[i, :, COLS:] = edge
        for half, here in enumerate((own, edge)):
            first, last = here[:8], here[ROWS - 8 :]
            lat1_ref[CORNERS + 2 * i + half] = pick(lat_par, last, first)
            lat2_ref[CORNERS + 2 * i + half] = pick(lat_par, first, last)
    lat2_ref[CORNERS + 6] = jnp.zeros((8, COLS), F32)
    near = lane % 4 < 2

    def receive(place):
        b1, b2 = get_tile(o1_ref, place), get_tile(o2_ref, place)
        return pick(lon_par, b1, b2), pick(lon_par, b2, b1)

    def side_of(i, west_a, west_b, east_a, east_b):
        own_a, own_b = slots_ref[i, 0], slots_ref[i, 1]
        side_ref[0, i, 0] = jnp.where(near, west_a, own_a)
        side_ref[0, i, 1] = jnp.where(near, west_b, own_b)
        side_ref[1, i, 0] = jnp.where(near, own_a, east_a)
        side_ref[1, i, 1] = jnp.where(near, own_b, east_b)

    for place, i in enumerate(PAIRED):
        east, west = receive(1 + place)
        side_of(i, west, roll(west, COLS - 2, 1), roll(east, 2, 1), east)
    east, west = receive(1 + len(PAIRED))
    side_of(3, west, roll(west, COLS - 2, 1), east, roll(east, 2, 1))
    side_of(4, roll(west, 1, 1), roll(west, COLS - 1, 1), roll(east, COLS - 1, 1), roll(east, 1, 1))
    pair = iota((8, COLS), 0) // 2
    for c in range(CORNERS):
        first = jnp.zeros((8, COLS), F32)
        last = first
        for q in range(4):
            side, field, tile = corner_of(4 * c + q)
            x = side_ref[side, field, tile]
            first = jnp.where(pair == q, roll(x[:8], 2 * q, 0) if q else x[:8], first)
            last = jnp.where(pair == (q + 3) % 4, roll(x[ROWS - 8 :], 2 * q, 0) if q else x[ROWS - 8 :], last)
        lat1_ref[c] = pick(lat_par, last, first)
        lat2_ref[c] = pick(lat_par, first, last)


def krylov_kernel(ext_ref, lat1_ref, lat2_ref, vec_ref, lev_ref, gram_ref):
    lat_par = lax.rem(lax.axis_index("lat"), 2)
    rows, cols = ROWS + 16, 2 * COLS
    whole = []
    for i in range(3):
        s1 = jnp.concatenate([lat1_ref[CORNERS + 2 * i + half] for half in range(2)], axis=1)
        s2 = jnp.concatenate([lat2_ref[CORNERS + 2 * i + half] for half in range(2)], axis=1)
        whole.append(jnp.concatenate([ext_ref[i], pick(lat_par, s1, s2), pick(lat_par, s2, s1)], axis=0))
    f, depth, lev = whole

    def east(x):
        return roll(x, cols - 1, 1)

    def west(x):
        return roll(x, 1, 1)

    def north(x):
        return roll(x, rows - 1, 0)

    def south(x):
        return roll(x, 1, 0)

    sea = jnp.where(lev > 0.0, 1.0, 0.0)
    face_east = 0.5 * (depth + east(depth)) * sea * east(sea)
    face_north = 0.5 * (depth + north(depth)) * sea * north(sea)
    base = (1.0 - sea) + SURFACE_DAMPING * sea
    sub = iota((8, cols), 0)

    def trim(x):
        return jnp.concatenate([x[:ROWS], jnp.where(sub < 4, x[ROWS : ROWS + 8], x[ROWS + 8 :])], axis=0)

    lev_ref[...] = trim(lev)
    vectors = [f]
    vec_ref[0] = trim(f)
    for i in range(1, 5):
        p = vectors[-1]
        flow_east = face_east * (p - east(p))
        flow_north = face_north * (p - north(p))
        p = base * p + (flow_east - west(flow_east)) + (flow_north - south(flow_north))
        vectors.append(p)
        if i < 4:
            vec_ref[i] = trim(p)
    own = [v[:ROWS, :COLS] for v in vectors]
    parts = [split(v) for v in own]
    row = iota((16, COLS), 0)
    hi = jnp.zeros((16, COLS), F32)
    lo = hi
    for at, (i, j) in enumerate(PAIRS):
        p, e = two_prod(own[i], own[j], parts[i], parts[j])
        quarters = [(p[8 * r : 8 * r + 8], e[8 * r : 8 * r + 8]) for r in range(ROWS // 8)]
        total = dd_add(dd_add(quarters[0], quarters[1]), dd_add(quarters[2], quarters[3]))
        for s in (4, 2, 1):
            total = dd_add(total, (roll(total[0], s, 0), roll(total[1], s, 0)))
        hi = jnp.where(row == at, jnp.concatenate([total[0]] * 2, axis=0), hi)
        lo = jnp.where(row == at, jnp.concatenate([total[1]] * 2, axis=0), lo)
    total = (hi, lo)
    for s in (64, 32, 16, 8, 4, 2, 1):
        total = dd_add(total, (roll(total[0], s, 1), roll(total[1], s, 1)))
    lane = iota((16, COLS), 1)
    line = jnp.where(lane == row, total[0], jnp.where(lane == row + 16, total[1], 0.0))
    line = line[:8] + line[8:]
    for s in (4, 2, 1):
        line = line + roll(line, s, 0)
    gram_ref[...] = jnp.concatenate([line] * (gram_ref.shape[0] // 8), axis=0)


def galerkin(gram):
    rows = gram.shape[0]
    parts = [(gram[8 * r : 8 * r + 8], roll(gram[8 * r : 8 * r + 8], COLS - 16, 1)) for r in range(rows // 8)]
    while len(parts) > 1:
        parts = [dd_add(parts[i], parts[i + 1]) for i in range(0, len(parts) - 1, 2)] + parts[len(parts) // 2 * 2 :]
    total = parts[0]
    for s in (4, 2, 1):
        total = dd_add(total, (roll(total[0], s, 0), roll(total[1], s, 0)))
    entry = {}
    for at, (i, j) in enumerate(PAIRS):
        entry[i, j] = entry[j, i] = tuple(jnp.broadcast_to(t[:, at : at + 1], (8, COLS)) for t in total)
    mat = [[entry[i, j + 1] for j in range(4)] for i in range(4)]
    rhs = [entry[i, 0] for i in range(4)]
    size = [jnp.abs(mat[i][i][0]) for i in range(4)]
    for k in range(4):
        fine = mat[k][k][0] > 1e-12 * size[k]
        inv = dd_inv((jnp.where(fine, mat[k][k][0], 1.0), jnp.where(fine, mat[k][k][1], 0.0)))
        inv = tuple(jnp.where(fine, t, 0.0) for t in inv)
        for j in range(k + 1, 4):
            mat[k][j] = dd_mul(mat[k][j], inv)
        rhs[k] = dd_mul(rhs[k], inv)
        for i in range(k + 1, 4):
            less = dd_neg(mat[i][k])
            for j in range(k + 1, 4):
                mat[i][j] = dd_add(mat[i][j], dd_mul(less, mat[k][j]))
            rhs[i] = dd_add(rhs[i], dd_mul(less, rhs[k]))
    for k in range(2, -1, -1):
        for j in range(k + 1, 4):
            rhs[k] = dd_add(rhs[k], dd_neg(dd_mul(mat[k][j], rhs[j])))
    return [r[0] for r in rhs]


SPANS = ((0, 8), (8, 20), (20, 32), (32, 44), (44, LEVELS))
SPAN_LEVELS = 14
PART_LEVELS = 8
TALL = ROWS + 8
BF16 = jnp.bfloat16


class Sweeps:
    def __init__(self, lev_ref, side_ref, h1_ref, h2_ref, c1_ref, c2_ref, weights):
        self.lev_ref, self.side_ref = lev_ref, side_ref
        self.deep, self.corners = (h1_ref, h2_ref), (c1_ref, c2_ref)
        shape = (COLS, COLS)
        source, target = iota(shape, 0), iota(shape, 1)
        shift = jnp.where(source == target + 1, 1.0, jnp.where(source == target - 1, -1.0, 0.0)).astype(BF16)
        ends = jnp.where(
            (target == COLS - 1) & (source % 2 == 0), 1.0, jnp.where((target == 0) & (source % 2 == 1), -1.0, 0.0)
        ).astype(BF16)
        weights[:COLS] = shift
        weights[COLS : 2 * COLS] = shift
        weights[2 * COLS :] = ends
        self.lane = iota((TALL, COLS), 1)
        pair = iota((8, COLS), 0) // 2
        even = jnp.broadcast_to(lax.rem(lax.axis_index("lat"), 2), (8, COLS)) == 0
        self.masks = [(pair == q) == even for q in range(4)]

    def edge_rows(self, index, q):
        one, two = (r[index] for r in self.deep) if index < EDGES else (r[index - EDGES] for r in self.corners)
        x = jnp.where(self.masks[q], one, two)
        return roll(x, 8 - 2 * q, 0) if q else x

    def tall(self, ref, n, field, k):
        return jnp.concatenate([ref[n, k], self.edge_rows(field * GROUPS + k // 4, k % 4)], axis=0)

    def wet(self, k, rows):
        return jnp.where(float(k) < self.lev_ref[:rows, :COLS], 1.0, 0.0)

    def around(self, ref, side):
        lane = self.lane
        own, edge = roll(ref[:, :COLS], 2, 1), roll(ref[:, COLS:], 2, 1)
        x = jnp.where(lane < 2, own, edge) if side else jnp.where(lane < 2, edge, own)
        for s in (4, 8, 16, 32, 64):
            x = jnp.where(lane < s, x, roll(x, s, 1))
        return x

    def columns(self, first_fields):
        flux1, flux2 = [], []
        for side in range(2):
            levels = self.around(self.lev_ref, side)
            flux1.append([])
            flux2.append([])
            for tile in range(2):
                def column(field, side=side, tile=tile):
                    index = side * 8 + field * 2 + tile
                    return jnp.concatenate(
                        [self.side_ref[side, field, tile], self.edge_rows(EDGES + index // 4, index % 4)], axis=0
                    )

                wet = jnp.where((self.lane // 4 + tile * SLOTS).astype(F32) < levels, 1.0, 0.0)
                move = COURANT * wet
                u, v = column(2), column(3)
                flux1[-1].append([])
                flux2[-1].append([])
                for x in first_fields(side, tile, column, wet):
                    flux = u * x
                    flux1[-1][-1].append(flux)
                    x = x + move * (roll(flux, COLS - 1, 1) - roll(flux, 1, 1))
                    for _ in range(2):
                        x = x + move * self.meridional(v * x)
                    flux2[-1][-1].append((u * x)[:ROWS])
        return flux1, flux2

    @staticmethod
    def meridional(x):
        return roll(x, TALL - 1, 0) - roll(x, 1, 0)

    @staticmethod
    def parts(x):
        hi = x.astype(BF16)
        return hi, (x - hi.astype(F32)).astype(BF16)

    def pack(self, west, east):
        at = iota(east.shape, 1) % 4
        both = jnp.where(at == 2, east, roll(west, 2, 1))
        hi, mid = (t.astype(F32) for t in self.parts(both))
        return jnp.where(at >= 2, hi, roll(mid, COLS - 2, 1))

    def put(self, lhs, at, fields):
        x = jnp.concatenate([f for f, _, _ in fields], axis=0)
        edge = [
            jnp.where(iota(e.shape, 1) // 4 == k % SLOTS, e, 0.0) for _, e, k in fields
        ]
        here = pl.ds(at, x.shape[0])
        hi, mid = self.parts(x)
        lhs[here, :COLS] = hi
        lhs[here, COLS : 2 * COLS] = mid
        lhs[here, 2 * COLS :] = jnp.concatenate(edge, axis=0).astype(BF16)


def halves(span, lhs, diff):
    first, last = span
    middle = first + (last - first) // 4 * 2
    return [(a, b, l, d) for (a, b), l, d in zip(((first, middle), (middle, last)), lhs, diff)]


def fetch(pairs, sem):
    out = []
    for c, (first, last) in enumerate(SPANS):
        here = pl.ds(first, last - first)
        out.append([pltpu.make_async_copy(a.at[:, here], b.at[:, here], sem.at[c, i]) for i, (a, b) in enumerate(pairs)])
    return out


def mixed_kernel(
    lev_ref, side_ref, h1_ref, h2_ref, c1_ref, c2_ref, mixed, vel_h, tr_h,
    swept, ties_h,
    vel, tr, ties, edge1, edge2, edge3, lhs0, lhs1, diff0, diff1, weights, in_sem, out_sem,
):
    reads = fetch(((vel_h, vel), (tr_h, tr)), in_sem)
    for r in sum(reads, []):
        r.start()
    sw = Sweeps(lev_ref, side_ref, h1_ref, h2_ref, c1_ref, c2_ref, weights)
    flux1, flux2 = sw.columns(lambda side, tile, column, wet: (column(0), column(1)))
    for tile in range(2):
        for n in range(2):
            edge1[n, tile] = sw.pack(flux1[0][tile][n], flux1[1][tile][n])
            edge2[n, tile] = sw.pack(flux2[0][tile][n], flux2[1][tile][n])
            edge3[n, tile] = sw.pack(side_ref[0, 4 + n, tile], side_ref[1, 4 + n, tile])
    writes = []
    for span, part in zip(SPANS, reads):
        for r in part:
            r.wait()
        parts = halves(span, (lhs0, lhs1), (diff0, diff1))
        for first, last, lhs, diff in parts:
            rows = 0
            for k in range(first, last):
                u, tile = sw.tall(vel, 0, 2, k), k // SLOTS
                sw.put(lhs, rows, [(u * sw.tall(mixed, n, n, k), edge1[n, tile], k) for n in range(2)])
                rows += 2 * TALL
            diff[:rows] = jnp.dot(lhs[:rows], weights[...], preferred_element_type=F32)
        for first, last, lhs, diff in parts:
            rows = 0
            for k in range(first, last):
                move, tile = COURANT * sw.wet(k, TALL), k // SLOTS
                u, v = vel[0, k], sw.tall(vel, 1, 3, k)
                fields = []
                for n in range(2):
                    at = (2 * (k - first) + n) * TALL
                    x = sw.tall(mixed, n, n, k) + move * diff[at : at + TALL]
                    x = x + move * sw.meridional(v * x)
                    x = (x + move * sw.meridional(v * x))[:ROWS]
                    swept[n, k] = x
                    fields.append((u * x, edge2[n, tile], k))
                sw.put(lhs, rows, fields + [(tr[n, k], edge3[n, tile], k) for n in range(2)])
                rows += 4 * ROWS
            diff[:rows] = jnp.dot(lhs[:rows], weights[...], preferred_element_type=F32)
        for first, last, lhs, diff in parts:
            for k in range(first, last):
                move, at = COURANT * sw.wet(k, ROWS), 4 * (k - first) * ROWS
                x, east, north = [], [], []
                for n in range(2):
                    x.append(swept[n, k] + move * diff[at + n * ROWS : at + (n + 1) * ROWS])
                    swept[n, k] = x[n]
                    east.append(diff[at + (2 + n) * ROWS : at + (3 + n) * ROWS])
                    north.append(sw.meridional(sw.tall(tr, n, 4 + n, k))[:ROWS])
                for i, d in enumerate((east, north)):
                    ties[2 * i, k] = -move * (x[0] * d[0] + x[1] * d[1])
                    ties[2 * i + 1, k] = -move * (GAINS[0] * d[0] + GAINS[1] * d[1])
        here = pl.ds(span[0], span[1] - span[0])
        copy = pltpu.make_async_copy(ties.at[:, here], ties_h.at[:, here], out_sem.at[len(writes)])
        copy.start()
        writes.append(copy)
    for copy in writes:
        copy.wait()


def final_kernel(
    gram_ref, vec_ref, lev_ref, side_ref, h1_ref, h2_ref, c1_ref, c2_ref, swept, vel_h, ties_h,
    adj_h, avel_h, sol_ref,
    vel, ties, adj, avel, sol_s, edge1, edge2, late, lhs0, lhs1, diff0, diff1, weights, in_sem, out_sem,
):
    reads = fetch(((vel_h, vel), (ties_h, ties)), in_sem)
    for r in sum(reads, []):
        r.start()
    sw = Sweeps(lev_ref, side_ref, h1_ref, h2_ref, c1_ref, c2_ref, weights)
    coefs = galerkin(gram_ref[...])
    for half in range(2):
        at = half * COLS
        total = 0.0
        for i in range(4):
            wide = jnp.concatenate([coefs[i]] * (TALL // 8), axis=0)
            total = total + wide * vec_ref[i, :, at : at + COLS]
        sol_s[:, at : at + COLS] = total
    sol_ref[...] = sol_s[:ROWS, :COLS]
    flux1, flux2 = sw.columns(lambda side, tile, column, wet: (wet * sw.around(sol_s, side),))
    for tile in range(2):
        edge1[tile] = sw.pack(flux1[0][tile][0], flux1[1][tile][0])
        edge2[tile] = sw.pack(flux2[0][tile][0], flux2[1][tile][0])
    writes = []
    for span, part in zip(SPANS, reads):
        for r in part:
            r.wait()
        parts = halves(span, (lhs0, lhs1), (diff0, diff1))
        for first, last, lhs, diff in parts:
            rows = 0
            for k in range(first, last, 2):
                fields = []
                for m in (k, k + 1):
                    x = sw.wet(m, TALL) * sol_s[:, :COLS]
                    fields.append((sw.tall(vel, 0, 2, m) * x, edge1[m // SLOTS], m))
                sw.put(lhs, rows, fields)
                rows += 2 * TALL
            diff[:rows] = jnp.dot(lhs[:rows], weights[...], preferred_element_type=F32)
        for first, last, lhs, diff in parts:
            rows = 0
            for k in range(first, last):
                wet = sw.wet(k, TALL)
                move, at = COURANT * wet, (k - first) * TALL
                v = sw.tall(vel, 1, 3, k)
                x = wet * sol_s[:, :COLS] + move * diff[at : at + TALL]
                x = x + move * sw.meridional(v * x)
                x = (x + move * sw.meridional(v * x))[:ROWS]
                late[k - span[0]] = x
                sw.put(lhs, rows, [(vel[0, k] * x, edge2[k // SLOTS], k)])
                rows += ROWS
            diff[:rows] = jnp.dot(lhs[:rows], weights[...], preferred_element_type=F32)
        for first, last, lhs, diff in parts:
            for k in range(first, last):
                at = (k - first) * ROWS
                x = late[k - span[0]] + COURANT * sw.wet(k, ROWS) * diff[at : at + ROWS]
                for n in range(2):
                    adj[n, k] = swept[n, k] + GAINS[n] * x
                    avel[n, k] = ties[2 * n, k] + ties[2 * n + 1, k] * x
        first, last = span
        here = pl.ds(first, last - first)
        for i, (src, dst) in enumerate(((adj, adj_h), (avel, avel_h))):
            copy = pltpu.make_async_copy(src.at[:, here], dst.at[:, here], out_sem.at[len(writes) // 2, i])
            copy.start()
            writes.append(copy)
    for copy in writes:
        copy.wait()


def swaps(size, first, periodic):
    out = []
    for i in range(first, size, 2):
        if i + 1 < size or periodic:
            out += [(i, (i + 1) % size), ((i + 1) % size, i)]
    return out


def shape(*dims):
    return jax.ShapeDtypeStruct(dims, F32)


def call(kernel, name, ins, outs, scratch, args, aliases=None):
    here, there = pl.BlockSpec(memory_space=VMEM), pl.BlockSpec(memory_space=pltpu.HBM)
    args = [pltpu.with_memory_space_constraint(a, pltpu.HBM if far else VMEM) for a, far in zip(args, ins)]
    return pl.pallas_call(
        kernel,
        name=name,
        out_shape=tuple(o for o, _ in outs),
        in_specs=[there if far else here for far in ins],
        out_specs=tuple(there if far else here for _, far in outs),
        scratch_shapes=scratch,
        input_output_aliases=aliases or {},
        compiler_params=pltpu.CompilerParams(vmem_limit_bytes=VMEM_LIMIT),
    )(*args)


def kept(*dims):
    return VMEM(dims, F32), False


def per_device(lam_tracer, tracer, velocity, diffusivity, lam_surface, sea_depth, levels):
    lon, lat = lax.axis_size("lon"), lax.axis_size("lat")
    tile = (ROWS, COLS)
    deep = (2, LEVELS) + tile
    mixed, base, lon1, lon2, slots, g1, g2 = call(
        solve_kernel, "column_solve", (True,) * 7,
        (kept(*deep), kept(3, *tile), kept(4 * LON_TILES, 8, COLS), kept(4 * LON_TILES + 1, 8, COLS),
         kept(FIELDS, 2, *tile), kept(FIELDS * GROUPS, 8, COLS), kept(FIELDS * GROUPS, 8, COLS)),
        [VMEM(deep, F32), VMEM(deep, F32), VMEM(deep, F32), VMEM((LEVELS,) + tile, F32), VMEM(tile, F32), VMEM(tile, jnp.int32),
         VMEM((LEVELS,) + tile, F32), VMEM(deep, F32),
         pltpu.SemaphoreType.DMA((HALF // 5, 4)), pltpu.SemaphoreType.DMA((5,))],
        (lam_tracer, velocity, tracer, diffusivity, lam_surface, sea_depth, levels),
    )
    h1 = lax.ppermute(g1, "lat", swaps(lat, 0, False))
    h2 = lax.ppermute(g2, "lat", swaps(lat, 1, False))
    o1 = lax.ppermute(lon1, "lon", swaps(lon, 0, True))
    o2 = lax.ppermute(lon2, "lon", swaps(lon, 1, True))
    o1, o2, h1, h2 = lax.optimization_barrier((o1, o2, h1, h2))
    ext, lat1, lat2, side = call(
        lon_kernel, "after_lon", (False,) * 4,
        (kept(3, ROWS, 2 * COLS), kept(CORNERS + 6, 8, COLS), kept(CORNERS + 7, 8, COLS), kept(2, FIELDS, 2, *tile)),
        [],
        (base, o1, o2, slots),
    )
    lat1 = lax.ppermute(lat1, "lat", swaps(lat, 0, False))
    lat2 = lax.ppermute(lat2, "lat", swaps(lat, 1, False))
    vec, lev, gram = call(
        krylov_kernel, "krylov", (False,) * 3,
        (kept(4, TALL, 2 * COLS), kept(TALL, 2 * COLS), kept(lon * lat, COLS)),
        [],
        (ext, lat1, lat2),
    )
    gram = lax.all_to_all(gram, ("lon", "lat"), 0, 0, tiled=True)
    rows, many = PART_LEVELS * 4 * ROWS, (4, LEVELS) + tile
    swept, ties = call(
        mixed_kernel, "mixed_sweeps", (False,) * 7 + (True,) * 2,
        (kept(*deep), (pltpu.HBM(many, F32), True)),
        [VMEM(deep, F32), VMEM(deep, F32), VMEM(many, F32), VMEM((2, 2, TALL, COLS), F32), VMEM((2, 2) + tile, F32), VMEM((2, 2) + tile, F32),
         VMEM((rows, 3 * COLS), BF16), VMEM((rows, 3 * COLS), BF16), VMEM((rows, COLS), F32), VMEM((rows, COLS), F32), VMEM((3 * COLS, COLS), BF16),
         pltpu.SemaphoreType.DMA((len(SPANS), 2)), pltpu.SemaphoreType.DMA((len(SPANS),))],
        (lev, side, h1, h2, lat1, lat2, mixed, velocity, tracer), {6: 0},
    )
    rows = PART_LEVELS * TALL
    return call(
        final_kernel, "sweeps", (False,) * 9 + (True,) * 2,
        ((shape(*deep), True), (shape(*deep), True), (shape(*tile), False)),
        [VMEM(deep, F32), VMEM(many, F32), VMEM(deep, F32), VMEM(deep, F32), VMEM((TALL, 2 * COLS), F32),
         VMEM((2, TALL, COLS), F32), VMEM((2,) + tile, F32), VMEM((SPAN_LEVELS,) + tile, F32),
         VMEM((rows, 3 * COLS), BF16), VMEM((rows, 3 * COLS), BF16), VMEM((rows, COLS), F32), VMEM((rows, COLS), F32), VMEM((3 * COLS, COLS), BF16),
         pltpu.SemaphoreType.DMA((len(SPANS), 2)), pltpu.SemaphoreType.DMA((len(SPANS), 2))],
        (gram, vec, lev, side, h1, h2, lat1, lat2, swept, velocity, ties),
    )


def solution(mesh):
    deep, flat = P(None, None, "lat", "lon"), P("lat", "lon")
    return jax.shard_map(
        per_device,
        mesh=mesh,
        in_specs=(deep, deep, deep, P(None, "lat", "lon"), flat, flat, flat),
        out_specs=(deep, deep, flat),
        check_vma=False,
    )
```
